128 devices in a mesh: row: 16 (over y_lo, x, core), col: 8 (over z, y_hi).
Axes of the slice: x: 4, y: 4 (y_hi: 2, y_lo: 2; y = y_hi * 2 + y_lo), z: 4, core: 2. Of those that a mesh axis runs over, the one named last changes fastest.
Arguments:
- core_matrix: bfloat16 [8192, 8192], P('row', 'col'), may hold values from -0.1875 to 0.1875
- pattern: int32 [64, 64], P('row', 'col'), may hold values from 0 to 1, as said below
- shift: float32 [1], replicated, may hold values from -1 to 1
- potential: float32 [128, 64, 128], P('row', 'col'), may hold values from -6 to 6
- home: int32 [64], replicated, may hold values from 0 to 127, as said below
- centres: int32 [3, 64, 128], replicated, may hold values from 0 to 127, as said below
- exponents: float32 [64, 128], replicated, may hold values from 0.05 to 1
- extents: int32 [64, 128], replicated, may hold values from 2 to 7
Outputs:
- scaled: bfloat16 [8192, 8192], P('row', 'col')
- square: bfloat16 [8192, 8192], P('row', 'col')
The draws below stay inside these ranges and needn't reach their ends.
Inputs may be any that keep to these rules, and one draw needn't show every extreme that they name: `pattern`: entries are 0 or 1; every diagonal entry is 1. `home`: at most 2 clusters share a brick, and some brick holds exactly 2. `centres`: the x coordinates lie below 8, the y below 8, the z below 128.
All inputs are finite; a program needn't handle non-finite values.
Results may differ from the reference program's by a relative error of at most 0.0058.
Values may be sent and summed in bfloat16 or wider, within the bound.
No kernel may reach another device: no remote copies, remote signals or barrier semaphores. Data moves between devices by JAX's collectives and lax.ppermute only.
A program may use at most 128 MiB of HBM per device.

```python
import math
import jax
import jax.numpy as jnp
from jax import lax

BS = 128
BX = 8
BY = 8
BZ = 128
CAP = 2
NB = 64
ORDER = 8192
BRICKS = 128
NGX = 128
NGY = 64
N_COL = 8


def draw_pattern(key, part):
    key = jax.random.fold_in(key, 12)
    picked = jax.random.randint(key, (NB, NB), 0, 10)
    kept = (picked < 3) | (jnp.arange(NB)[:, None] == jnp.arange(NB)[None, :])
    return kept.astype(jnp.int32)


def draw_home(key, part):
    key = jax.random.fold_in(key, 11)
    first_key, second_key, third_key = jax.random.split(key, 3)
    slots = BRICKS * CAP
    chosen = jax.random.randint(first_key, (), 0, BRICKS)
    ranking = jax.random.permutation(second_key, slots).astype(jnp.int32)
    numbers = jnp.arange(slots, dtype=jnp.int32)
    order_key = jnp.where(numbers // CAP == chosen, numbers % CAP - CAP, ranking)
    picks = jnp.argsort(order_key)[:NB]
    picks = picks[jax.random.permutation(third_key, NB)]
    return (picks // CAP).astype(jnp.int32)


def draw_centres(key, part):
    key = jax.random.fold_in(key, 13)
    first_key, second_key, third_key = jax.random.split(key, 3)
    along_x = jax.random.randint(first_key, (NB, BS), 0, BX)
    along_y = jax.random.randint(second_key, (NB, BS), 0, BY)
    along_z = jax.random.randint(third_key, (NB, BS), 0, BZ)
    return jnp.stack([along_x, along_y, along_z]).astype(jnp.int32)


def set_ends(array, stream_key, least, high):
    shape = array.shape
    spot = [jax.random.randint(jax.random.fold_in(stream_key, axis), (), 0, shape[axis]) for axis in range(len(shape))]
    array = array.at[tuple(spot)].set(least)
    longest = shape.index(max(shape))
    spot[longest] = (spot[longest] + 1) % shape[longest]
    return array.at[tuple(spot)].set(high)


def steps_of(key, shape, cuts, smallest, top_value):
    level = 1.0
    for dim, parts in cuts:
        draws = jax.random.uniform(jax.random.fold_in(jax.random.fold_in(key, 6), dim), (parts,), jnp.float32, smallest / len(cuts), top_value / len(cuts))
        level = level * jnp.repeat(jnp.exp(draws), shape[dim] // parts).reshape((-1,) + (1,) * (len(shape) - 1 - dim))
    return level


def centred(rng, dims, deviation, bound, pieces=(), kind=jnp.bfloat16):
    drawn = deviation * jax.random.normal(rng, dims, jnp.float32)
    if pieces:
        drawn = drawn * steps_of(rng, dims, pieces, -0.22, 0.18)
    return jnp.clip(drawn, -bound, bound).astype(kind)


def setup_inputs(seed: int = 0) -> dict:
    key_list = jax.random.split(jax.random.key(seed), 9)
    return {
        "core_matrix": centred(key_list[0], (ORDER, ORDER), (BS * 8) ** -0.5, 0.1875, ((0, 16), (1, 8))),
        "pattern": draw_pattern(jax.random.fold_in(key_list[8], 71), 0),
        "shift": jnp.clip(jax.random.uniform(key_list[2], (1,), jnp.float32, -1.0, 1.0), -1.0, 1.0),
        "potential": centred(key_list[3], (NGX, NGY, BZ), 1.0, 6.0, ((0, 16), (1, 8)), jnp.float32),
        "home": draw_home(jax.random.fold_in(key_list[8], 71), 0),
        "centres": draw_centres(jax.random.fold_in(key_list[8], 71), 0),
        "exponents": jnp.clip(jnp.exp(jax.random.uniform(key_list[6], (NB, BS), jnp.float32, math.log(0.05), math.log(1.0))), 0.05, 1.0),
        "extents": set_ends(jax.random.randint(key_list[7], (NB, BS), 2, 8), jax.random.fold_in(key_list[7], 1), 2, 7).astype(jnp.int32),
    }


volume_element = 0.015625

def collocate(centre_xyz, decays, radius, values, span_y, span_z):
    count_points = values.shape[0]
    position = jnp.arange(count_points, dtype=jnp.int32)
    coord_x = position // (span_y * span_z)
    coord_y = position // span_z % span_y
    coord_z = position % span_z
    offset_x = coord_x[None, :] - centre_xyz[0][:, None]
    offset_y = coord_y[None, :] - centre_xyz[1][:, None]
    offset_z = coord_z[None, :] - centre_xyz[2][:, None]
    distance = offset_x * offset_x + offset_y * offset_y + offset_z * offset_z
    inside = distance <= (radius * radius)[:, None]
    values_phi = jnp.where(inside, jnp.exp(-decays[:, None] * distance.astype(jnp.float32)), jnp.float32(0.0))
    basis = values_phi.astype(jnp.bfloat16)
    weighted = (basis.astype(jnp.float32) * values[None, :]).astype(jnp.bfloat16)
    block_value = jnp.dot(weighted, basis.T, preferred_element_type=jnp.float32) * volume_element
    return block_value.astype(jnp.bfloat16)

def reference(core_matrix, pattern, shift, potential, home, centres, exponents, extents):

    def one_cluster(cluster):
        brick = home[cluster]
        brick_row = (brick // N_COL).astype(jnp.int32)
        brick_col = (brick % N_COL).astype(jnp.int32)
        piece = lax.dynamic_slice(potential, (brick_row * BX, brick_col * BY, jnp.int32(0)), (BX, BY, BZ))
        return collocate(centres[:, cluster], exponents[cluster], extents[cluster], piece.reshape(-1), BY, BZ)
    grid_blocks = lax.map(one_cluster, jnp.arange(NB, dtype=jnp.int32))
    identity = jnp.eye(BS, dtype=jnp.float32)
    diagonal = grid_blocks.astype(jnp.float32) - shift[0] * identity[None, :, :]
    selector = jnp.eye(NB, dtype=jnp.float32)
    blocked = core_matrix.astype(jnp.float32).reshape(NB, BS, NB, BS)
    blocked = blocked + selector[:, None, :, None] * diagonal[:, :, None, :]
    keep = pattern.astype(jnp.float32)[:, None, :, None]
    hamiltonian = (blocked * keep).reshape(ORDER, ORDER)
    frob = jnp.sum(hamiltonian * hamiltonian)
    scaled = (hamiltonian * lax.rsqrt(frob / ORDER + 1e-06)).astype(jnp.bfloat16)
    product = jnp.dot(scaled, scaled, preferred_element_type=jnp.float32)
    square = (product.reshape(NB, BS, NB, BS) * keep).reshape(ORDER, ORDER).astype(jnp.bfloat16)
    return (scaled, square)
```

```python
import functools

import jax
import jax.numpy as jnp
from jax import lax
from jax.experimental import pallas as pl
from jax.experimental.pallas import tpu as pltpu
from jax.sharding import PartitionSpec as P

BS = 128
CAP = 20
GROUP = 8
ORDER = 8192
VOLUME = 0.015625
LISTED = 2048 + 32 * GROUP
F32 = jnp.float32
BF16 = jnp.bfloat16


def params(limit=48 * 1024 * 1024):
    return pltpu.CompilerParams(vmem_limit_bytes=limit)


def pack_kernel(pattern_ref, place_ref, core_ref, payload_ref, sum_ref):
    first_row = place_ref[0] * 4
    first_col = place_ref[1] * 8
    sum_ref[...] = jnp.zeros_like(sum_ref)

    def put(i, j, slot):
        payload_ref[pl.ds(pl.multiple_of(slot * BS, BS), BS), :] = core_ref[
            i * BS : (i + 1) * BS, j * BS : (j + 1) * BS
        ]

    slot = jnp.int32(0)
    for i in range(4):
        for j in range(8):
            kept = pattern_ref[i, j] != 0

            @pl.when(kept & (slot < CAP))
            def _():
                put(i, j, slot)

            @pl.when(kept & (first_row + i != first_col + j))
            def _():
                block = core_ref[i * BS : (i + 1) * BS, j * BS : (j + 1) * BS].astype(F32)
                squares = (block * block).reshape(16, 8, BS)
                sum_ref[...] += jnp.sum(squares, axis=0)

            slot += kept.astype(jnp.int32)
    for i in range(4):
        for j in range(8):
            dropped = pattern_ref[i, j] == 0

            @pl.when(dropped & (slot < CAP))
            def _():
                put(i, j, slot)

            slot += dropped.astype(jnp.int32)


def brick_kernel(pattern_ref, potential_ref, brick_ref):
    brick_ref[:64] = potential_ref[...].astype(BF16)
    rows = lax.broadcasted_iota(jnp.int32, (16, BS), 0)
    columns = lax.broadcasted_iota(jnp.int32, (16, BS), 1)
    note = jnp.zeros((16, BS), F32)
    for i in range(4):
        for j in range(8):
            note = jnp.where((rows == 0) & (columns == i * 8 + j), pattern_ref[i, j].astype(F32), note)
    brick_ref[64:] = note.astype(BF16)


def column(row_values):
    return jnp.broadcast_to(row_values, (BS, BS)).T


def collocate(cluster, brick_ref, centres_ref, exponents_ref, extents_ref, along_ref, phi_ref, weighted_ref):
    decay = column(exponents_ref[pl.ds(cluster, 1), :])
    reach = column(extents_ref[pl.ds(cluster, 1), :].astype(F32))
    cut = jnp.exp(-decay * (reach * reach + 0.5))
    at_x = column(centres_ref[0, pl.ds(cluster, 1), :].astype(F32))
    at_y = column(centres_ref[1, pl.ds(cluster, 1), :].astype(F32))
    at_z = column(centres_ref[2, pl.ds(cluster, 1), :].astype(F32))
    off_z = lax.broadcasted_iota(jnp.int32, (BS, BS), 1).astype(F32) - at_z
    along_z = jnp.exp(-decay * (off_z * off_z))
    for y in range(8):
        off_y = y - at_y
        along_ref[y] = jnp.exp(-decay * (off_y * off_y))

    total = jnp.zeros((BS, BS), F32)
    for x in range(8):
        off_x = x - at_x
        along_xz = along_z * jnp.exp(-decay * (off_x * off_x))
        for y in range(8):
            phi = along_xz * along_ref[y]
            basis = jnp.where(phi >= cut, phi, 0.0).astype(BF16)
            phi_ref[x, :, y * BS : (y + 1) * BS] = basis
            weighted_ref[x, :, y * BS : (y + 1) * BS] = basis * brick_ref[x * 8 + y : x * 8 + y + 1, :]
        total += lax.dot_general(
            weighted_ref[x], phi_ref[x], (((1,), (1,)), ((), ())), preferred_element_type=F32
        )
    return (total * VOLUME).astype(BF16)


def grid_kernel(
    count, with_sum, place_ref, home_ref, shift_ref, bricks_ref, centres_ref, exponents_ref, extents_ref, *rest
):
    if with_sum:
        core_ref, sum_ref, blocks_ref, total_ref, along_ref, phi_ref, weighted_ref = rest
    else:
        blocks_ref, along_ref, phi_ref, weighted_ref = rest
    row, col = place_ref[0], place_ref[1]
    first = row * 4 if with_sum else col * 8 + row % 2 * 4

    def one(k, carry):
        cluster = first + k
        home = home_ref[cluster]
        index = (home // 8 ^ row) % 2 * 64 + home // 16 * 8 + home % 8
        blocks_ref[k] = collocate(
            cluster, bricks_ref.at[index], centres_ref, exponents_ref, extents_ref, along_ref, phi_ref, weighted_ref
        )
        return carry

    lax.fori_loop(0, count, one, 0)
    if with_sum:
        total_ref[...] = jnp.sum(sum_ref[...], axis=0, keepdims=True)

        @pl.when(col == row // 2)
        def _():
            eye = identity()
            for i in range(4):
                corner = pl.multiple_of((row % 2 * 4 + i) * BS, BS)
                block = core_ref[i * BS : (i + 1) * BS, pl.ds(corner, BS)].astype(F32)
                block = block + blocks_ref[i].astype(F32) - shift_ref[0] * eye
                total_ref[...] += jnp.sum(block * block, axis=0, keepdims=True)


def identity():
    rows = lax.broadcasted_iota(jnp.int32, (BS, BS), 0)
    columns = lax.broadcasted_iota(jnp.int32, (BS, BS), 1)
    return (rows == columns).astype(F32)


def plan_kernel(
    place_ref, bricks_ref, start_ref, left_ref, right_ref, most_ref, slots_ref, slots, kept_k, kept_slot, kept_device, sem
):
    row, col = place_ref[0], place_ref[1]
    kept = jnp.sum(bricks_ref[:, 64:80, :].astype(F32), axis=1)
    earlier = lax.broadcasted_iota(jnp.int32, (BS, BS), 0) < lax.broadcasted_iota(jnp.int32, (BS, BS), 1)
    before = jnp.dot(kept.astype(BF16), earlier.astype(BF16), preferred_element_type=F32)
    slots_ref[...] = jnp.where(kept > 0.5, before, -1.0).astype(jnp.int32)
    most_ref[0] = jnp.max(jnp.sum(kept, axis=1, keepdims=True)).astype(jnp.int32)
    copy = pltpu.make_async_copy(slots_ref, slots, sem)
    copy.start()
    copy.wait()

    def left_row(i, number):
        def piece(other, number):
            device = row // 2 * 8 + other
            base = ((other ^ col) % 2 * 4 + (other // 2 - col // 2) % 4) * CAP
            for j in range(8):
                slot = slots[device, i * 8 + j]
                holder = other * 2 + j // 4
                kept_slot[number] = base + slot
                kept_device[number] = (holder ^ row) % 2 * 64 + other * 8 + col
                kept_k[number] = other * 8 + j
                number += (slot >= 0).astype(jnp.int32)
            return number

        return lax.fori_loop(0, 8, piece, number)

    def block_row(i, number):
        count = left_row(i, jnp.int32(0))

        def block(j, number):
            start_ref[i * 8 + j] = number // GROUP

            def listing(number):
                def entry(n, number):
                    k = kept_k[n]
                    holder = k // 4
                    slot = slots[kept_device[n], k % 4 * 8 + j]
                    base = (holder ^ row) % 2 * 8 + (holder // 8 ^ row // 8) * 4 + (holder // 2 - row // 2) % 4
                    left_ref[number] = kept_slot[n]
                    right_ref[number] = base * CAP + slot
                    return number + (slot >= 0).astype(jnp.int32)

                number = lax.fori_loop(0, count, entry, number)
                for more in range(GROUP - 1):
                    left_ref[number + more] = 8 * CAP
                    right_ref[number + more] = 0
                return (number + GROUP - 1) // GROUP * GROUP

            wanted = slots[row // 2 * 8 + col, i * 8 + j] >= 0
            return lax.cond(wanted, listing, lambda n: n, number)

        return lax.fori_loop(0, 8, block, number)

    number = lax.fori_loop(0, 4, block_row, jnp.int32(0))
    start_ref[32] = number // GROUP


def scaling(frob_ref):
    total = jnp.sum(frob_ref[...], axis=(0, 1), keepdims=True)
    return lax.rsqrt(total / ORDER + 1e-6)


def product_kernel(
    place_ref, pattern_ref, shift_ref, start_ref, left_ref, right_ref, frob_ref, core_ref, row_grid_ref, col_own_ref, col_other_ref,
    *rest
):
    lefts, rights = rest[:8], rest[8:24]
    scaled_ref, square_ref, left_all, right_all, acc_ref, col_grid_ref, sems = rest[24:]
    parts = [(left_all, k, ref) for k, ref in enumerate(lefts)] + [(right_all, k, ref) for k, ref in enumerate(rights)]
    copies = [
        pltpu.make_async_copy(ref, whole.at[pl.ds(k * CAP, CAP)], sems.at[n])
        for n, (whole, k, ref) in enumerate(parts)
    ]
    for copy in copies:
        copy.start()
    left_all[8 * CAP] = jnp.zeros((BS, BS), BF16)
    first_row = place_ref[0] * 4
    first_col = place_ref[1] * 8
    core = place_ref[0] % 2
    for n in range(4):
        col_grid_ref[core * 4 + n] = col_own_ref[n]
        col_grid_ref[(1 - core) * 4 + n] = col_other_ref[n]
    shift = shift_ref[0]
    scale = scaling(frob_ref)
    eye = identity()
    dot = functools.partial(jnp.dot, preferred_element_type=F32)
    for i in range(4):
        for j in range(8):
            block = (slice(i * BS, (i + 1) * BS), slice(j * BS, (j + 1) * BS))
            kept = pattern_ref[i, j] != 0
            diagonal = first_row + i == first_col + j

            @pl.when(kept)
            def _():
                here = core_ref[block]
                wide = here.astype(F32)
                acc_ref[i * 8 + j] = dot(row_grid_ref[i], here) + dot(here, col_grid_ref[j]) - 2.0 * shift * wide

                @pl.when(diagonal)
                def _():
                    grid = row_grid_ref[i]
                    grid_wide = grid.astype(F32)
                    acc_ref[i * 8 + j] += dot(grid, grid) - 2.0 * shift * grid_wide + shift * shift * eye
                    scaled_ref[block] = ((wide + grid_wide - shift * eye) * scale).astype(BF16)

                @pl.when(jnp.logical_not(diagonal))
                def _():
                    scaled_ref[block] = (wide * scale).astype(BF16)

            @pl.when(jnp.logical_not(kept))
            def _():
                scaled_ref[block] = jnp.zeros((BS, BS), BF16)
                square_ref[block] = jnp.zeros((BS, BS), BF16)

    for copy in copies:
        copy.wait()

    for i in range(4):
        for j in range(8):
            block = (slice(i * BS, (i + 1) * BS), slice(j * BS, (j + 1) * BS))

            @pl.when(pattern_ref[i, j] != 0)
            def _():
                def group(k, acc):
                    at = [k * GROUP + n for n in range(GROUP)]
                    left = jnp.concatenate([left_all[left_ref[n]] for n in at], axis=1)
                    right = jnp.concatenate([right_all[right_ref[n]] for n in at], axis=0)
                    return acc + dot(left, right)

                acc = lax.fori_loop(start_ref[i * 8 + j], start_ref[i * 8 + j + 1], group, acc_ref[i * 8 + j])
                square_ref[block] = (acc * (scale * scale)).astype(BF16)


VM = pl.BlockSpec(memory_space=pltpu.VMEM)
SM = pl.BlockSpec(memory_space=pltpu.SMEM)
ANY = pl.BlockSpec(memory_space=pl.ANY)


def to_all(value, axis, count, groups=None):
    copies = jnp.broadcast_to(value[None], (count,) + value.shape)
    return lax.all_to_all(copies, axis, 0, 0, axis_index_groups=groups)


def along_z(value, off):
    return lax.ppermute(value, "col", [((k + 2 * off) % 8, k) for k in range(8)])


def along_x(value, off):
    return lax.ppermute(value, "row", [(k // 8 * 8 + (k + 2 * off) % 8, k) for k in range(16)])


def half_round_y(value):
    pairs = []
    for row in range(16):
        for col in range(8):
            y = (col % 2 * 2 + row // 8 + (1 if row % 2 == 0 else 3)) % 4
            pairs.append((row * 8 + col, (y % 2 * 8 + row % 8) * 8 + col // 2 * 2 + y // 2))
    return lax.ppermute(value, ("row", "col"), pairs)


def to_core(value):
    return lax.ppermute(value, "row", [(k, k ^ 1) for k in range(16)])


def lasting(microseconds):
    return pl.CostEstimate(flops=int(microseconds * 1e9), bytes_accessed=2**20, transcendentals=0)


def body(core_matrix, pattern, shift, potential, home, centres, exponents, extents):
    row = lax.axis_index("row")
    col = lax.axis_index("col")
    place = jnp.stack([row, col]).astype(jnp.int32)

    payload, squares = pl.pallas_call(
        pack_kernel,
        in_specs=[SM, SM, VM],
        out_specs=[VM, VM],
        out_shape=[jax.ShapeDtypeStruct((CAP * BS, BS), BF16), jax.ShapeDtypeStruct((8, BS), F32)],
        compiler_params=params(),
        cost_estimate=lasting(2),
        name="pack",
    )(pattern, place, core_matrix)
    payload = payload.reshape(CAP, BS, BS)
    own_crossed = to_core(payload)

    (potential, _) = lax.optimization_barrier((potential, own_crossed))
    brick = pl.pallas_call(
        brick_kernel,
        in_specs=[SM, VM],
        out_specs=VM,
        out_shape=jax.ShapeDtypeStruct((80, BS), BF16),
        compiler_params=params(),
        cost_estimate=lasting(1),
        name="brick",
    )(pattern, potential.reshape(64, BS))
    same_core = [[row * 8 + col for row in range(core, 16, 2) for col in range(8)] for core in range(2)]
    half = to_all(brick, ("row", "col"), 64, same_core)

    other_left = half_round_y(half_round_y(payload))
    other_right = lax.ppermute(payload, "row", [(k, k ^ 8) for k in range(16)])
    lefts = [payload, along_z(payload, 1), along_z(payload, -1)]
    rights = [payload, along_x(payload, 1), along_x(payload, -1)]
    half, *_ = lax.optimization_barrier((half, lefts[1], lefts[2], rights[1], rights[2]))
    bricks = jnp.concatenate([half, to_core(half)])
    lefts.insert(2, along_z(lefts[1], 1))
    lefts += [other_left, along_z(other_left, 1), along_z(other_left, -1)]
    rights.insert(2, along_x(rights[1], 1))
    crossed = [own_crossed] + [to_core(piece) for piece in rights[1:]]
    rights += [other_right, along_x(other_right, 1), along_x(other_right, -1)]

    def grid_blocks(count, with_sum, *more):
        extra = [VM, VM] if with_sum else []
        out_shape = [jax.ShapeDtypeStruct((count, BS, BS), BF16)]
        if with_sum:
            out_shape.append(jax.ShapeDtypeStruct((1, BS), F32))
        return pl.pallas_call(
            functools.partial(grid_kernel, count, with_sum),
            in_specs=[SM, SM, SM, VM, VM, VM, VM] + extra,
            out_specs=[VM] * len(out_shape),
            out_shape=out_shape,
            scratch_shapes=[
                pltpu.VMEM((8, BS, BS), F32),
                pltpu.VMEM((8, BS, 8 * BS), BF16),
                pltpu.VMEM((8, BS, 8 * BS), BF16),
            ],
            compiler_params=params(),
            cost_estimate=lasting(2.2 * count),
            name="grid_rows" if with_sum else "grid_cols",
        )(place, home, shift, bricks, centres, exponents, extents, *more)

    row_grid, total = grid_blocks(4, True, core_matrix, squares)
    frob = to_all(total, ("row", "col"), 128).reshape(128, BS)

    left_before, right_before, other_right, right_after, _ = lax.optimization_barrier(
        (lefts[6], rights[6], other_right, rights[5], frob)
    )
    lefts.insert(6, along_z(left_before, -1))
    rights.insert(6, along_x(right_before, -1))
    crossed += [to_core(piece) for piece in (other_right, right_after, rights[6], right_before)]
    rights = rights + crossed

    (col_grid,) = grid_blocks(4, False)
    col_grid_crossed = to_core(col_grid)

    *listed, most = pl.pallas_call(
        plan_kernel,
        in_specs=[SM, VM],
        out_specs=[SM] * 4,
        out_shape=[
            jax.ShapeDtypeStruct((40,), jnp.int32),
            jax.ShapeDtypeStruct((LISTED,), jnp.int32),
            jax.ShapeDtypeStruct((LISTED,), jnp.int32),
            jax.ShapeDtypeStruct((1,), jnp.int32),
        ],
        scratch_shapes=[pltpu.VMEM((BS, BS), jnp.int32), pltpu.SMEM((BS, BS), jnp.int32)]
        + [pltpu.SMEM((72,), jnp.int32)] * 3
        + [pltpu.SemaphoreType.DMA],
        cost_estimate=lasting(5),
        name="plan",
    )(place, bricks)
    overflow = most[0] > CAP

    def sparse():
        return pl.pallas_call(
            product_kernel,
            in_specs=[SM] * 6 + [VM] * 5 + [ANY] * 24,
            out_specs=[VM, VM],
            out_shape=[jax.ShapeDtypeStruct((512, 1024), BF16)] * 2,
            scratch_shapes=[
                pltpu.VMEM((8 * CAP + 1, BS, BS), BF16),
                pltpu.VMEM((16 * CAP, BS, BS), BF16),
                pltpu.VMEM((32, BS, BS), F32),
                pltpu.VMEM((8, BS, BS), BF16),
                pltpu.SemaphoreType.DMA((24,)),
            ],
            compiler_params=params(),
            cost_estimate=lasting(12),
            name="product",
        )(place, pattern, shift, *listed, frob, core_matrix, row_grid, col_grid, col_grid_crossed, *lefts, *rights)

    def dense():
        keep = pattern.astype(F32)[:, None, :, None]
        numbers_row = row * 4 + jnp.arange(4)
        numbers_col = col * 8 + jnp.arange(8)
        on = (numbers_row[:, None] == numbers_col[None, :]).astype(F32)
        grid = row_grid.astype(F32) - shift[0] * jnp.eye(BS, dtype=F32)
        whole = core_matrix.astype(F32).reshape(4, BS, 8, BS) + on[:, None, :, None] * grid[:, :, None, :]
        whole = (whole * keep).reshape(512, 1024)
        scaled = (whole * lax.rsqrt(jnp.sum(frob) / ORDER + 1e-6)).astype(BF16)
        product = jnp.dot(
            lax.all_gather(scaled, "col", axis=1, tiled=True),
            lax.all_gather(scaled, "row", axis=0, tiled=True),
            preferred_element_type=F32,
        )
        square = (product.reshape(4, BS, 8, BS) * keep).reshape(512, 1024).astype(BF16)
        return scaled, square

    return tuple(lax.cond(overflow, lambda: tuple(dense()), lambda: tuple(sparse())))


def solution(mesh):
    in_specs = (P("row", "col"), P("row", "col"), P(), P("row", "col", None), P(), P(), P(), P())
    out_specs = (P("row", "col"), P("row", "col"))
    return jax.shard_map(body, mesh=mesh, in_specs=in_specs, out_specs=out_specs, check_vma=False)
```

```python
import functools

import jax
import jax.numpy as jnp
from jax import lax
from jax.experimental import pallas as pl
from jax.experimental.pallas import tpu as pltpu
from jax.sharding import PartitionSpec as P

BS = 128
CAP = 20
GROUP = 4
TURN = 4
ORDER = 8192
VOLUME = 0.015625
LISTED = 2048 + 32 * GROUP + TURN * GROUP
F32 = jnp.float32
BF16 = jnp.bfloat16


def params(limit=48 * 1024 * 1024):
    return pltpu.CompilerParams(vmem_limit_bytes=limit)


def pack_kernel(pattern_ref, place_ref, core_ref, payload_ref, sum_ref):
    first_row = place_ref[0] * 4
    first_col = place_ref[1] * 8
    sum_ref[...] = jnp.zeros_like(sum_ref)

    def put(i, j, slot):
        payload_ref[pl.ds(pl.multiple_of(slot * BS, BS), BS), :] = core_ref[
            i * BS : (i + 1) * BS, j * BS : (j + 1) * BS
        ]

    slot = jnp.int32(0)
    for i in range(4):
        for j in range(8):
            kept = pattern_ref[i, j] != 0

            @pl.when(kept & (slot < CAP))
            def _():
                put(i, j, slot)

            @pl.when(kept & (first_row + i != first_col + j))
            def _():
                block = core_ref[i * BS : (i + 1) * BS, j * BS : (j + 1) * BS].astype(F32)
                squares = (block * block).reshape(16, 8, BS)
                sum_ref[...] += jnp.sum(squares, axis=0)

            slot += kept.astype(jnp.int32)
    for i in range(4):
        for j in range(8):
            dropped = pattern_ref[i, j] == 0

            @pl.when(dropped & (slot < CAP))
            def _():
                put(i, j, slot)

            slot += dropped.astype(jnp.int32)


def brick_kernel(pattern_ref, potential_ref, brick_ref):
    brick_ref[:64] = potential_ref[...].astype(BF16)
    rows = lax.broadcasted_iota(jnp.int32, (16, BS), 0)
    columns = lax.broadcasted_iota(jnp.int32, (16, BS), 1)
    note = jnp.zeros((16, BS), F32)
    for i in range(4):
        for j in range(8):
            note = jnp.where((rows == 0) & (columns == i * 8 + j), pattern_ref[i, j].astype(F32), note)
    brick_ref[64:] = note.astype(BF16)


def column(row_values):
    return jnp.broadcast_to(row_values, (BS, BS)).T


def collocate(cluster, brick_ref, centres_ref, exponents_ref, extents_ref, along_ref, phi_ref, weighted_ref):
    decay = column(exponents_ref[pl.ds(cluster, 1), :])
    reach = column(extents_ref[pl.ds(cluster, 1), :].astype(F32))
    cut = jnp.exp(-decay * (reach * reach + 0.5))
    at_x = column(centres_ref[0, pl.ds(cluster, 1), :].astype(F32))
    at_y = column(centres_ref[1, pl.ds(cluster, 1), :].astype(F32))
    at_z = column(centres_ref[2, pl.ds(cluster, 1), :].astype(F32))
    off_z = lax.broadcasted_iota(jnp.int32, (BS, BS), 1).astype(F32) - at_z
    along_z = jnp.exp(-decay * (off_z * off_z))
    for y in range(8):
        off_y = y - at_y
        along_ref[y] = jnp.exp(-decay * (off_y * off_y))

    total = jnp.zeros((BS, BS), F32)
    for x in range(8):
        off_x = x - at_x
        along_xz = along_z * jnp.exp(-decay * (off_x * off_x))
        for y in range(8):
            phi = along_xz * along_ref[y]
            basis = jnp.where(phi >= cut, phi, 0.0).astype(BF16)
            phi_ref[x, :, y * BS : (y + 1) * BS] = basis
            weighted_ref[x, :, y * BS : (y + 1) * BS] = basis * brick_ref[x * 8 + y : x * 8 + y + 1, :]
        total += lax.dot_general(
            weighted_ref[x], phi_ref[x], (((1,), (1,)), ((), ())), preferred_element_type=F32
        )
    return (total * VOLUME).astype(BF16)


def grid_kernel(
    count, with_sum, place_ref, home_ref, shift_ref, bricks_ref, centres_ref, exponents_ref, extents_ref, *rest
):
    if with_sum:
        core_ref, sum_ref, blocks_ref, total_ref, along_ref, phi_ref, weighted_ref = rest
    else:
        blocks_ref, along_ref, phi_ref, weighted_ref = rest
    row, col = place_ref[0], place_ref[1]
    first = row * 4 if with_sum else col * 8 + row % 2 * 4

    def one(k, carry):
        cluster = first + k
        home = home_ref[cluster]
        index = (home // 8 ^ row) % 2 * 64 + home // 16 * 8 + home % 8
        blocks_ref[k] = collocate(
            cluster, bricks_ref.at[index], centres_ref, exponents_ref, extents_ref, along_ref, phi_ref, weighted_ref
        )
        return carry

    lax.fori_loop(0, count, one, 0)
    if with_sum:
        total_ref[...] = jnp.sum(sum_ref[...], axis=0, keepdims=True)

        @pl.when(col == row // 2)
        def _():
            eye = identity()
            for i in range(4):
                corner = pl.multiple_of((row % 2 * 4 + i) * BS, BS)
                block = core_ref[i * BS : (i + 1) * BS, pl.ds(corner, BS)].astype(F32)
                block = block + blocks_ref[i].astype(F32) - shift_ref[0] * eye
                total_ref[...] += jnp.sum(block * block, axis=0, keepdims=True)


def identity():
    rows = lax.broadcasted_iota(jnp.int32, (BS, BS), 0)
    columns = lax.broadcasted_iota(jnp.int32, (BS, BS), 1)
    return (rows == columns).astype(F32)


def plan_kernel(
    place_ref, bricks_ref, turns_ref, out_ref, left_ref, right_ref, most_ref, slots_ref, slots, kept_left, kept_right, kept_at, sem
):
    row, col = place_ref[0], place_ref[1]
    kept = jnp.sum(bricks_ref[:, 64:80, :].astype(F32), axis=1)
    kept = kept.T
    earlier = lax.broadcasted_iota(jnp.int32, (BS, BS), 1) < lax.broadcasted_iota(jnp.int32, (BS, BS), 0)
    before = jnp.dot(earlier.astype(BF16), kept.astype(BF16), preferred_element_type=F32)
    slots_ref[...] = jnp.where(kept > 0.5, before, -1.0)[:40].astype(jnp.int32)
    most_ref[0] = jnp.max(jnp.sum(kept, axis=0, keepdims=True)).astype(jnp.int32)
    copy = pltpu.make_async_copy(slots_ref, slots, sem)
    copy.start()
    copy.wait()

    def block_row(i, number):
        def piece(other, count):
            device = row // 2 * 8 + other
            base = ((other ^ col) % 2 * 4 + (other // 2 - col // 2) % 4) * CAP
            right = ((other // 4 ^ row // 8) * 4 + (other - row // 2) % 4) * 2 * CAP
            for j in range(8):
                slot = slots[i * 8 + j, device]
                kept_left[count] = base + slot
                kept_right[count] = right + j // 4 * CAP
                kept_at[count] = j % 4 * 8 * BS + (j // 4 ^ row) % 2 * 64 + other * 8 + col
                count += (slot >= 0).astype(jnp.int32)
            return count

        count = lax.fori_loop(0, 8, piece, jnp.int32(0))
        for more in range(3):
            kept_left[count + more] = 0
            kept_right[count + more] = 0
            kept_at[count + more] = 32 * BS

        def block(j, number):
            def listing(number):
                start = number // GROUP
                def four(n, number):
                    for inner in range(4):
                        at = kept_at[n * 4 + inner] + j * BS
                        slot = slots[at >> 7, at & 127]
                        left_ref[number] = kept_left[n * 4 + inner]
                        right_ref[number] = kept_right[n * 4 + inner] + slot
                        number += (slot >= 0).astype(jnp.int32)
                    return number

                number = lax.fori_loop(0, (count + 3) // 4, four, number)
                for more in range(GROUP - 1):
                    left_ref[number + more] = 8 * CAP
                    right_ref[number + more] = 0
                end = (number + GROUP - 1) // GROUP

                def name(group, carry):
                    out_ref[group] = i * 8 + j
                    return carry

                lax.fori_loop(start, end, name, 0)
                return end * GROUP

            wanted = slots[i * 8 + j, row // 2 * 8 + col] >= 0
            return lax.cond(wanted, listing, lambda n: n, number)

        return lax.fori_loop(0, 8, block, number)

    number = lax.fori_loop(0, 4, block_row, jnp.int32(0))
    groups = number // GROUP
    for more in range(TURN):
        out_ref[groups + more] = 32
        for inner in range(GROUP):
            left_ref[number + more * GROUP + inner] = 8 * CAP
            right_ref[number + more * GROUP + inner] = 0
    turns_ref[0] = (groups + TURN - 1) // TURN


def scaling(frob_ref):
    total = jnp.sum(frob_ref[...], axis=(0, 1), keepdims=True)
    return lax.rsqrt(total / ORDER + 1e-6)


def product_kernel(
    place_ref, pattern_ref, shift_ref, turns_ref, out_ref, left_ref, right_ref, frob_ref, core_ref, row_grid_ref, col_own_ref, col_other_ref,
    *rest
):
    payload, crossed, own_role, other_role = rest[0], rest[1], rest[2:9], rest[9:16]
    scaled_ref, square_ref, left_all, right_all, acc_ref, col_grid_ref, sems = rest[16:]
    core = place_ref[0] % 2

    def part(whole, at, size, source, number):
        return pltpu.make_async_copy(source, whole.at[pl.ds(at, size)], sems.at[number])

    copies = [
        part(left_all, 0, CAP, payload, 0),
        part(right_all, core * CAP, CAP, payload, 1),
        part(right_all, (1 - core) * CAP, CAP, crossed, 2),
    ]
    for copy in copies:
        copy.start()
    for k in range(1, 8):
        mine, others = own_role[k - 1], other_role[k - 1]
        of_core_0 = [
            part(left_all, k * CAP, CAP, others.at[pl.ds(CAP, CAP)], 1 + 2 * k),
            part(right_all, 2 * k * CAP, 2 * CAP, mine, 2 + 2 * k),
        ]
        of_core_1 = [
            part(left_all, k * CAP, CAP, mine.at[pl.ds(0, CAP)], 1 + 2 * k),
            part(right_all, 2 * k * CAP, 2 * CAP, others, 2 + 2 * k),
        ]
        copies += of_core_0

        @pl.when(core == 0)
        def _():
            for copy in of_core_0:
                copy.start()

        @pl.when(core == 1)
        def _():
            for copy in of_core_1:
                copy.start()

    left_all[8 * CAP] = jnp.zeros((BS, BS), BF16)
    acc_ref[32] = jnp.zeros((BS, BS), F32)
    first_row = place_ref[0] * 4
    first_col = place_ref[1] * 8
    for n in range(4):
        col_grid_ref[core * 4 + n] = col_own_ref[n]
        col_grid_ref[(1 - core) * 4 + n] = col_other_ref[n]
    shift = shift_ref[0]
    scale = scaling(frob_ref)
    eye = identity()
    dot = functools.partial(jnp.dot, preferred_element_type=F32)
    for i in range(4):
        for j in range(8):
            block = (slice(i * BS, (i + 1) * BS), slice(j * BS, (j + 1) * BS))
            kept = pattern_ref[i, j] != 0
            diagonal = first_row + i == first_col + j

            @pl.when(kept)
            def _():
                here = core_ref[block]
                wide = here.astype(F32)
                acc_ref[i * 8 + j] = dot(row_grid_ref[i], here) + dot(here, col_grid_ref[j]) - 2.0 * shift * wide

                @pl.when(diagonal)
                def _():
                    grid = row_grid_ref[i]
                    grid_wide = grid.astype(F32)
                    acc_ref[i * 8 + j] += dot(grid, grid) - 2.0 * shift * grid_wide + shift * shift * eye
                    scaled_ref[block] = ((wide + grid_wide - shift * eye) * scale).astype(BF16)

                @pl.when(jnp.logical_not(diagonal))
                def _():
                    scaled_ref[block] = (wide * scale).astype(BF16)

            @pl.when(jnp.logical_not(kept))
            def _():
                scaled_ref[block] = jnp.zeros((BS, BS), BF16)
                square_ref[block] = jnp.zeros((BS, BS), BF16)

    for copy in copies:
        copy.wait()

    def turn(t, carry):
        sums = []
        for group in range(TURN):
            at = [(t * TURN + group) * GROUP + n for n in range(GROUP)]
            left = jnp.concatenate([left_all[left_ref[n]] for n in at], axis=1)
            right = jnp.concatenate([right_all[right_ref[n]] for n in at], axis=0)
            sums.append(dot(left, right))
        for group in range(TURN):
            acc_ref[out_ref[t * TURN + group]] += sums[group]
        return carry

    lax.fori_loop(0, turns_ref[0], turn, 0)
    for i in range(4):
        for j in range(8):
            block = (slice(i * BS, (i + 1) * BS), slice(j * BS, (j + 1) * BS))

            @pl.when(pattern_ref[i, j] != 0)
            def _():
                square_ref[block] = (acc_ref[i * 8 + j] * (scale * scale)).astype(BF16)


VM = pl.BlockSpec(memory_space=pltpu.VMEM)
SM = pl.BlockSpec(memory_space=pltpu.SMEM)
ANY = pl.BlockSpec(memory_space=pl.ANY)


def to_all(value, axis, count, groups=None):
    copies = jnp.broadcast_to(value[None], (count,) + value.shape)
    return lax.all_to_all(copies, axis, 0, 0, axis_index_groups=groups)


def place_of(device):
    row, col = device // 8, device % 8
    return row // 2 % 4, col % 2 * 2 + row // 8, col // 2, row % 2


def device_of(x, y, z, core):
    return ((y % 2 * 4 + x % 4) * 2 + core) * 8 + z % 4 * 2 + y // 2


def move(value, where):
    return lax.ppermute(value, ("row", "col"), [(k, device_of(*where(*place_of(k)))) for k in range(128)])


def ring(value, off):
    return move(value, lambda x, y, z, core: (x, y, z - off, core) if core else (x - off, y, z, core))


def across_y(value):
    return move(value, lambda x, y, z, core: (x, 3 - y if core else y ^ 1, z, core))


def across_y_again(value):
    return move(value, lambda x, y, z, core: (x, y ^ 1 if core else y, z, core))


def to_core(value):
    return lax.ppermute(value, "row", [(k, k ^ 1) for k in range(16)])


def lasting(microseconds):
    return pl.CostEstimate(flops=int(microseconds * 1e9), bytes_accessed=2**20, transcendentals=0)


def body(core_matrix, pattern, shift, potential, home, centres, exponents, extents):
    row = lax.axis_index("row")
    col = lax.axis_index("col")
    place = jnp.stack([row, col]).astype(jnp.int32)

    brick = pl.pallas_call(
        brick_kernel,
        in_specs=[SM, VM],
        out_specs=VM,
        out_shape=jax.ShapeDtypeStruct((80, BS), BF16),
        compiler_params=params(),
        cost_estimate=lasting(1),
        name="brick",
    )(pattern, potential.reshape(64, BS))
    same_core = [[row * 8 + col for row in range(core, 16, 2) for col in range(8)] for core in range(2)]
    half = to_all(brick, ("row", "col"), 64, same_core)

    (core_after_brick, _) = lax.optimization_barrier((core_matrix, brick))
    payload, squares = pl.pallas_call(
        pack_kernel,
        in_specs=[SM, SM, VM],
        out_specs=[VM, VM],
        out_shape=[jax.ShapeDtypeStruct((CAP * BS, BS), BF16), jax.ShapeDtypeStruct((8, BS), F32)],
        compiler_params=params(),
        cost_estimate=lasting(2),
        name="pack",
    )(pattern, place, core_after_brick)
    payload = payload.reshape(CAP, BS, BS)
    crossed = to_core(payload)

    pair = jnp.concatenate([payload, crossed])
    step = across_y(pair)
    after, before = ring(pair, 1), ring(pair, -1)
    half, step, after, before = lax.optimization_barrier((half, step, after, before))

    far = ring(after, 1)
    other = across_y_again(step)
    bricks = jnp.concatenate([half, to_core(half)])

    def grid_blocks(count, with_sum, *more):
        extra = [VM, VM] if with_sum else []
        out_shape = [jax.ShapeDtypeStruct((count, BS, BS), BF16)]
        if with_sum:
            out_shape.append(jax.ShapeDtypeStruct((1, BS), F32))
        return pl.pallas_call(
            functools.partial(grid_kernel, count, with_sum),
            in_specs=[SM, SM, SM, VM, VM, VM, VM] + extra,
            out_specs=[VM] * len(out_shape),
            out_shape=out_shape,
            scratch_shapes=[
                pltpu.VMEM((8, BS, BS), F32),
                pltpu.VMEM((8, BS, 8 * BS), BF16),
                pltpu.VMEM((8, BS, 8 * BS), BF16),
            ],
            compiler_params=params(),
            cost_estimate=lasting(2.2 * count),
            name="grid_rows" if with_sum else "grid_cols",
        )(place, home, shift, bricks, centres, exponents, extents, *more)

    row_grid, total = grid_blocks(4, True, core_matrix, squares)
    after, before, far, other, row_grid, total, bricks = lax.optimization_barrier(
        (after, before, far, other, row_grid, total, bricks)
    )

    other_after, other_before = ring(other, 1), ring(other, -1)
    crossings = [to_core(after), to_core(far), to_core(before)]
    (col_grid,) = grid_blocks(4, False)
    *listed, most = pl.pallas_call(
        plan_kernel,
        in_specs=[SM, VM],
        out_specs=[SM] * 5,
        out_shape=[
            jax.ShapeDtypeStruct((1,), jnp.int32),
            jax.ShapeDtypeStruct((LISTED // GROUP,), jnp.int32),
            jax.ShapeDtypeStruct((LISTED,), jnp.int32),
            jax.ShapeDtypeStruct((LISTED,), jnp.int32),
            jax.ShapeDtypeStruct((1,), jnp.int32),
        ],
        scratch_shapes=[pltpu.VMEM((40, BS), jnp.int32), pltpu.SMEM((40, BS), jnp.int32)]
        + [pltpu.SMEM((72,), jnp.int32)] * 3
        + [pltpu.SemaphoreType.DMA],
        cost_estimate=lasting(7),
        name="plan",
    )(place, bricks)
    other_after, other_before, col_grid, total, *rest = lax.optimization_barrier(
        (other_after, other_before, col_grid, total, *crossings, *listed)
    )
    crossings, listed = rest[:3], rest[3:]

    other_far = ring(other_before, -1)
    crossings += [to_core(other), to_core(other_after), to_core(other_before)]
    col_grid_crossed = to_core(col_grid)
    frob = to_all(total, ("row", "col"), 128).reshape(128, BS)
    other_far, col_grid_crossed, frob, *crossings = lax.optimization_barrier(
        (other_far, col_grid_crossed, frob, *crossings)
    )

    crossings.insert(5, to_core(other_far))
    own_role = [after, far, before, other, other_after, other_far, other_before]
    overflow = most[0] > CAP

    def sparse():
        return pl.pallas_call(
            product_kernel,
            in_specs=[SM] * 7 + [VM] * 5 + [ANY] * 16,
            out_specs=[VM, VM],
            out_shape=[jax.ShapeDtypeStruct((512, 1024), BF16)] * 2,
            scratch_shapes=[
                pltpu.VMEM((8 * CAP + 1, BS, BS), BF16),
                pltpu.VMEM((16 * CAP, BS, BS), BF16),
                pltpu.VMEM((33, BS, BS), F32),
                pltpu.VMEM((8, BS, BS), BF16),
                pltpu.SemaphoreType.DMA((17,)),
            ],
            compiler_params=params(),
            cost_estimate=lasting(12),
            name="product",
        )(place, pattern, shift, *listed, frob, core_matrix, row_grid, col_grid, col_grid_crossed, payload, crossed, *own_role, *crossings)

    def dense():
        keep = pattern.astype(F32)[:, None, :, None]
        numbers_row = row * 4 + jnp.arange(4)
        numbers_col = col * 8 + jnp.arange(8)
        on = (numbers_row[:, None] == numbers_col[None, :]).astype(F32)
        grid = row_grid.astype(F32) - shift[0] * jnp.eye(BS, dtype=F32)
        whole = core_matrix.astype(F32).reshape(4, BS, 8, BS) + on[:, None, :, None] * grid[:, :, None, :]
        whole = (whole * keep).reshape(512, 1024)
        scaled = (whole * lax.rsqrt(jnp.sum(frob) / ORDER + 1e-6)).astype(BF16)
        product = jnp.dot(
            lax.all_gather(scaled, "col", axis=1, tiled=True),
            lax.all_gather(scaled, "row", axis=0, tiled=True),
            preferred_element_type=F32,
        )
        square = (product.reshape(4, BS, 8, BS) * keep).reshape(512, 1024).astype(BF16)
        return scaled, square

    return tuple(lax.cond(overflow, lambda: tuple(dense()), lambda: tuple(sparse())))


def solution(mesh):
    in_specs = (P("row", "col"), P("row", "col"), P(), P("row", "col", None), P(), P(), P(), P())
    out_specs = (P("row", "col"), P("row", "col"))
    return jax.shard_map(body, mesh=mesh, in_specs=in_specs, out_specs=out_specs, check_vma=False)
```

```python
import functools

import jax
import jax.numpy as jnp
from jax import lax
from jax.experimental import pallas as pl
from jax.experimental.pallas import tpu as pltpu
from jax.sharding import PartitionSpec as P

BS = 128
CAP = 20
GROUP = 4
TURN = 4
ORDER = 8192
VOLUME = 0.015625
LISTED = 2048 + 32 * GROUP + TURN * GROUP
F32 = jnp.float32
BF16 = jnp.bfloat16


def params(mebibytes):
    return pltpu.CompilerParams(vmem_limit_bytes=mebibytes * 2**20)


def pack_kernel(pattern_ref, place_ref, core_ref, payload_ref, sum_ref):
    first_row = place_ref[0] * 4
    first_col = place_ref[1] * 8
    sum_ref[...] = jnp.zeros_like(sum_ref)

    def put(i, j, slot):
        payload_ref[pl.ds(pl.multiple_of(slot * BS, BS), BS), :] = core_ref[
            i * BS : (i + 1) * BS, j * BS : (j + 1) * BS
        ]

    slot = jnp.int32(0)
    for i in range(4):
        for j in range(8):
            kept = pattern_ref[i, j] != 0

            @pl.when(kept & (slot < CAP))
            def _():
                put(i, j, slot)

            @pl.when(kept & (first_row + i != first_col + j))
            def _():
                block = core_ref[i * BS : (i + 1) * BS, j * BS : (j + 1) * BS].astype(F32)
                squares = (block * block).reshape(16, 8, BS)
                sum_ref[...] += jnp.sum(squares, axis=0)

            slot += kept.astype(jnp.int32)
    for i in range(4):
        for j in range(8):
            dropped = pattern_ref[i, j] == 0

            @pl.when(dropped & (slot < CAP))
            def _():
                put(i, j, slot)

            slot += dropped.astype(jnp.int32)


def brick_kernel(pattern_ref, potential_ref, brick_ref):
    brick_ref[:64] = potential_ref[...].astype(BF16)
    rows = lax.broadcasted_iota(jnp.int32, (16, BS), 0)
    columns = lax.broadcasted_iota(jnp.int32, (16, BS), 1)
    note = jnp.zeros((16, BS), F32)
    for i in range(4):
        for j in range(8):
            note = jnp.where((rows == 0) & (columns == i * 8 + j), pattern_ref[i, j].astype(F32), note)
    brick_ref[64:] = note.astype(BF16)


def column(row_values):
    return jnp.broadcast_to(row_values, (BS, BS)).T


def values_kernel(place_ref, centres_ref, exponents_ref, extents_ref, phi_ref, along_ref):
    row, col = place_ref[0], place_ref[1]

    def one(k, carry):
        cluster = jnp.where(k < 4, row * 4 + k, col * 8 + row % 2 * 4 + k - 4)
        decay = column(exponents_ref[pl.ds(cluster, 1), :])
        reach = column(extents_ref[pl.ds(cluster, 1), :].astype(F32))
        cut = jnp.exp(-decay * (reach * reach + 0.5))
        at_x = column(centres_ref[0, pl.ds(cluster, 1), :].astype(F32))
        at_y = column(centres_ref[1, pl.ds(cluster, 1), :].astype(F32))
        at_z = column(centres_ref[2, pl.ds(cluster, 1), :].astype(F32))
        off_z = lax.broadcasted_iota(jnp.int32, (BS, BS), 1).astype(F32) - at_z
        along_z = jnp.exp(-decay * (off_z * off_z))
        for y in range(8):
            off_y = y - at_y
            along_ref[y] = jnp.exp(-decay * (off_y * off_y))
        for x in range(8):
            off_x = x - at_x
            along_xz = along_z * jnp.exp(-decay * (off_x * off_x))
            for y in range(8):
                phi = along_xz * along_ref[y]
                phi_ref[k, x, :, y * BS : (y + 1) * BS] = jnp.where(phi >= cut, phi, 0.0).astype(BF16)
        return carry

    lax.fori_loop(0, 8, one, 0)


def grid_kernel(with_sum, place_ref, home_ref, shift_ref, bricks_ref, phi_ref, *rest):
    if with_sum:
        core_ref, sum_ref, blocks_ref, total_ref = rest
    else:
        (blocks_ref,) = rest
    row, col = place_ref[0], place_ref[1]
    first = row * 4 if with_sum else col * 8 + row % 2 * 4
    place = 0 if with_sum else 4

    def one(k, carry):
        home = home_ref[first + k]
        index = (home // 8 ^ row) % 2 * 64 + home // 16 * 8 + home % 8
        total = jnp.zeros((BS, BS), F32)
        for x in range(8):
            values = jnp.concatenate([bricks_ref[index, x * 8 + y : x * 8 + y + 1, :] for y in range(8)], axis=1)
            phi = phi_ref[place + k, x]
            total += lax.dot_general(phi * values, phi, (((1,), (1,)), ((), ())), preferred_element_type=F32)
        blocks_ref[k] = (total * VOLUME).astype(BF16)
        return carry

    lax.fori_loop(0, 4, one, 0)
    if with_sum:
        total_ref[...] = jnp.sum(sum_ref[...], axis=0, keepdims=True)

        @pl.when(col == row // 2)
        def _():
            eye = identity()
            for i in range(4):
                corner = pl.multiple_of((row % 2 * 4 + i) * BS, BS)
                block = core_ref[i * BS : (i + 1) * BS, pl.ds(corner, BS)].astype(F32)
                block = block + blocks_ref[i].astype(F32) - shift_ref[0] * eye
                total_ref[...] += jnp.sum(block * block, axis=0, keepdims=True)


def identity():
    rows = lax.broadcasted_iota(jnp.int32, (BS, BS), 0)
    columns = lax.broadcasted_iota(jnp.int32, (BS, BS), 1)
    return (rows == columns).astype(F32)


def plan_kernel(
    place_ref, bricks_ref, turns_ref, out_ref, left_ref, right_ref, most_ref, slots_ref, slots, kept_left, kept_right, kept_at, sem
):
    row, col = place_ref[0], place_ref[1]
    kept = jnp.sum(bricks_ref[:, 64:80, :].astype(F32), axis=1)
    kept = kept.T
    earlier = lax.broadcasted_iota(jnp.int32, (BS, BS), 1) < lax.broadcasted_iota(jnp.int32, (BS, BS), 0)
    before = jnp.dot(earlier.astype(BF16), kept.astype(BF16), preferred_element_type=F32)
    slots_ref[...] = jnp.where(kept > 0.5, before, -1.0)[:40].astype(jnp.int32)
    most_ref[0] = jnp.max(jnp.sum(kept, axis=0, keepdims=True)).astype(jnp.int32)
    copy = pltpu.make_async_copy(slots_ref, slots, sem)
    copy.start()
    copy.wait()

    def block_row(i, number):
        def piece(other, count):
            device = row // 2 * 8 + other
            base = ((other ^ col) % 2 * 4 + (other // 2 - col // 2) % 4) * CAP
            right = ((other // 4 ^ row // 8) * 4 + (other - row // 2) % 4) * 2 * CAP
            for j in range(8):
                slot = slots[i * 8 + j, device]
                kept_left[count] = base + slot
                kept_right[count] = right + j // 4 * CAP
                kept_at[count] = j % 4 * 8 * BS + (j // 4 ^ row) % 2 * 64 + other * 8 + col
                count += (slot >= 0).astype(jnp.int32)
            return count

        count = lax.fori_loop(0, 8, piece, jnp.int32(0))
        for more in range(3):
            kept_left[count + more] = 0
            kept_right[count + more] = 0
            kept_at[count + more] = 32 * BS

        def block(j, number):
            def listing(number):
                start = number // GROUP
                def four(n, number):
                    for inner in range(4):
                        at = kept_at[n * 4 + inner] + j * BS
                        slot = slots[at >> 7, at & 127]
                        left_ref[number] = kept_left[n * 4 + inner]
                        right_ref[number] = kept_right[n * 4 + inner] + slot
                        number += (slot >= 0).astype(jnp.int32)
                    return number

                number = lax.fori_loop(0, (count + 3) // 4, four, number)
                for more in range(GROUP - 1):
                    left_ref[number + more] = 8 * CAP
                    right_ref[number + more] = 0
                end = (number + GROUP - 1) // GROUP

                def name(group, carry):
                    out_ref[group] = i * 8 + j
                    return carry

                lax.fori_loop(start, end, name, 0)
                return end * GROUP

            wanted = slots[i * 8 + j, row // 2 * 8 + col] >= 0
            return lax.cond(wanted, listing, lambda n: n, number)

        return lax.fori_loop(0, 8, block, number)

    number = lax.fori_loop(0, 4, block_row, jnp.int32(0))
    groups = number // GROUP
    for more in range(TURN):
        out_ref[groups + more] = 32
        for inner in range(GROUP):
            left_ref[number + more * GROUP + inner] = 8 * CAP
            right_ref[number + more * GROUP + inner] = 0
    turns_ref[0] = (groups + TURN - 1) // TURN


def scaling(frob_ref):
    total = jnp.sum(frob_ref[...], axis=(0, 1), keepdims=True)
    return lax.rsqrt(total / ORDER + 1e-6)


def product_kernel(
    place_ref, pattern_ref, shift_ref, turns_ref, out_ref, left_ref, right_ref, frob_ref, core_ref, row_grid_ref, col_own_ref, col_other_ref,
    *rest
):
    payload, crossed, own_role, other_role = rest[0], rest[1], rest[2:9], rest[9:16]
    scaled_ref, square_ref, left_all, right_all, acc_ref, col_grid_ref, sems = rest[16:]
    core = place_ref[0] % 2

    def part(whole, at, size, source, number):
        return pltpu.make_async_copy(source, whole.at[pl.ds(at, size)], sems.at[number])

    copies = [
        part(left_all, 0, CAP, payload, 0),
        part(right_all, core * CAP, CAP, payload, 1),
        part(right_all, (1 - core) * CAP, CAP, crossed, 2),
    ]
    for copy in copies:
        copy.start()
    for k in range(1, 8):
        mine, others = own_role[k - 1], other_role[k - 1]
        of_core_0 = [
            part(left_all, k * CAP, CAP, others.at[pl.ds(CAP, CAP)], 1 + 2 * k),
            part(right_all, 2 * k * CAP, 2 * CAP, mine, 2 + 2 * k),
        ]
        of_core_1 = [
            part(left_all, k * CAP, CAP, mine.at[pl.ds(0, CAP)], 1 + 2 * k),
            part(right_all, 2 * k * CAP, 2 * CAP, others, 2 + 2 * k),
        ]
        copies += of_core_0

        @pl.when(core == 0)
        def _():
            for copy in of_core_0:
                copy.start()

        @pl.when(core == 1)
        def _():
            for copy in of_core_1:
                copy.start()

    left_all[8 * CAP] = jnp.zeros((BS, BS), BF16)
    acc_ref[32] = jnp.zeros((BS, BS), F32)
    first_row = place_ref[0] * 4
    first_col = place_ref[1] * 8
    for n in range(4):
        col_grid_ref[core * 4 + n] = col_own_ref[n]
        col_grid_ref[(1 - core) * 4 + n] = col_other_ref[n]
    shift = shift_ref[0]
    scale = scaling(frob_ref)
    eye = identity()
    dot = functools.partial(jnp.dot, preferred_element_type=F32)
    for i in range(4):
        for j in range(8):
            block = (slice(i * BS, (i + 1) * BS), slice(j * BS, (j + 1) * BS))
            kept = pattern_ref[i, j] != 0
            diagonal = first_row + i == first_col + j

            @pl.when(kept)
            def _():
                here = core_ref[block]
                wide = here.astype(F32)
                acc_ref[i * 8 + j] = dot(row_grid_ref[i], here) + dot(here, col_grid_ref[j]) - 2.0 * shift * wide

                @pl.when(diagonal)
                def _():
                    grid = row_grid_ref[i]
                    grid_wide = grid.astype(F32)
                    acc_ref[i * 8 + j] += dot(grid, grid) - 2.0 * shift * grid_wide + shift * shift * eye
                    scaled_ref[block] = ((wide + grid_wide - shift * eye) * scale).astype(BF16)

                @pl.when(jnp.logical_not(diagonal))
                def _():
                    scaled_ref[block] = (wide * scale).astype(BF16)

            @pl.when(jnp.logical_not(kept))
            def _():
                scaled_ref[block] = jnp.zeros((BS, BS), BF16)
                square_ref[block] = jnp.zeros((BS, BS), BF16)

    for copy in copies:
        copy.wait()

    def turn(t, carry):
        sums = []
        for group in range(TURN):
            at = [(t * TURN + group) * GROUP + n for n in range(GROUP)]
            left = jnp.concatenate([left_all[left_ref[n]] for n in at], axis=1)
            right = jnp.concatenate([right_all[right_ref[n]] for n in at], axis=0)
            sums.append(dot(left, right))
        for group in range(TURN):
            acc_ref[out_ref[t * TURN + group]] += sums[group]
        return carry

    lax.fori_loop(0, turns_ref[0], turn, 0)
    for i in range(4):
        for j in range(8):
            block = (slice(i * BS, (i + 1) * BS), slice(j * BS, (j + 1) * BS))

            @pl.when(pattern_ref[i, j] != 0)
            def _():
                square_ref[block] = (acc_ref[i * 8 + j] * (scale * scale)).astype(BF16)


VM = pl.BlockSpec(memory_space=pltpu.VMEM)
SM = pl.BlockSpec(memory_space=pltpu.SMEM)
ANY = pl.BlockSpec(memory_space=pl.ANY)


def to_all(value, axis, count, groups=None):
    copies = jnp.broadcast_to(value[None], (count,) + value.shape)
    return lax.all_to_all(copies, axis, 0, 0, axis_index_groups=groups)


def place_of(device):
    row, col = device // 8, device % 8
    return row // 2 % 4, col % 2 * 2 + row // 8, col // 2, row % 2


def device_of(x, y, z, core):
    return ((y % 2 * 4 + x % 4) * 2 + core) * 8 + z % 4 * 2 + y // 2


def move(value, where):
    return lax.ppermute(value, ("row", "col"), [(k, device_of(*where(*place_of(k)))) for k in range(128)])


def ring(value, off):
    return move(value, lambda x, y, z, core: (x, y, z - off, core) if core else (x - off, y, z, core))


def across_y(value):
    return move(value, lambda x, y, z, core: (x, 3 - y if core else y ^ 1, z, core))


def across_y_again(value):
    return move(value, lambda x, y, z, core: (x, y ^ 1 if core else y, z, core))


def to_core(value):
    return lax.ppermute(value, "row", [(k, k ^ 1) for k in range(16)])


def lasting(microseconds):
    return pl.CostEstimate(flops=int(microseconds * 1e9), bytes_accessed=2**20, transcendentals=0)


def body(core_matrix, pattern, shift, potential, home, centres, exponents, extents):
    row = lax.axis_index("row")
    col = lax.axis_index("col")
    place = jnp.stack([row, col]).astype(jnp.int32)

    brick = pl.pallas_call(
        brick_kernel,
        in_specs=[SM, VM],
        out_specs=VM,
        out_shape=jax.ShapeDtypeStruct((80, BS), BF16),
        compiler_params=params(4),
        cost_estimate=lasting(1),
        name="brick",
    )(pattern, potential.reshape(64, BS))
    same_core = [[row * 8 + col for row in range(core, 16, 2) for col in range(8)] for core in range(2)]
    half = to_all(brick, ("row", "col"), 64, same_core)

    (core_after_brick, _) = lax.optimization_barrier((core_matrix, brick))
    payload, squares = pl.pallas_call(
        pack_kernel,
        in_specs=[SM, SM, VM],
        out_specs=[VM, VM],
        out_shape=[jax.ShapeDtypeStruct((CAP * BS, BS), BF16), jax.ShapeDtypeStruct((8, BS), F32)],
        compiler_params=params(4),
        cost_estimate=lasting(2),
        name="pack",
    )(pattern, place, core_after_brick)
    payload = payload.reshape(CAP, BS, BS)
    crossed = to_core(payload)

    pair = jnp.concatenate([payload, crossed])
    step = across_y(pair)
    after, before = ring(pair, 1), ring(pair, -1)
    phi = pl.pallas_call(
        values_kernel,
        in_specs=[SM, VM, VM, VM],
        out_specs=VM,
        out_shape=jax.ShapeDtypeStruct((8, 8, BS, 8 * BS), BF16),
        scratch_shapes=[pltpu.VMEM((8, BS, BS), F32)],
        compiler_params=params(4),
        cost_estimate=lasting(10),
        name="values",
    )(place, centres, exponents, extents)
    half, phi, step, after, before = lax.optimization_barrier((half, phi, step, after, before))

    far = ring(after, 1)
    other = across_y_again(step)
    bricks = jnp.concatenate([half, to_core(half)])

    def grid_blocks(with_sum, *more):
        extra = [VM, VM] if with_sum else []
        out_shape = [jax.ShapeDtypeStruct((4, BS, BS), BF16)]
        if with_sum:
            out_shape.append(jax.ShapeDtypeStruct((1, BS), F32))
        return pl.pallas_call(
            functools.partial(grid_kernel, with_sum),
            in_specs=[SM, SM, SM, VM, VM] + extra,
            out_specs=[VM] * len(out_shape),
            out_shape=out_shape,
            compiler_params=params(8),
            cost_estimate=lasting(5),
            name="grid_rows" if with_sum else "grid_cols",
        )(place, home, shift, bricks, phi, *more)

    row_grid, total = grid_blocks(True, core_matrix, squares)
    after, before, far, other, row_grid, total, bricks = lax.optimization_barrier(
        (after, before, far, other, row_grid, total, bricks)
    )

    other_after, other_before = ring(other, 1), ring(other, -1)
    crossings = [to_core(after), to_core(far), to_core(before)]
    (col_grid,) = grid_blocks(False)
    other_after, other_before, col_grid, total, bricks, *crossings = lax.optimization_barrier(
        (other_after, other_before, col_grid, total, bricks, *crossings)
    )

    other_far = ring(other_before, -1)
    crossings += [to_core(other), to_core(other_after), to_core(other_before)]
    col_grid_crossed = to_core(col_grid)
    frob = to_all(total, ("row", "col"), 128).reshape(128, BS)
    *listed, most = pl.pallas_call(
        plan_kernel,
        in_specs=[SM, VM],
        out_specs=[SM] * 5,
        out_shape=[
            jax.ShapeDtypeStruct((1,), jnp.int32),
            jax.ShapeDtypeStruct((LISTED // GROUP,), jnp.int32),
            jax.ShapeDtypeStruct((LISTED,), jnp.int32),
            jax.ShapeDtypeStruct((LISTED,), jnp.int32),
            jax.ShapeDtypeStruct((1,), jnp.int32),
        ],
        scratch_shapes=[pltpu.VMEM((40, BS), jnp.int32), pltpu.SMEM((40, BS), jnp.int32)]
        + [pltpu.SMEM((72,), jnp.int32)] * 3
        + [pltpu.SemaphoreType.DMA],
        compiler_params=params(4),
        cost_estimate=lasting(9),
        name="plan",
    )(place, bricks)
    other_far, col_grid_crossed, frob, *rest = lax.optimization_barrier(
        (other_far, col_grid_crossed, frob, *crossings, *listed)
    )
    crossings, listed = rest[:6], rest[6:]

    crossings.insert(5, to_core(other_far))
    own_role = [after, far, before, other, other_after, other_far, other_before]
    overflow = most[0] > CAP

    def sparse():
        return pl.pallas_call(
            product_kernel,
            in_specs=[SM] * 7 + [VM] * 5 + [ANY] * 16,
            out_specs=[VM, VM],
            out_shape=[jax.ShapeDtypeStruct((512, 1024), BF16)] * 2,
            scratch_shapes=[
                pltpu.VMEM((8 * CAP + 1, BS, BS), BF16),
                pltpu.VMEM((16 * CAP, BS, BS), BF16),
                pltpu.VMEM((33, BS, BS), F32),
                pltpu.VMEM((8, BS, BS), BF16),
                pltpu.SemaphoreType.DMA((17,)),
            ],
            compiler_params=params(24),
            cost_estimate=lasting(12),
            name="product",
        )(place, pattern, shift, *listed, frob, core_matrix, row_grid, col_grid, col_grid_crossed, payload, crossed, *own_role, *crossings)

    def dense():
        keep = pattern.astype(F32)[:, None, :, None]
        numbers_row = row * 4 + jnp.arange(4)
        numbers_col = col * 8 + jnp.arange(8)
        on = (numbers_row[:, None] == numbers_col[None, :]).astype(F32)
        grid = row_grid.astype(F32) - shift[0] * jnp.eye(BS, dtype=F32)
        whole = core_matrix.astype(F32).reshape(4, BS, 8, BS) + on[:, None, :, None] * grid[:, :, None, :]
        whole = (whole * keep).reshape(512, 1024)
        scaled = (whole * lax.rsqrt(jnp.sum(frob) / ORDER + 1e-6)).astype(BF16)
        product = jnp.dot(
            lax.all_gather(scaled, "col", axis=1, tiled=True),
            lax.all_gather(scaled, "row", axis=0, tiled=True),
            preferred_element_type=F32,
        )
        square = (product.reshape(4, BS, 8, BS) * keep).reshape(512, 1024).astype(BF16)
        return scaled, square

    return tuple(lax.cond(overflow, lambda: tuple(dense()), lambda: tuple(sparse())))


def solution(mesh):
    in_specs = (P("row", "col"), P("row", "col"), P(), P("row", "col", None), P(), P(), P(), P())
    out_specs = (P("row", "col"), P("row", "col"))
    return jax.shard_map(body, mesh=mesh, in_specs=in_specs, out_specs=out_specs, check_vma=False)
```

```python
import functools

import jax
import jax.numpy as jnp
from jax import lax
from jax.experimental import pallas as pl
from jax.experimental.pallas import tpu as pltpu
from jax.sharding import PartitionSpec as P

BS = 128
CAP = 20
GROUP = 4
TURN = 4
ORDER = 8192
VOLUME = 0.015625
LISTED = 2048 + 32 * GROUP + TURN * GROUP
F32 = jnp.float32
BF16 = jnp.bfloat16


def params(mebibytes):
    return pltpu.CompilerParams(vmem_limit_bytes=mebibytes * 2**20)


def pack_kernel(pattern_ref, place_ref, core_ref, payload_ref, sum_ref):
    first_row = place_ref[0] * 4
    first_col = place_ref[1] * 8
    sum_ref[...] = jnp.zeros_like(sum_ref)

    def put(i, j, slot):
        payload_ref[pl.ds(pl.multiple_of(slot * BS, BS), BS), :] = core_ref[
            i * BS : (i + 1) * BS, j * BS : (j + 1) * BS
        ]

    slot = jnp.int32(0)
    for i in range(4):
        for j in range(8):
            kept = pattern_ref[i, j] != 0

            @pl.when(kept & (slot < CAP))
            def _():
                put(i, j, slot)

            @pl.when(kept & (first_row + i != first_col + j))
            def _():
                block = core_ref[i * BS : (i + 1) * BS, j * BS : (j + 1) * BS].astype(F32)
                squares = (block * block).reshape(16, 8, BS)
                sum_ref[...] += jnp.sum(squares, axis=0)

            slot += kept.astype(jnp.int32)
    for i in range(4):
        for j in range(8):
            dropped = pattern_ref[i, j] == 0

            @pl.when(dropped & (slot < CAP))
            def _():
                put(i, j, slot)

            slot += dropped.astype(jnp.int32)


def brick_kernel(pattern_ref, potential_ref, brick_ref):
    brick_ref[:64] = potential_ref[...].astype(BF16)
    rows = lax.broadcasted_iota(jnp.int32, (16, BS), 0)
    columns = lax.broadcasted_iota(jnp.int32, (16, BS), 1)
    note = jnp.zeros((16, BS), F32)
    for i in range(4):
        for j in range(8):
            note = jnp.where((rows == 0) & (columns == i * 8 + j), pattern_ref[i, j].astype(F32), note)
    brick_ref[64:] = note.astype(BF16)


def column(row_values):
    return jnp.broadcast_to(row_values, (BS, BS)).T


def values_kernel(place_ref, centres_ref, exponents_ref, extents_ref, phi_ref, along_ref):
    row, col = place_ref[0], place_ref[1]

    k = pl.program_id(0)
    cluster = jnp.where(k < 4, row * 4 + k, col * 8 + row % 2 * 4 + k - 4)
    decay = column(exponents_ref[pl.ds(cluster, 1), :])
    reach = column(extents_ref[pl.ds(cluster, 1), :].astype(F32))
    cut = jnp.exp(-decay * (reach * reach + 0.5))
    at_x = column(centres_ref[0, pl.ds(cluster, 1), :].astype(F32))
    at_y = column(centres_ref[1, pl.ds(cluster, 1), :].astype(F32))
    at_z = column(centres_ref[2, pl.ds(cluster, 1), :].astype(F32))
    off_z = lax.broadcasted_iota(jnp.int32, (BS, BS), 1).astype(F32) - at_z
    along_z = jnp.exp(-decay * (off_z * off_z))
    for y in range(8):
        off_y = y - at_y
        along_ref[y] = jnp.exp(-decay * (off_y * off_y))
    for x in range(8):
        off_x = x - at_x
        along_xz = along_z * jnp.exp(-decay * (off_x * off_x))
        for y in range(8):
            phi = along_xz * along_ref[y]
            phi_ref[0, x, :, y * BS : (y + 1) * BS] = jnp.where(phi >= cut, phi, 0.0).astype(BF16)


def grid_kernel(with_sum, place_ref, home_ref, shift_ref, bricks_ref, phi_ref, *rest):
    if with_sum:
        core_ref, sum_ref, blocks_ref, total_ref = rest
    else:
        (blocks_ref,) = rest
    row, col = place_ref[0], place_ref[1]
    first = row * 4 if with_sum else col * 8 + row % 2 * 4

    k = pl.program_id(0)
    home = home_ref[first + k]
    index = (home // 8 ^ row) % 2 * 64 + home // 16 * 8 + home % 8
    total = jnp.zeros((BS, BS), F32)
    for x in range(8):
        values = jnp.concatenate([bricks_ref[index, x * 8 + y : x * 8 + y + 1, :] for y in range(8)], axis=1)
        phi = phi_ref[0, x]
        total += lax.dot_general(phi * values, phi, (((1,), (1,)), ((), ())), preferred_element_type=F32)
    blocks_ref[k] = (total * VOLUME).astype(BF16)
    if with_sum:

        @pl.when(k == 0)
        def _():
            total_ref[...] = jnp.sum(sum_ref[...], axis=0, keepdims=True)

        @pl.when((k == 3) & (col == row // 2))
        def _():
            eye = identity()
            for i in range(4):
                corner = pl.multiple_of((row % 2 * 4 + i) * BS, BS)
                block = core_ref[i * BS : (i + 1) * BS, pl.ds(corner, BS)].astype(F32)
                block = block + blocks_ref[i].astype(F32) - shift_ref[0] * eye
                total_ref[...] += jnp.sum(block * block, axis=0, keepdims=True)


def identity():
    rows = lax.broadcasted_iota(jnp.int32, (BS, BS), 0)
    columns = lax.broadcasted_iota(jnp.int32, (BS, BS), 1)
    return (rows == columns).astype(F32)


def plan_kernel(
    place_ref, bricks_ref, turns_ref, out_ref, left_ref, right_ref, most_ref, slots_ref, slots, kept_left, kept_right, kept_at, sem
):
    row, col = place_ref[0], place_ref[1]
    kept = jnp.sum(bricks_ref[:, 64:80, :].astype(F32), axis=1)
    kept = kept.T
    earlier = lax.broadcasted_iota(jnp.int32, (BS, BS), 1) < lax.broadcasted_iota(jnp.int32, (BS, BS), 0)
    before = jnp.dot(earlier.astype(BF16), kept.astype(BF16), preferred_element_type=F32)
    slots_ref[...] = jnp.where(kept > 0.5, before, -1.0)[:40].astype(jnp.int32)
    most_ref[0] = jnp.max(jnp.sum(kept, axis=0, keepdims=True)).astype(jnp.int32)
    copy = pltpu.make_async_copy(slots_ref, slots, sem)
    copy.start()
    copy.wait()

    def block_row(i, number):
        def piece(other, count):
            device = row // 2 * 8 + other
            base = ((other ^ col) % 2 * 4 + (other // 2 - col // 2) % 4) * CAP
            right = ((other // 4 ^ row // 8) * 4 + (other - row // 2) % 4) * 2 * CAP
            for j in range(8):
                slot = slots[i * 8 + j, device]
                kept_left[count] = base + slot
                kept_right[count] = right + j // 4 * CAP
                kept_at[count] = j % 4 * 8 * BS + (j // 4 ^ row) % 2 * 64 + other * 8 + col
                count += (slot >= 0).astype(jnp.int32)
            return count

        count = lax.fori_loop(0, 8, piece, jnp.int32(0))
        for more in range(3):
            kept_left[count + more] = 0
            kept_right[count + more] = 0
            kept_at[count + more] = 32 * BS

        def block(j, number):
            def listing(number):
                start = number // GROUP
                def four(n, number):
                    for inner in range(4):
                        at = kept_at[n * 4 + inner] + j * BS
                        slot = slots[at >> 7, at & 127]
                        left_ref[number] = kept_left[n * 4 + inner]
                        right_ref[number] = kept_right[n * 4 + inner] + slot
                        number += (slot >= 0).astype(jnp.int32)
                    return number

                number = lax.fori_loop(0, (count + 3) // 4, four, number)
                for more in range(GROUP - 1):
                    left_ref[number + more] = 8 * CAP
                    right_ref[number + more] = 0
                end = (number + GROUP - 1) // GROUP

                def name(group, carry):
                    out_ref[group] = i * 8 + j
                    return carry

                lax.fori_loop(start, end, name, 0)
                return end * GROUP

            wanted = slots[i * 8 + j, row // 2 * 8 + col] >= 0
            return lax.cond(wanted, listing, lambda n: n, number)

        return lax.fori_loop(0, 8, block, number)

    number = lax.fori_loop(0, 4, block_row, jnp.int32(0))
    groups = number // GROUP
    for more in range(TURN):
        out_ref[groups + more] = 32
        for inner in range(GROUP):
            left_ref[number + more * GROUP + inner] = 8 * CAP
            right_ref[number + more * GROUP + inner] = 0
    turns_ref[0] = (groups + TURN - 1) // TURN


def scaling(frob_ref):
    total = jnp.sum(frob_ref[...], axis=(0, 1), keepdims=True)
    return lax.rsqrt(total / ORDER + 1e-6)


def product_kernel(
    place_ref, pattern_ref, shift_ref, turns_ref, out_ref, left_ref, right_ref, frob_ref, core_ref, row_grid_ref, col_own_ref, col_other_ref,
    *rest
):
    payload, crossed, own_role, other_role = rest[0], rest[1], rest[2:9], rest[9:16]
    scaled_ref, square_ref, left_all, right_all, acc_ref, col_grid_ref, sems = rest[16:]
    core = place_ref[0] % 2

    def part(whole, at, size, source, number):
        return pltpu.make_async_copy(source, whole.at[pl.ds(at, size)], sems.at[number])

    copies = [
        part(left_all, 0, CAP, payload, 0),
        part(right_all, core * CAP, CAP, payload, 1),
        part(right_all, (1 - core) * CAP, CAP, crossed, 2),
    ]
    for copy in copies:
        copy.start()
    for k in range(1, 8):
        mine, others = own_role[k - 1], other_role[k - 1]
        of_core_0 = [
            part(left_all, k * CAP, CAP, others.at[pl.ds(CAP, CAP)], 1 + 2 * k),
            part(right_all, 2 * k * CAP, 2 * CAP, mine, 2 + 2 * k),
        ]
        of_core_1 = [
            part(left_all, k * CAP, CAP, mine.at[pl.ds(0, CAP)], 1 + 2 * k),
            part(right_all, 2 * k * CAP, 2 * CAP, others, 2 + 2 * k),
        ]
        copies += of_core_0

        @pl.when(core == 0)
        def _():
            for copy in of_core_0:
                copy.start()

        @pl.when(core == 1)
        def _():
            for copy in of_core_1:
                copy.start()

    left_all[8 * CAP] = jnp.zeros((BS, BS), BF16)
    acc_ref[32] = jnp.zeros((BS, BS), F32)
    first_row = place_ref[0] * 4
    first_col = place_ref[1] * 8
    for n in range(4):
        col_grid_ref[core * 4 + n] = col_own_ref[n]
        col_grid_ref[(1 - core) * 4 + n] = col_other_ref[n]
    shift = shift_ref[0]
    scale = scaling(frob_ref)
    eye = identity()
    dot = functools.partial(jnp.dot, preferred_element_type=F32)
    for i in range(4):
        for j in range(8):
            block = (slice(i * BS, (i + 1) * BS), slice(j * BS, (j + 1) * BS))
            kept = pattern_ref[i, j] != 0
            diagonal = first_row + i == first_col + j

            @pl.when(kept)
            def _():
                here = core_ref[block]
                wide = here.astype(F32)
                acc_ref[i * 8 + j] = dot(row_grid_ref[i], here) + dot(here, col_grid_ref[j]) - 2.0 * shift * wide

                @pl.when(diagonal)
                def _():
                    grid = row_grid_ref[i]
                    grid_wide = grid.astype(F32)
                    acc_ref[i * 8 + j] += dot(grid, grid) - 2.0 * shift * grid_wide + shift * shift * eye
                    scaled_ref[block] = ((wide + grid_wide - shift * eye) * scale).astype(BF16)

                @pl.when(jnp.logical_not(diagonal))
                def _():
                    scaled_ref[block] = (wide * scale).astype(BF16)

            @pl.when(jnp.logical_not(kept))
            def _():
                scaled_ref[block] = jnp.zeros((BS, BS), BF16)
                square_ref[block] = jnp.zeros((BS, BS), BF16)

    for copy in copies:
        copy.wait()

    def turn(t, carry):
        sums = []
        for group in range(TURN):
            at = [(t * TURN + group) * GROUP + n for n in range(GROUP)]
            left = jnp.concatenate([left_all[left_ref[n]] for n in at], axis=1)
            right = jnp.concatenate([right_all[right_ref[n]] for n in at], axis=0)
            sums.append(dot(left, right))
        for group in range(TURN):
            acc_ref[out_ref[t * TURN + group]] += sums[group]
        return carry

    lax.fori_loop(0, turns_ref[0], turn, 0)
    for i in range(4):
        for j in range(8):
            block = (slice(i * BS, (i + 1) * BS), slice(j * BS, (j + 1) * BS))

            @pl.when(pattern_ref[i, j] != 0)
            def _():
                square_ref[block] = (acc_ref[i * 8 + j] * (scale * scale)).astype(BF16)


VM = pl.BlockSpec(memory_space=pltpu.VMEM)
SM = pl.BlockSpec(memory_space=pltpu.SMEM)
ANY = pl.BlockSpec(memory_space=pl.ANY)


def to_all(value, axis, count, groups=None):
    copies = jnp.broadcast_to(value[None], (count,) + value.shape)
    return lax.all_to_all(copies, axis, 0, 0, axis_index_groups=groups)


def place_of(device):
    row, col = device // 8, device % 8
    return row // 2 % 4, col % 2 * 2 + row // 8, col // 2, row % 2


def device_of(x, y, z, core):
    return ((y % 2 * 4 + x % 4) * 2 + core) * 8 + z % 4 * 2 + y // 2


def move(value, where):
    return lax.ppermute(value, ("row", "col"), [(k, device_of(*where(*place_of(k)))) for k in range(128)])


def ring(value, off):
    return move(value, lambda x, y, z, core: (x, y, z - off, core) if core else (x - off, y, z, core))


def across_y(value):
    return move(value, lambda x, y, z, core: (x, 3 - y if core else y ^ 1, z, core))


def across_y_again(value):
    return move(value, lambda x, y, z, core: (x, y ^ 1 if core else y, z, core))


def to_core(value):
    return lax.ppermute(value, "row", [(k, k ^ 1) for k in range(16)])


def lasting(microseconds):
    return pl.CostEstimate(flops=int(microseconds * 1e9), bytes_accessed=2**20, transcendentals=0)


def body(core_matrix, pattern, shift, potential, home, centres, exponents, extents):
    row = lax.axis_index("row")
    col = lax.axis_index("col")
    place = jnp.stack([row, col]).astype(jnp.int32)

    brick = pl.pallas_call(
        brick_kernel,
        in_specs=[SM, VM],
        out_specs=VM,
        out_shape=jax.ShapeDtypeStruct((80, BS), BF16),
        compiler_params=params(4),
        cost_estimate=lasting(1),
        name="brick",
    )(pattern, potential.reshape(64, BS))
    same_core = [[row * 8 + col for row in range(core, 16, 2) for col in range(8)] for core in range(2)]
    half = to_all(brick, ("row", "col"), 64, same_core)

    (core_after_brick, _) = lax.optimization_barrier((core_matrix, brick))
    payload, squares = pl.pallas_call(
        pack_kernel,
        in_specs=[SM, SM, VM],
        out_specs=[VM, VM],
        out_shape=[jax.ShapeDtypeStruct((CAP * BS, BS), BF16), jax.ShapeDtypeStruct((8, BS), F32)],
        compiler_params=params(4),
        cost_estimate=lasting(2),
        name="pack",
    )(pattern, place, core_after_brick)
    payload = payload.reshape(CAP, BS, BS)
    crossed = to_core(payload)

    pair = jnp.concatenate([payload, crossed])
    step = across_y(pair)
    after, before = ring(pair, 1), ring(pair, -1)
    phi = pl.pallas_call(
        values_kernel,
        grid=(8,),
        in_specs=[SM, VM, VM, VM],
        out_specs=pl.BlockSpec((1, 8, BS, 8 * BS), lambda k: (k, 0, 0, 0)),
        out_shape=jax.ShapeDtypeStruct((8, 8, BS, 8 * BS), BF16),
        scratch_shapes=[pltpu.VMEM((8, BS, BS), F32)],
        compiler_params=params(8),
        cost_estimate=lasting(10),
        name="values",
    )(place, centres, exponents, extents)
    half, phi, step, after, before = lax.optimization_barrier((half, phi, step, after, before))

    far = ring(after, 1)
    other = across_y_again(step)
    bricks = jnp.concatenate([half, to_core(half)])

    def grid_blocks(with_sum, *more):
        extra = [VM, VM] if with_sum else []
        first = 0 if with_sum else 4
        out_shape = [jax.ShapeDtypeStruct((4, BS, BS), BF16)]
        if with_sum:
            out_shape.append(jax.ShapeDtypeStruct((1, BS), F32))
        return pl.pallas_call(
            functools.partial(grid_kernel, with_sum),
            grid=(4,),
            in_specs=[SM, SM, SM, VM, pl.BlockSpec((1, 8, BS, 8 * BS), lambda k: (first + k, 0, 0, 0))] + extra,
            out_specs=[VM] * len(out_shape),
            out_shape=out_shape,
            compiler_params=params(8),
            cost_estimate=lasting(5),
            name="grid_rows" if with_sum else "grid_cols",
        )(place, home, shift, bricks, phi, *more)

    row_grid, total = grid_blocks(True, core_matrix, squares)
    after, before, far, other, row_grid, bricks = lax.optimization_barrier(
        (after, before, far, other, row_grid, bricks)
    )

    other_after, other_before = ring(other, 1), ring(other, -1)
    crossings = [to_core(after), to_core(far), to_core(before)]
    (col_grid,) = grid_blocks(False)
    frob = to_all(total, ("row", "col"), 128).reshape(128, BS)
    other_after, other_before, col_grid, frob, bricks, *crossings = lax.optimization_barrier(
        (other_after, other_before, col_grid, frob, bricks, *crossings)
    )

    other_far = ring(other_before, -1)
    crossings += [to_core(other), to_core(other_after), to_core(other_before)]
    col_grid_crossed = to_core(col_grid)
    *listed, most = pl.pallas_call(
        plan_kernel,
        in_specs=[SM, VM],
        out_specs=[SM] * 5,
        out_shape=[
            jax.ShapeDtypeStruct((1,), jnp.int32),
            jax.ShapeDtypeStruct((LISTED // GROUP,), jnp.int32),
            jax.ShapeDtypeStruct((LISTED,), jnp.int32),
            jax.ShapeDtypeStruct((LISTED,), jnp.int32),
            jax.ShapeDtypeStruct((1,), jnp.int32),
        ],
        scratch_shapes=[pltpu.VMEM((40, BS), jnp.int32), pltpu.SMEM((40, BS), jnp.int32)]
        + [pltpu.SMEM((72,), jnp.int32)] * 3
        + [pltpu.SemaphoreType.DMA],
        compiler_params=params(4),
        cost_estimate=lasting(9),
        name="plan",
    )(place, bricks)
    other_far, col_grid_crossed, *rest = lax.optimization_barrier(
        (other_far, col_grid_crossed, *crossings, *listed)
    )
    crossings, listed = rest[:6], rest[6:]

    crossings.insert(5, to_core(other_far))
    own_role = [after, far, before, other, other_after, other_far, other_before]
    overflow = most[0] > CAP

    def sparse():
        return pl.pallas_call(
            product_kernel,
            in_specs=[SM] * 7 + [VM] * 5 + [ANY] * 16,
            out_specs=[VM, VM],
            out_shape=[jax.ShapeDtypeStruct((512, 1024), BF16)] * 2,
            scratch_shapes=[
                pltpu.VMEM((8 * CAP + 1, BS, BS), BF16),
                pltpu.VMEM((16 * CAP, BS, BS), BF16),
                pltpu.VMEM((33, BS, BS), F32),
                pltpu.VMEM((8, BS, BS), BF16),
                pltpu.SemaphoreType.DMA((17,)),
            ],
            compiler_params=params(24),
            cost_estimate=lasting(12),
            name="product",
        )(place, pattern, shift, *listed, frob, core_matrix, row_grid, col_grid, col_grid_crossed, payload, crossed, *own_role, *crossings)

    def dense():
        keep = pattern.astype(F32)[:, None, :, None]
        numbers_row = row * 4 + jnp.arange(4)
        numbers_col = col * 8 + jnp.arange(8)
        on = (numbers_row[:, None] == numbers_col[None, :]).astype(F32)
        grid = row_grid.astype(F32) - shift[0] * jnp.eye(BS, dtype=F32)
        whole = core_matrix.astype(F32).reshape(4, BS, 8, BS) + on[:, None, :, None] * grid[:, :, None, :]
        whole = (whole * keep).reshape(512, 1024)
        scaled = (whole * lax.rsqrt(jnp.sum(frob) / ORDER + 1e-6)).astype(BF16)
        product = jnp.dot(
            lax.all_gather(scaled, "col", axis=1, tiled=True),
            lax.all_gather(scaled, "row", axis=0, tiled=True),
            preferred_element_type=F32,
        )
        square = (product.reshape(4, BS, 8, BS) * keep).reshape(512, 1024).astype(BF16)
        return scaled, square

    return tuple(lax.cond(overflow, lambda: tuple(dense()), lambda: tuple(sparse())))


def solution(mesh):
    in_specs = (P("row", "col"), P("row", "col"), P(), P("row", "col", None), P(), P(), P(), P())
    out_specs = (P("row", "col"), P("row", "col"))
    return jax.shard_map(body, mesh=mesh, in_specs=in_specs, out_specs=out_specs, check_vma=False)
```

```python
import functools

import jax
import jax.numpy as jnp
from jax import lax
from jax.experimental import pallas as pl
from jax.experimental.pallas import tpu as pltpu
from jax.sharding import PartitionSpec as P

BS = 128
CAP = 20
GROUP = 4
TURN = 4
ORDER = 8192
VOLUME = 0.015625
LISTED = 2048 + 32 * GROUP + TURN * GROUP
F32 = jnp.float32
BF16 = jnp.bfloat16


def params(mebibytes):
    return pltpu.CompilerParams(vmem_limit_bytes=mebibytes * 2**20)


def pack_kernel(pattern_ref, place_ref, core_ref, payload_ref, sum_ref):
    first_row = place_ref[0] * 4
    first_col = place_ref[1] * 8
    sum_ref[...] = jnp.zeros_like(sum_ref)

    def put(i, j, slot):
        payload_ref[pl.ds(pl.multiple_of(slot * BS, BS), BS), :] = core_ref[
            i * BS : (i + 1) * BS, j * BS : (j + 1) * BS
        ]

    slot = jnp.int32(0)
    for i in range(4):
        for j in range(8):
            kept = pattern_ref[i, j] != 0

            @pl.when(kept & (slot < CAP))
            def _():
                put(i, j, slot)

            @pl.when(kept & (first_row + i != first_col + j))
            def _():
                block = core_ref[i * BS : (i + 1) * BS, j * BS : (j + 1) * BS].astype(F32)
                squares = (block * block).reshape(16, 8, BS)
                sum_ref[...] += jnp.sum(squares, axis=0)

            slot += kept.astype(jnp.int32)
    for i in range(4):
        for j in range(8):
            dropped = pattern_ref[i, j] == 0

            @pl.when(dropped & (slot < CAP))
            def _():
                put(i, j, slot)

            slot += dropped.astype(jnp.int32)


def brick_kernel(pattern_ref, potential_ref, brick_ref):
    brick_ref[:64] = potential_ref[...].astype(BF16)
    rows = lax.broadcasted_iota(jnp.int32, (16, BS), 0)
    columns = lax.broadcasted_iota(jnp.int32, (16, BS), 1)
    note = jnp.zeros((16, BS), F32)
    for i in range(4):
        for j in range(8):
            note = jnp.where((rows == 0) & (columns == i * 8 + j), pattern_ref[i, j].astype(F32), note)
    brick_ref[64:] = note.astype(BF16)


def column(row_values):
    return jnp.broadcast_to(row_values, (BS, BS)).T


def values_kernel(place_ref, centres_ref, exponents_ref, extents_ref, phi_ref, along_ref, slots, sems):
    row, col = place_ref[0], place_ref[1]

    def copy(k):
        return pltpu.make_async_copy(slots.at[k % 2], phi_ref.at[k], sems.at[k % 2])

    def one(k, carry):
        @pl.when(k >= 2)
        def _():
            copy(k - 2).wait()

        cluster = jnp.where(k < 4, row * 4 + k, col * 8 + row % 2 * 4 + k - 4)
        decay = column(exponents_ref[pl.ds(cluster, 1), :])
        reach = column(extents_ref[pl.ds(cluster, 1), :].astype(F32))
        cut = jnp.exp(-decay * (reach * reach + 0.5))
        at_x = column(centres_ref[0, pl.ds(cluster, 1), :].astype(F32))
        at_y = column(centres_ref[1, pl.ds(cluster, 1), :].astype(F32))
        at_z = column(centres_ref[2, pl.ds(cluster, 1), :].astype(F32))
        off_z = lax.broadcasted_iota(jnp.int32, (BS, BS), 1).astype(F32) - at_z
        along_z = jnp.exp(-decay * (off_z * off_z))
        for y in range(8):
            off_y = y - at_y
            along_ref[y] = jnp.exp(-decay * (off_y * off_y))
        for x in range(8):
            off_x = x - at_x
            along_xz = along_z * jnp.exp(-decay * (off_x * off_x))
            for y in range(8):
                phi = along_xz * along_ref[y]
                slots[k % 2, x, :, y * BS : (y + 1) * BS] = jnp.where(phi >= cut, phi, 0.0).astype(BF16)
        copy(k).start()
        return carry

    lax.fori_loop(0, 8, one, 0)
    copy(6).wait()
    copy(7).wait()


def grid_kernel(with_sum, place_ref, home_ref, shift_ref, bricks_ref, phi_ref, *rest):
    if with_sum:
        core_ref, sum_ref, blocks_ref, total_ref, slots, sems = rest
    else:
        blocks_ref, slots, sems = rest
    row, col = place_ref[0], place_ref[1]
    first = row * 4 if with_sum else col * 8 + row % 2 * 4
    place = 0 if with_sum else 4

    def copy(k):
        return pltpu.make_async_copy(phi_ref.at[place + k], slots.at[k], sems.at[k])

    for k in range(4):
        copy(k).start()

    def one(k, carry):
        home = home_ref[first + k]
        index = (home // 8 ^ row) % 2 * 64 + home // 16 * 8 + home % 8
        copy(k).wait()
        total = jnp.zeros((BS, BS), F32)
        for x in range(8):
            values = jnp.concatenate([bricks_ref[index, x * 8 + y : x * 8 + y + 1, :] for y in range(8)], axis=1)
            phi = slots[k, x]
            total += lax.dot_general(phi * values, phi, (((1,), (1,)), ((), ())), preferred_element_type=F32)
        blocks_ref[k] = (total * VOLUME).astype(BF16)
        return carry

    lax.fori_loop(0, 4, one, 0)
    if with_sum:
        total_ref[...] = jnp.sum(sum_ref[...], axis=0, keepdims=True)

        @pl.when(col == row // 2)
        def _():
            eye = identity()
            for i in range(4):
                corner = pl.multiple_of((row % 2 * 4 + i) * BS, BS)
                block = core_ref[i * BS : (i + 1) * BS, pl.ds(corner, BS)].astype(F32)
                block = block + blocks_ref[i].astype(F32) - shift_ref[0] * eye
                total_ref[...] += jnp.sum(block * block, axis=0, keepdims=True)


def identity():
    rows = lax.broadcasted_iota(jnp.int32, (BS, BS), 0)
    columns = lax.broadcasted_iota(jnp.int32, (BS, BS), 1)
    return (rows == columns).astype(F32)


def plan_kernel(
    place_ref, bricks_ref, turns_ref, out_ref, left_ref, right_ref, most_ref, slots_ref, slots, kept_left, kept_right, kept_at, sem
):
    row, col = place_ref[0], place_ref[1]
    kept = jnp.sum(bricks_ref[:, 64:80, :].astype(F32), axis=1)
    kept = kept.T
    earlier = lax.broadcasted_iota(jnp.int32, (BS, BS), 1) < lax.broadcasted_iota(jnp.int32, (BS, BS), 0)
    before = jnp.dot(earlier.astype(BF16), kept.astype(BF16), preferred_element_type=F32)
    slots_ref[...] = jnp.where(kept > 0.5, before, -1.0)[:40].astype(jnp.int32)
    most_ref[0] = jnp.max(jnp.sum(kept, axis=0, keepdims=True)).astype(jnp.int32)
    copy = pltpu.make_async_copy(slots_ref, slots, sem)
    copy.start()
    copy.wait()

    def block_row(i, number):
        def piece(other, count):
            device = row // 2 * 8 + other
            base = ((other ^ col) % 2 * 4 + (other // 2 - col // 2) % 4) * CAP
            right = ((other // 4 ^ row // 8) * 4 + (other - row // 2) % 4) * 2 * CAP
            for j in range(8):
                slot = slots[i * 8 + j, device]
                kept_left[count] = base + slot
                kept_right[count] = right + j // 4 * CAP
                kept_at[count] = j % 4 * 8 * BS + (j // 4 ^ row) % 2 * 64 + other * 8 + col
                count += (slot >= 0).astype(jnp.int32)
            return count

        count = lax.fori_loop(0, 8, piece, jnp.int32(0))
        for more in range(3):
            kept_left[count + more] = 0
            kept_right[count + more] = 0
            kept_at[count + more] = 32 * BS

        def block(j, number):
            def listing(number):
                start = number // GROUP
                def four(n, number):
                    for inner in range(4):
                        at = kept_at[n * 4 + inner] + j * BS
                        slot = slots[at >> 7, at & 127]
                        left_ref[number] = kept_left[n * 4 + inner]
                        right_ref[number] = kept_right[n * 4 + inner] + slot
                        number += (slot >= 0).astype(jnp.int32)
                    return number

                number = lax.fori_loop(0, (count + 3) // 4, four, number)
                for more in range(GROUP - 1):
                    left_ref[number + more] = 8 * CAP
                    right_ref[number + more] = 0
                end = (number + GROUP - 1) // GROUP

                def name(group, carry):
                    out_ref[group] = i * 8 + j
                    return carry

                lax.fori_loop(start, end, name, 0)
                return end * GROUP

            wanted = slots[i * 8 + j, row // 2 * 8 + col] >= 0
            return lax.cond(wanted, listing, lambda n: n, number)

        return lax.fori_loop(0, 8, block, number)

    number = lax.fori_loop(0, 4, block_row, jnp.int32(0))
    groups = number // GROUP
    for more in range(TURN):
        out_ref[groups + more] = 32
        for inner in range(GROUP):
            left_ref[number + more * GROUP + inner] = 8 * CAP
            right_ref[number + more * GROUP + inner] = 0
    turns_ref[0] = (groups + TURN - 1) // TURN


def scaling(frob_ref):
    total = jnp.sum(frob_ref[...], axis=(0, 1), keepdims=True)
    return lax.rsqrt(total / ORDER + 1e-6)


def product_kernel(
    place_ref, pattern_ref, shift_ref, turns_ref, out_ref, left_ref, right_ref, frob_ref, core_ref, row_grid_ref, col_own_ref, col_other_ref,
    *rest
):
    payload, crossed, own_role, other_role, halves = rest[0], rest[1], rest[2:9], rest[9:16], rest[16:18]
    scaled_ref, square_ref, left_all, right_all, acc_ref, col_grid_ref, sems = rest[18:]
    core = place_ref[0] % 2

    def part(whole, at, size, source, number):
        return pltpu.make_async_copy(source, whole.at[pl.ds(at, size)], sems.at[number])

    copies = [
        part(left_all, 0, CAP, payload, 0),
        part(right_all, core * CAP, CAP, payload, 1),
        part(right_all, (1 - core) * CAP, CAP, crossed, 2),
    ]
    for copy in copies:
        copy.start()
    along_x = {1: 0, 2: 2, 3: 1, 4: 3, 5: 5, 6: 6, 7: 4}
    along_z = {1: 0, 2: 2, 3: 1, 4: 4, 5: 5, 7: 6}
    low, others_high = halves
    for k in range(1, 8):
        of_core_0 = [part(right_all, 2 * k * CAP, 2 * CAP, own_role[along_x[k]], 2 + 2 * k)]
        of_core_1 = [part(right_all, 2 * k * CAP, 2 * CAP, other_role[along_x[k]], 2 + 2 * k)]
        if k == 6:
            of_core_0.append(part(left_all, k * CAP, CAP, others_high, 1 + 2 * k))
            of_core_1.append(part(left_all, k * CAP, CAP, low, 1 + 2 * k))
        else:
            theirs, mine = other_role[along_z[k]], own_role[along_z[k]]
            of_core_0.append(part(left_all, k * CAP, CAP, theirs.at[pl.ds(CAP, CAP)], 1 + 2 * k))
            of_core_1.append(part(left_all, k * CAP, CAP, mine.at[pl.ds(0, CAP)], 1 + 2 * k))
        copies += of_core_0

        @pl.when(core == 0)
        def _():
            for copy in of_core_0:
                copy.start()

        @pl.when(core == 1)
        def _():
            for copy in of_core_1:
                copy.start()

    left_all[8 * CAP] = jnp.zeros((BS, BS), BF16)
    acc_ref[32] = jnp.zeros((BS, BS), F32)
    first_row = place_ref[0] * 4
    first_col = place_ref[1] * 8
    for n in range(4):
        col_grid_ref[core * 4 + n] = col_own_ref[n]
        col_grid_ref[(1 - core) * 4 + n] = col_other_ref[n]
    shift = shift_ref[0]
    scale = scaling(frob_ref)
    eye = identity()
    dot = functools.partial(jnp.dot, preferred_element_type=F32)
    for i in range(4):
        for j in range(8):
            block = (slice(i * BS, (i + 1) * BS), slice(j * BS, (j + 1) * BS))
            kept = pattern_ref[i, j] != 0
            diagonal = first_row + i == first_col + j

            @pl.when(kept)
            def _():
                here = core_ref[block]
                wide = here.astype(F32)
                acc_ref[i * 8 + j] = dot(row_grid_ref[i], here) + dot(here, col_grid_ref[j]) - 2.0 * shift * wide

                @pl.when(diagonal)
                def _():
                    grid = row_grid_ref[i]
                    grid_wide = grid.astype(F32)
                    acc_ref[i * 8 + j] += dot(grid, grid) - 2.0 * shift * grid_wide + shift * shift * eye
                    scaled_ref[block] = ((wide + grid_wide - shift * eye) * scale).astype(BF16)

                @pl.when(jnp.logical_not(diagonal))
                def _():
                    scaled_ref[block] = (wide * scale).astype(BF16)

            @pl.when(jnp.logical_not(kept))
            def _():
                scaled_ref[block] = jnp.zeros((BS, BS), BF16)
                square_ref[block] = jnp.zeros((BS, BS), BF16)

    for copy in copies:
        copy.wait()

    def turn(t, carry):
        sums = []
        for group in range(TURN):
            at = [(t * TURN + group) * GROUP + n for n in range(GROUP)]
            left = jnp.concatenate([left_all[left_ref[n]] for n in at], axis=1)
            right = jnp.concatenate([right_all[right_ref[n]] for n in at], axis=0)
            sums.append(dot(left, right))
        for group in range(TURN):
            acc_ref[out_ref[t * TURN + group]] += sums[group]
        return carry

    lax.fori_loop(0, turns_ref[0], turn, 0)
    for i in range(4):
        for j in range(8):
            block = (slice(i * BS, (i + 1) * BS), slice(j * BS, (j + 1) * BS))

            @pl.when(pattern_ref[i, j] != 0)
            def _():
                square_ref[block] = (acc_ref[i * 8 + j] * (scale * scale)).astype(BF16)


VM = pl.BlockSpec(memory_space=pltpu.VMEM)
SM = pl.BlockSpec(memory_space=pltpu.SMEM)
ANY = pl.BlockSpec(memory_space=pl.ANY)
HBM = pl.BlockSpec(memory_space=pltpu.HBM)


def to_all(value, axis, count, groups=None):
    copies = jnp.broadcast_to(value[None], (count,) + value.shape)
    return lax.all_to_all(copies, axis, 0, 0, axis_index_groups=groups)


def place_of(device):
    row, col = device // 8, device % 8
    return row // 2 % 4, col % 2 * 2 + row // 8, col // 2, row % 2


def device_of(x, y, z, core):
    return ((y % 2 * 4 + x % 4) * 2 + core) * 8 + z % 4 * 2 + y // 2


def move(value, where):
    return lax.ppermute(value, ("row", "col"), [(k, device_of(*where(*place_of(k)))) for k in range(128)])


def ring(value, off):
    return move(value, lambda x, y, z, core: (x, y, z - off, core) if core else (x - off, y, z, core))


def across_y(value):
    return move(value, lambda x, y, z, core: (x, 3 - y if core else y ^ 1, z, core))


def across_y_again(value):
    return move(value, lambda x, y, z, core: (x, y ^ 1, z, core) if core else (x + 1, y, z, core))


def ring_of_core_1(value, off):
    pairs = []
    for k in range(128):
        x, y, z, core = place_of(k)
        if core == 1:
            pairs.append((k, device_of(x, y, z - off, core)))
    return lax.ppermute(value, ("row", "col"), pairs)


def to_core(value):
    return lax.ppermute(value, "row", [(k, k ^ 1) for k in range(16)])


def lasting(microseconds):
    return pl.CostEstimate(flops=int(microseconds * 1e9), bytes_accessed=2**20, transcendentals=0)


def body(core_matrix, pattern, shift, potential, home, centres, exponents, extents):
    row = lax.axis_index("row")
    col = lax.axis_index("col")
    place = jnp.stack([row, col]).astype(jnp.int32)

    brick = pl.pallas_call(
        brick_kernel,
        in_specs=[SM, VM],
        out_specs=VM,
        out_shape=jax.ShapeDtypeStruct((80, BS), BF16),
        compiler_params=params(4),
        cost_estimate=lasting(1),
        name="brick",
    )(pattern, potential.reshape(64, BS))
    same_core = [[row * 8 + col for row in range(core, 16, 2) for col in range(8)] for core in range(2)]
    half = to_all(brick, ("row", "col"), 64, same_core)

    (core_after_brick, _) = lax.optimization_barrier((core_matrix, brick))
    payload, squares = pl.pallas_call(
        pack_kernel,
        in_specs=[SM, SM, VM],
        out_specs=[VM, VM],
        out_shape=[jax.ShapeDtypeStruct((CAP * BS, BS), BF16), jax.ShapeDtypeStruct((8, BS), F32)],
        compiler_params=params(4),
        cost_estimate=lasting(2),
        name="pack",
    )(pattern, place, core_after_brick)
    payload = payload.reshape(CAP, BS, BS)
    crossed = to_core(payload)

    pair = jnp.concatenate([payload, crossed])
    step = across_y(pair)
    after, before = ring(pair, 1), ring(pair, -1)
    phi = pl.pallas_call(
        values_kernel,
        in_specs=[SM, VM, VM, VM],
        out_specs=HBM,
        out_shape=jax.ShapeDtypeStruct((8, 8, BS, 8 * BS), BF16),
        scratch_shapes=[
            pltpu.VMEM((8, BS, BS), F32),
            pltpu.VMEM((2, 8, BS, 8 * BS), BF16),
            pltpu.SemaphoreType.DMA((2,)),
        ],
        compiler_params=params(49),
        cost_estimate=lasting(10),
        name="values",
    )(place, centres, exponents, extents)

    half, phi = lax.optimization_barrier((half, phi))
    far = ring(after, 1)
    second = across_y_again(step)
    bricks = jnp.concatenate([half, to_core(half)])

    def grid_blocks(with_sum, *more):
        extra = [VM, VM] if with_sum else []
        out_shape = [jax.ShapeDtypeStruct((4, BS, BS), BF16)]
        if with_sum:
            out_shape.append(jax.ShapeDtypeStruct((1, BS), F32))
        return pl.pallas_call(
            functools.partial(grid_kernel, with_sum),
            in_specs=[SM, SM, SM, VM, HBM] + extra,
            out_specs=[VM] * len(out_shape),
            out_shape=out_shape,
            scratch_shapes=[pltpu.VMEM((4, 8, BS, 8 * BS), BF16), pltpu.SemaphoreType.DMA((4,))],
            compiler_params=params(49),
            cost_estimate=lasting(5),
            name="grid_rows" if with_sum else "grid_cols",
        )(place, home, shift, bricks, phi, *more)

    row_grid, total = grid_blocks(True, core_matrix, squares)
    crossings = [to_core(after), to_core(before)]
    after, before, far, step, second, row_grid, total, bricks, *crossings = lax.optimization_barrier(
        (after, before, far, step, second, row_grid, total, bricks, *crossings)
    )

    third = ring(second, -1)
    other_after = ring(jnp.where(row % 2 == 0, step, second), 1)
    crossings += [to_core(far), to_core(step)]
    (col_grid,) = grid_blocks(False)
    *listed, most = pl.pallas_call(
        plan_kernel,
        in_specs=[SM, VM],
        out_specs=[SM] * 5,
        out_shape=[
            jax.ShapeDtypeStruct((1,), jnp.int32),
            jax.ShapeDtypeStruct((LISTED // GROUP,), jnp.int32),
            jax.ShapeDtypeStruct((LISTED,), jnp.int32),
            jax.ShapeDtypeStruct((LISTED,), jnp.int32),
            jax.ShapeDtypeStruct((1,), jnp.int32),
        ],
        scratch_shapes=[pltpu.VMEM((40, BS), jnp.int32), pltpu.SMEM((40, BS), jnp.int32)]
        + [pltpu.SMEM((72,), jnp.int32)] * 3
        + [pltpu.SemaphoreType.DMA],
        compiler_params=params(4),
        cost_estimate=lasting(9),
        name="plan",
    )(place, bricks)
    other_after, third, second, col_grid, total, *rest = lax.optimization_barrier(
        (other_after, third, second, col_grid, total, *crossings, *listed)
    )
    crossings, listed = rest[:4], rest[4:]

    low, high = ring_of_core_1(third[:CAP], -1), ring_of_core_1(other_after[CAP:], 1)
    crossings += [to_core(second), to_core(other_after), to_core(third)]
    col_grid_crossed = to_core(col_grid)
    frob = to_all(total, ("row", "col"), 128).reshape(128, BS)
    low, high, col_grid_crossed, frob, *crossings = lax.optimization_barrier(
        (low, high, col_grid_crossed, frob, *crossings)
    )

    halves = [low, to_core(high)]
    own_role = [after, before, far, step, second, other_after, third]
    overflow = most[0] > CAP

    def sparse():
        return pl.pallas_call(
            product_kernel,
            in_specs=[SM] * 7 + [VM] * 5 + [ANY] * 18,
            out_specs=[VM, VM],
            out_shape=[jax.ShapeDtypeStruct((512, 1024), BF16)] * 2,
            scratch_shapes=[
                pltpu.VMEM((8 * CAP + 1, BS, BS), BF16),
                pltpu.VMEM((16 * CAP, BS, BS), BF16),
                pltpu.VMEM((33, BS, BS), F32),
                pltpu.VMEM((8, BS, BS), BF16),
                pltpu.SemaphoreType.DMA((18,)),
            ],
            compiler_params=params(24),
            cost_estimate=lasting(12),
            name="product",
        )(place, pattern, shift, *listed, frob, core_matrix, row_grid, col_grid, col_grid_crossed, payload, crossed, *own_role, *crossings, *halves)

    def dense():
        keep = pattern.astype(F32)[:, None, :, None]
        numbers_row = row * 4 + jnp.arange(4)
        numbers_col = col * 8 + jnp.arange(8)
        on = (numbers_row[:, None] == numbers_col[None, :]).astype(F32)
        grid = row_grid.astype(F32) - shift[0] * jnp.eye(BS, dtype=F32)
        whole = core_matrix.astype(F32).reshape(4, BS, 8, BS) + on[:, None, :, None] * grid[:, :, None, :]
        whole = (whole * keep).reshape(512, 1024)
        scaled = (whole * lax.rsqrt(jnp.sum(frob) / ORDER + 1e-6)).astype(BF16)
        product = jnp.dot(
            lax.all_gather(scaled, "col", axis=1, tiled=True),
            lax.all_gather(scaled, "row", axis=0, tiled=True),
            preferred_element_type=F32,
        )
        square = (product.reshape(4, BS, 8, BS) * keep).reshape(512, 1024).astype(BF16)
        return scaled, square

    return tuple(lax.cond(overflow, lambda: tuple(dense()), lambda: tuple(sparse())))


def solution(mesh):
    in_specs = (P("row", "col"), P("row", "col"), P(), P("row", "col", None), P(), P(), P(), P())
    out_specs = (P("row", "col"), P("row", "col"))
    return jax.shard_map(body, mesh=mesh, in_specs=in_specs, out_specs=out_specs, check_vma=False)
```

```python
import functools

import jax
import jax.numpy as jnp
from jax import lax
from jax.experimental import pallas as pl
from jax.experimental.pallas import tpu as pltpu
from jax.sharding import PartitionSpec as P

BS = 128
CAP = 20
GROUP = 4
TURN = 4
ORDER = 8192
VOLUME = 0.015625
LISTED = 2048 + 32 * GROUP + TURN * GROUP
F32 = jnp.float32
BF16 = jnp.bfloat16


def params(mebibytes):
    return pltpu.CompilerParams(vmem_limit_bytes=mebibytes * 2**20)


def pack_kernel(pattern_ref, place_ref, core_ref, payload_ref, sum_ref):
    first_row = place_ref[0] * 4
    first_col = place_ref[1] * 8
    sum_ref[...] = jnp.zeros_like(sum_ref)

    def put(i, j, slot):
        payload_ref[pl.ds(pl.multiple_of(slot * BS, BS), BS), :] = core_ref[
            i * BS : (i + 1) * BS, j * BS : (j + 1) * BS
        ]

    slot = jnp.int32(0)
    for i in range(4):
        for j in range(8):
            kept = pattern_ref[i, j] != 0

            @pl.when(kept & (slot < CAP))
            def _():
                put(i, j, slot)

            @pl.when(kept & (first_row + i != first_col + j))
            def _():
                block = core_ref[i * BS : (i + 1) * BS, j * BS : (j + 1) * BS].astype(F32)
                squares = (block * block).reshape(16, 8, BS)
                sum_ref[...] += jnp.sum(squares, axis=0)

            slot += kept.astype(jnp.int32)
    for i in range(4):
        for j in range(8):
            dropped = pattern_ref[i, j] == 0

            @pl.when(dropped & (slot < CAP))
            def _():
                put(i, j, slot)

            slot += dropped.astype(jnp.int32)


def brick_kernel(pattern_ref, potential_ref, brick_ref):
    brick_ref[:64] = potential_ref[...].astype(BF16)
    rows = lax.broadcasted_iota(jnp.int32, (16, BS), 0)
    columns = lax.broadcasted_iota(jnp.int32, (16, BS), 1)
    note = jnp.zeros((16, BS), F32)
    for i in range(4):
        for j in range(8):
            note = jnp.where((rows == 0) & (columns == i * 8 + j), pattern_ref[i, j].astype(F32), note)
    brick_ref[64:] = note.astype(BF16)


def column(row_values):
    return jnp.broadcast_to(row_values, (BS, BS)).T


def values_kernel(place_ref, centres_ref, exponents_ref, extents_ref, phi_ref, along_ref, slots, sems):
    row, col = place_ref[0], place_ref[1]

    def copy(k):
        return pltpu.make_async_copy(slots.at[k % 2], phi_ref.at[k], sems.at[k % 2])

    def one(k, carry):
        @pl.when(k >= 2)
        def _():
            copy(k - 2).wait()

        cluster = jnp.where(k < 4, row * 4 + k, col * 8 + row % 2 * 4 + k - 4)
        decay = column(exponents_ref[pl.ds(cluster, 1), :])
        reach = column(extents_ref[pl.ds(cluster, 1), :].astype(F32))
        cut = jnp.exp(-decay * (reach * reach + 0.5))
        at_x = column(centres_ref[0, pl.ds(cluster, 1), :].astype(F32))
        at_y = column(centres_ref[1, pl.ds(cluster, 1), :].astype(F32))
        at_z = column(centres_ref[2, pl.ds(cluster, 1), :].astype(F32))
        off_z = lax.broadcasted_iota(jnp.int32, (BS, BS), 1).astype(F32) - at_z
        along_z = jnp.exp(-decay * (off_z * off_z))
        for y in range(8):
            off_y = y - at_y
            along_ref[y] = jnp.exp(-decay * (off_y * off_y))
        for x in range(8):
            off_x = x - at_x
            along_xz = along_z * jnp.exp(-decay * (off_x * off_x))
            for y in range(8):
                phi = along_xz * along_ref[y]
                slots[k % 2, x, :, y * BS : (y + 1) * BS] = jnp.where(phi >= cut, phi, 0.0).astype(BF16)
        copy(k).start()
        return carry

    lax.fori_loop(0, 8, one, 0)
    copy(6).wait()
    copy(7).wait()


def grid_kernel(with_sum, place_ref, home_ref, shift_ref, bricks_ref, phi_ref, *rest):
    if with_sum:
        core_ref, sum_ref, blocks_ref, total_ref, slots, sems = rest
    else:
        blocks_ref, slots, sems = rest
    row, col = place_ref[0], place_ref[1]
    first = row * 4 if with_sum else col * 8 + row % 2 * 4
    place = 0 if with_sum else 4

    def copy(k):
        return pltpu.make_async_copy(phi_ref.at[place + k], slots.at[k], sems.at[k])

    for k in range(4):
        copy(k).start()

    def one(k, carry):
        home = home_ref[first + k]
        index = (home // 8 ^ row) % 2 * 64 + home // 16 * 8 + home % 8
        copy(k).wait()
        total = jnp.zeros((BS, BS), F32)
        for x in range(8):
            values = jnp.concatenate([bricks_ref[index, x * 8 + y : x * 8 + y + 1, :] for y in range(8)], axis=1)
            phi = slots[k, x]
            total += lax.dot_general(phi * values, phi, (((1,), (1,)), ((), ())), preferred_element_type=F32)
        blocks_ref[k] = (total * VOLUME).astype(BF16)
        return carry

    lax.fori_loop(0, 4, one, 0)
    if with_sum:
        total_ref[...] = jnp.sum(sum_ref[...], axis=0, keepdims=True)

        @pl.when(col == row // 2)
        def _():
            eye = identity()
            for i in range(4):
                corner = pl.multiple_of((row % 2 * 4 + i) * BS, BS)
                block = core_ref[i * BS : (i + 1) * BS, pl.ds(corner, BS)].astype(F32)
                block = block + blocks_ref[i].astype(F32) - shift_ref[0] * eye
                total_ref[...] += jnp.sum(block * block, axis=0, keepdims=True)


def identity():
    rows = lax.broadcasted_iota(jnp.int32, (BS, BS), 0)
    columns = lax.broadcasted_iota(jnp.int32, (BS, BS), 1)
    return (rows == columns).astype(F32)


def plan_kernel(
    place_ref, bricks_ref, turns_ref, out_ref, left_ref, right_ref, most_ref, slots_ref, slots, kept_left, kept_right, kept_at, sem
):
    row, col = place_ref[0], place_ref[1]
    kept = jnp.sum(bricks_ref[:, 64:80, :].astype(F32), axis=1)
    kept = kept.T
    earlier = lax.broadcasted_iota(jnp.int32, (BS, BS), 1) < lax.broadcasted_iota(jnp.int32, (BS, BS), 0)
    before = jnp.dot(earlier.astype(BF16), kept.astype(BF16), preferred_element_type=F32)
    slots_ref[...] = jnp.where(kept > 0.5, before, -1.0)[:40].astype(jnp.int32)
    most_ref[0] = jnp.max(jnp.sum(kept, axis=0, keepdims=True)).astype(jnp.int32)
    copy = pltpu.make_async_copy(slots_ref, slots, sem)
    copy.start()
    copy.wait()

    def block_row(i, number):
        def piece(other, count):
            device = row // 2 * 8 + other
            base = ((other ^ col) % 2 * 4 + (other // 2 - col // 2) % 4) * CAP
            right = ((other // 4 ^ row // 8) * 4 + (other - row // 2) % 4) * 2 * CAP
            for j in range(8):
                slot = slots[i * 8 + j, device]
                kept_left[count] = base + slot
                kept_right[count] = right + j // 4 * CAP
                kept_at[count] = j % 4 * 8 * BS + (j // 4 ^ row) % 2 * 64 + other * 8 + col
                count += (slot >= 0).astype(jnp.int32)
            return count

        count = lax.fori_loop(0, 8, piece, jnp.int32(0))
        for more in range(3):
            kept_left[count + more] = 0
            kept_right[count + more] = 0
            kept_at[count + more] = 32 * BS

        def block(j, number):
            def listing(number):
                start = number // GROUP
                def four(n, number):
                    for inner in range(4):
                        at = kept_at[n * 4 + inner] + j * BS
                        slot = slots[at >> 7, at & 127]
                        left_ref[number] = kept_left[n * 4 + inner]
                        right_ref[number] = kept_right[n * 4 + inner] + slot
                        number += (slot >= 0).astype(jnp.int32)
                    return number

                number = lax.fori_loop(0, (count + 3) // 4, four, number)
                for more in range(GROUP - 1):
                    left_ref[number + more] = 8 * CAP
                    right_ref[number + more] = 0
                end = (number + GROUP - 1) // GROUP

                def name(group, carry):
                    out_ref[group] = i * 8 + j
                    return carry

                lax.fori_loop(start, end, name, 0)
                return end * GROUP

            wanted = slots[i * 8 + j, row // 2 * 8 + col] >= 0
            return lax.cond(wanted, listing, lambda n: n, number)

        return lax.fori_loop(0, 8, block, number)

    number = lax.fori_loop(0, 4, block_row, jnp.int32(0))
    groups = number // GROUP
    for more in range(TURN):
        out_ref[groups + more] = 32
        for inner in range(GROUP):
            left_ref[number + more * GROUP + inner] = 8 * CAP
            right_ref[number + more * GROUP + inner] = 0
    turns_ref[0] = (groups + TURN - 1) // TURN


def scaling(frob_ref):
    total = jnp.sum(frob_ref[...], axis=(0, 1), keepdims=True)
    return lax.rsqrt(total / ORDER + 1e-6)


def product_kernel(
    place_ref, pattern_ref, shift_ref, turns_ref, out_ref, left_ref, right_ref, frob_ref, core_ref, row_grid_ref, col_own_ref, col_other_ref,
    *rest
):
    payload, crossed, own_role, other_role, halves = rest[0], rest[1], rest[2:9], rest[9:16], rest[16:18]
    scaled_ref, square_ref, left_all, right_all, acc_ref, col_grid_ref, sems = rest[18:]
    core = place_ref[0] % 2

    def part(whole, at, size, source, number):
        return pltpu.make_async_copy(source, whole.at[pl.ds(at, size)], sems.at[number])

    copies = [
        part(left_all, 0, CAP, payload, 0),
        part(right_all, core * CAP, CAP, payload, 1),
        part(right_all, (1 - core) * CAP, CAP, crossed, 2),
    ]
    for copy in copies:
        copy.start()
    along_x = {1: 0, 2: 2, 3: 1, 4: 3, 5: 5, 6: 6, 7: 4}
    along_z = {1: 0, 2: 2, 3: 1, 4: 4, 5: 5, 7: 6}
    low, high = halves
    for k in range(1, 8):
        of_core_0 = [part(right_all, 2 * k * CAP, 2 * CAP, own_role[along_x[k]], 2 + 2 * k)]
        of_core_1 = [part(right_all, 2 * k * CAP, 2 * CAP, other_role[along_x[k]], 2 + 2 * k)]
        if k == 6:
            of_core_0.append(part(left_all, k * CAP, CAP, high, 1 + 2 * k))
            of_core_1.append(part(left_all, k * CAP, CAP, low, 1 + 2 * k))
        else:
            theirs, mine = other_role[along_z[k]], own_role[along_z[k]]
            of_core_0.append(part(left_all, k * CAP, CAP, theirs.at[pl.ds(CAP, CAP)], 1 + 2 * k))
            of_core_1.append(part(left_all, k * CAP, CAP, mine.at[pl.ds(0, CAP)], 1 + 2 * k))
        copies += of_core_0

        @pl.when(core == 0)
        def _():
            for copy in of_core_0:
                copy.start()

        @pl.when(core == 1)
        def _():
            for copy in of_core_1:
                copy.start()

    left_all[8 * CAP] = jnp.zeros((BS, BS), BF16)
    acc_ref[32] = jnp.zeros((BS, BS), F32)
    first_row = place_ref[0] * 4
    first_col = place_ref[1] * 8
    for n in range(4):
        col_grid_ref[core * 4 + n] = col_own_ref[n]
        col_grid_ref[(1 - core) * 4 + n] = col_other_ref[n]
    shift = shift_ref[0]
    scale = scaling(frob_ref)
    eye = identity()
    dot = functools.partial(jnp.dot, preferred_element_type=F32)
    for i in range(4):
        for j in range(8):
            block = (slice(i * BS, (i + 1) * BS), slice(j * BS, (j + 1) * BS))
            kept = pattern_ref[i, j] != 0
            diagonal = first_row + i == first_col + j

            @pl.when(kept)
            def _():
                here = core_ref[block]
                wide = here.astype(F32)
                acc_ref[i * 8 + j] = dot(row_grid_ref[i], here) + dot(here, col_grid_ref[j]) - 2.0 * shift * wide

                @pl.when(diagonal)
                def _():
                    grid = row_grid_ref[i]
                    grid_wide = grid.astype(F32)
                    acc_ref[i * 8 + j] += dot(grid, grid) - 2.0 * shift * grid_wide + shift * shift * eye
                    scaled_ref[block] = ((wide + grid_wide - shift * eye) * scale).astype(BF16)

                @pl.when(jnp.logical_not(diagonal))
                def _():
                    scaled_ref[block] = (wide * scale).astype(BF16)

            @pl.when(jnp.logical_not(kept))
            def _():
                scaled_ref[block] = jnp.zeros((BS, BS), BF16)
                square_ref[block] = jnp.zeros((BS, BS), BF16)

    for copy in copies:
        copy.wait()

    def turn(t, carry):
        sums = []
        for group in range(TURN):
            at = [(t * TURN + group) * GROUP + n for n in range(GROUP)]
            left = jnp.concatenate([left_all[left_ref[n]] for n in at], axis=1)
            right = jnp.concatenate([right_all[right_ref[n]] for n in at], axis=0)
            sums.append(dot(left, right))
        for group in range(TURN):
            acc_ref[out_ref[t * TURN + group]] += sums[group]
        return carry

    lax.fori_loop(0, turns_ref[0], turn, 0)
    for i in range(4):
        for j in range(8):
            block = (slice(i * BS, (i + 1) * BS), slice(j * BS, (j + 1) * BS))

            @pl.when(pattern_ref[i, j] != 0)
            def _():
                square_ref[block] = (acc_ref[i * 8 + j] * (scale * scale)).astype(BF16)


VM = pl.BlockSpec(memory_space=pltpu.VMEM)
SM = pl.BlockSpec(memory_space=pltpu.SMEM)
ANY = pl.BlockSpec(memory_space=pl.ANY)
HBM = pl.BlockSpec(memory_space=pltpu.HBM)


def to_all(value, axis, count, groups=None):
    copies = jnp.broadcast_to(value[None], (count,) + value.shape)
    return lax.all_to_all(copies, axis, 0, 0, axis_index_groups=groups)


def place_of(device):
    row, col = device // 8, device % 8
    return row // 2 % 4, col % 2 * 2 + row // 8, col // 2, row % 2


def device_of(x, y, z, core):
    return ((y % 2 * 4 + x % 4) * 2 + core) * 8 + z % 4 * 2 + y // 2


def move(value, where):
    return lax.ppermute(value, ("row", "col"), [(k, device_of(*where(*place_of(k)))) for k in range(128)])


def ring(value, off):
    return move(value, lambda x, y, z, core: (x, y, z - off, core) if core else (x - off, y, z, core))


def across_y(value):
    return move(value, lambda x, y, z, core: (x, 3 - y if core else y ^ 1, z, core))


def across_y_again(value):
    return move(value, lambda x, y, z, core: (x, y ^ 1, z, core) if core else (x + 1, y, z, core))


def from_core_1(value, off, core):
    pairs = []
    for k in range(128):
        x, y, z, source = place_of(k)
        if source == 1:
            pairs.append((k, device_of(x, y, z - off, core)))
    return lax.ppermute(value, ("row", "col"), pairs)


def to_core(value):
    return lax.ppermute(value, "row", [(k, k ^ 1) for k in range(16)])


def lasting(microseconds):
    return pl.CostEstimate(flops=int(microseconds * 1e9), bytes_accessed=2**20, transcendentals=0)


def body(core_matrix, pattern, shift, potential, home, centres, exponents, extents):
    row = lax.axis_index("row")
    col = lax.axis_index("col")
    place = jnp.stack([row, col]).astype(jnp.int32)

    brick = pl.pallas_call(
        brick_kernel,
        in_specs=[SM, VM],
        out_specs=VM,
        out_shape=jax.ShapeDtypeStruct((80, BS), BF16),
        compiler_params=params(4),
        cost_estimate=lasting(1),
        name="brick",
    )(pattern, potential.reshape(64, BS))
    same_core = [[row * 8 + col for row in range(core, 16, 2) for col in range(8)] for core in range(2)]
    half = to_all(brick, ("row", "col"), 64, same_core)

    (core_after_brick, _) = lax.optimization_barrier((core_matrix, brick))
    payload, squares = pl.pallas_call(
        pack_kernel,
        in_specs=[SM, SM, VM],
        out_specs=[VM, VM],
        out_shape=[jax.ShapeDtypeStruct((CAP * BS, BS), BF16), jax.ShapeDtypeStruct((8, BS), F32)],
        compiler_params=params(4),
        cost_estimate=lasting(2),
        name="pack",
    )(pattern, place, core_after_brick)
    payload = payload.reshape(CAP, BS, BS)
    crossed = to_core(payload)

    pair = jnp.concatenate([payload, crossed])
    step = across_y(pair)
    after, before = ring(pair, 1), ring(pair, -1)
    phi = pl.pallas_call(
        values_kernel,
        in_specs=[SM, VM, VM, VM],
        out_specs=HBM,
        out_shape=jax.ShapeDtypeStruct((8, 8, BS, 8 * BS), BF16),
        scratch_shapes=[
            pltpu.VMEM((8, BS, BS), F32),
            pltpu.VMEM((2, 8, BS, 8 * BS), BF16),
            pltpu.SemaphoreType.DMA((2,)),
        ],
        compiler_params=params(49),
        cost_estimate=lasting(10),
        name="values",
    )(place, centres, exponents, extents)

    half, phi, step, after, before = lax.optimization_barrier((half, phi, step, after, before))

    far = ring(after, 1)
    second = across_y_again(step)
    bricks = jnp.concatenate([half, to_core(half)])

    def grid_blocks(with_sum, *more):
        extra = [VM, VM] if with_sum else []
        out_shape = [jax.ShapeDtypeStruct((4, BS, BS), BF16)]
        if with_sum:
            out_shape.append(jax.ShapeDtypeStruct((1, BS), F32))
        return pl.pallas_call(
            functools.partial(grid_kernel, with_sum),
            in_specs=[SM, SM, SM, VM, HBM] + extra,
            out_specs=[VM] * len(out_shape),
            out_shape=out_shape,
            scratch_shapes=[pltpu.VMEM((4, 8, BS, 8 * BS), BF16), pltpu.SemaphoreType.DMA((4,))],
            compiler_params=params(49),
            cost_estimate=lasting(5),
            name="grid_rows" if with_sum else "grid_cols",
        )(place, home, shift, bricks, phi, *more)

    row_grid, total = grid_blocks(True, core_matrix, squares)
    crossings = [to_core(after), to_core(before)]
    frob = to_all(total, ("row", "col"), 128).reshape(128, BS)
    after, before, far, step, second, row_grid, frob, bricks, *crossings = lax.optimization_barrier(
        (after, before, far, step, second, row_grid, frob, bricks, *crossings)
    )

    third = ring(second, -1)
    other_after = ring(jnp.where(row % 2 == 0, step, second), 1)
    crossings += [to_core(far), to_core(step), to_core(second)]
    (col_grid,) = grid_blocks(False)
    *listed, most = pl.pallas_call(
        plan_kernel,
        in_specs=[SM, VM],
        out_specs=[SM] * 5,
        out_shape=[
            jax.ShapeDtypeStruct((1,), jnp.int32),
            jax.ShapeDtypeStruct((LISTED // GROUP,), jnp.int32),
            jax.ShapeDtypeStruct((LISTED,), jnp.int32),
            jax.ShapeDtypeStruct((LISTED,), jnp.int32),
            jax.ShapeDtypeStruct((1,), jnp.int32),
        ],
        scratch_shapes=[pltpu.VMEM((40, BS), jnp.int32), pltpu.SMEM((40, BS), jnp.int32)]
        + [pltpu.SMEM((72,), jnp.int32)] * 3
        + [pltpu.SemaphoreType.DMA],
        compiler_params=params(4),
        cost_estimate=lasting(9),
        name="plan",
    )(place, bricks)
    other_after, third, col_grid, *rest = lax.optimization_barrier(
        (other_after, third, col_grid, *crossings, *listed)
    )
    crossings, listed = rest[:5], rest[5:]

    low, high = from_core_1(third[:CAP], -1, 1), from_core_1(other_after[CAP:], 1, 0)
    crossings += [to_core(other_after), to_core(third)]
    col_grid_crossed = to_core(col_grid)
    low, high, col_grid_crossed, *crossings = lax.optimization_barrier((low, high, col_grid_crossed, *crossings))

    halves = [low, high]
    own_role = [after, before, far, step, second, other_after, third]
    overflow = most[0] > CAP

    def sparse():
        return pl.pallas_call(
            product_kernel,
            in_specs=[SM] * 7 + [VM] * 5 + [ANY] * 18,
            out_specs=[VM, VM],
            out_shape=[jax.ShapeDtypeStruct((512, 1024), BF16)] * 2,
            scratch_shapes=[
                pltpu.VMEM((8 * CAP + 1, BS, BS), BF16),
                pltpu.VMEM((16 * CAP, BS, BS), BF16),
                pltpu.VMEM((33, BS, BS), F32),
                pltpu.VMEM((8, BS, BS), BF16),
                pltpu.SemaphoreType.DMA((18,)),
            ],
            compiler_params=params(24),
            cost_estimate=lasting(12),
            name="product",
        )(place, pattern, shift, *listed, frob, core_matrix, row_grid, col_grid, col_grid_crossed, payload, crossed, *own_role, *crossings, *halves)

    def dense():
        keep = pattern.astype(F32)[:, None, :, None]
        numbers_row = row * 4 + jnp.arange(4)
        numbers_col = col * 8 + jnp.arange(8)
        on = (numbers_row[:, None] == numbers_col[None, :]).astype(F32)
        grid = row_grid.astype(F32) - shift[0] * jnp.eye(BS, dtype=F32)
        whole = core_matrix.astype(F32).reshape(4, BS, 8, BS) + on[:, None, :, None] * grid[:, :, None, :]
        whole = (whole * keep).reshape(512, 1024)
        scaled = (whole * lax.rsqrt(jnp.sum(frob) / ORDER + 1e-6)).astype(BF16)
        product = jnp.dot(
            lax.all_gather(scaled, "col", axis=1, tiled=True),
            lax.all_gather(scaled, "row", axis=0, tiled=True),
            preferred_element_type=F32,
        )
        square = (product.reshape(4, BS, 8, BS) * keep).reshape(512, 1024).astype(BF16)
        return scaled, square

    return tuple(lax.cond(overflow, lambda: tuple(dense()), lambda: tuple(sparse())))


def solution(mesh):
    in_specs = (P("row", "col"), P("row", "col"), P(), P("row", "col", None), P(), P(), P(), P())
    out_specs = (P("row", "col"), P("row", "col"))
    return jax.shard_map(body, mesh=mesh, in_specs=in_specs, out_specs=out_specs, check_vma=False)
```

```python
import functools

import jax
import jax.numpy as jnp
from jax import lax
from jax.experimental import pallas as pl
from jax.experimental.pallas import tpu as pltpu
from jax.sharding import PartitionSpec as P

BS = 128
CAP = 20
GROUP = 4
TURN = 4
ORDER = 8192
VOLUME = 0.015625
LISTED = 2048 + 32 * GROUP + TURN * GROUP
F32 = jnp.float32
BF16 = jnp.bfloat16


def params(mebibytes):
    return pltpu.CompilerParams(vmem_limit_bytes=mebibytes * 2**20)


def pack_kernel(pattern_ref, place_ref, core_ref, payload_ref, sum_ref):
    first_row = place_ref[0] * 4
    first_col = place_ref[1] * 8
    sum_ref[...] = jnp.zeros_like(sum_ref)

    def put(i, j, slot):
        payload_ref[pl.ds(pl.multiple_of(slot * BS, BS), BS), :] = core_ref[
            i * BS : (i + 1) * BS, j * BS : (j + 1) * BS
        ]

    slot = jnp.int32(0)
    for i in range(4):
        for j in range(8):
            kept = pattern_ref[i, j] != 0

            @pl.when(kept & (slot < CAP))
            def _():
                put(i, j, slot)

            @pl.when(kept & (first_row + i != first_col + j))
            def _():
                block = core_ref[i * BS : (i + 1) * BS, j * BS : (j + 1) * BS].astype(F32)
                squares = (block * block).reshape(16, 8, BS)
                sum_ref[...] += jnp.sum(squares, axis=0)

            slot += kept.astype(jnp.int32)
    for i in range(4):
        for j in range(8):
            dropped = pattern_ref[i, j] == 0

            @pl.when(dropped & (slot < CAP))
            def _():
                put(i, j, slot)

            slot += dropped.astype(jnp.int32)


def brick_kernel(pattern_ref, potential_ref, brick_ref):
    brick_ref[:64] = potential_ref[...].astype(BF16)
    rows = lax.broadcasted_iota(jnp.int32, (16, BS), 0)
    columns = lax.broadcasted_iota(jnp.int32, (16, BS), 1)
    note = jnp.zeros((16, BS), F32)
    for i in range(4):
        for j in range(8):
            note = jnp.where((rows == 0) & (columns == i * 8 + j), pattern_ref[i, j].astype(F32), note)
    brick_ref[64:] = note.astype(BF16)


def column(row_values):
    return jnp.broadcast_to(row_values, (BS, BS)).T


def values_kernel(place_ref, centres_ref, exponents_ref, extents_ref, phi_ref, along_ref, slots, sems):
    row, col = place_ref[0], place_ref[1]

    def copy(k):
        return pltpu.make_async_copy(slots.at[k % 2], phi_ref.at[k], sems.at[k % 2])

    def one(k, carry):
        @pl.when(k >= 2)
        def _():
            copy(k - 2).wait()

        cluster = jnp.where(k < 4, row * 4 + k, col * 8 + row % 2 * 4 + k - 4)
        decay = column(exponents_ref[pl.ds(cluster, 1), :])
        reach = column(extents_ref[pl.ds(cluster, 1), :].astype(F32))
        cut = jnp.exp(-decay * (reach * reach + 0.5))
        at_x = column(centres_ref[0, pl.ds(cluster, 1), :].astype(F32))
        at_y = column(centres_ref[1, pl.ds(cluster, 1), :].astype(F32))
        at_z = column(centres_ref[2, pl.ds(cluster, 1), :].astype(F32))
        off_z = lax.broadcasted_iota(jnp.int32, (BS, BS), 1).astype(F32) - at_z
        along_z = jnp.exp(-decay * (off_z * off_z))
        for y in range(8):
            off_y = y - at_y
            along_ref[y] = jnp.exp(-decay * (off_y * off_y))
        for x in range(8):
            off_x = x - at_x
            along_xz = along_z * jnp.exp(-decay * (off_x * off_x))
            for y in range(8):
                phi = along_xz * along_ref[y]
                slots[k % 2, x, :, y * BS : (y + 1) * BS] = jnp.where(phi >= cut, phi, 0.0).astype(BF16)
        copy(k).start()
        return carry

    lax.fori_loop(0, 8, one, 0)
    copy(6).wait()
    copy(7).wait()


def grid_kernel(with_sum, place_ref, home_ref, shift_ref, bricks_ref, phi_ref, *rest):
    if with_sum:
        core_ref, sum_ref, blocks_ref, total_ref, slots, sems = rest
    else:
        blocks_ref, slots, sems = rest
    row, col = place_ref[0], place_ref[1]
    first = row * 4 if with_sum else col * 8 + row % 2 * 4
    place = 0 if with_sum else 4

    def copy(k):
        return pltpu.make_async_copy(phi_ref.at[place + k], slots.at[k], sems.at[k])

    for k in range(4):
        copy(k).start()

    def one(k, carry):
        home = home_ref[first + k]
        index = (home // 8 ^ row) % 2 * 64 + home // 16 * 8 + home % 8
        copy(k).wait()
        total = jnp.zeros((BS, BS), F32)
        for x in range(8):
            values = jnp.concatenate([bricks_ref[index, x * 8 + y : x * 8 + y + 1, :] for y in range(8)], axis=1)
            phi = slots[k, x]
            total += lax.dot_general(phi * values, phi, (((1,), (1,)), ((), ())), preferred_element_type=F32)
        blocks_ref[k] = (total * VOLUME).astype(BF16)
        return carry

    lax.fori_loop(0, 4, one, 0)
    if with_sum:
        total_ref[...] = jnp.sum(sum_ref[...], axis=0, keepdims=True)

        @pl.when(col == row // 2)
        def _():
            eye = identity()
            for i in range(4):
                corner = pl.multiple_of((row % 2 * 4 + i) * BS, BS)
                block = core_ref[i * BS : (i + 1) * BS, pl.ds(corner, BS)].astype(F32)
                block = block + blocks_ref[i].astype(F32) - shift_ref[0] * eye
                total_ref[...] += jnp.sum(block * block, axis=0, keepdims=True)


def identity():
    rows = lax.broadcasted_iota(jnp.int32, (BS, BS), 0)
    columns = lax.broadcasted_iota(jnp.int32, (BS, BS), 1)
    return (rows == columns).astype(F32)


def plan_kernel(
    place_ref, bricks_ref, turns_ref, out_ref, left_ref, right_ref, most_ref, slots_ref, slots, kept_left, kept_right, kept_at, sem
):
    row, col = place_ref[0], place_ref[1]
    kept = jnp.sum(bricks_ref[:, 64:80, :].astype(F32), axis=1)
    kept = kept.T
    earlier = lax.broadcasted_iota(jnp.int32, (BS, BS), 1) < lax.broadcasted_iota(jnp.int32, (BS, BS), 0)
    before = jnp.dot(earlier.astype(BF16), kept.astype(BF16), preferred_element_type=F32)
    slots_ref[...] = jnp.where(kept > 0.5, before, -1.0)[:40].astype(jnp.int32)
    most_ref[0] = jnp.max(jnp.sum(kept, axis=0, keepdims=True)).astype(jnp.int32)
    copy = pltpu.make_async_copy(slots_ref, slots, sem)
    copy.start()
    copy.wait()

    def block_row(i, number):
        def piece(other, count):
            device = row // 2 * 8 + other
            base = ((other ^ col) % 2 * 4 + (other // 2 - col // 2) % 4) * CAP
            right = ((other // 4 ^ row // 8) * 4 + (other - row // 2) % 4) * 2 * CAP
            for j in range(8):
                slot = slots[i * 8 + j, device]
                kept_left[count] = base + slot
                kept_right[count] = right + j // 4 * CAP
                kept_at[count] = j % 4 * 8 * BS + (j // 4 ^ row) % 2 * 64 + other * 8 + col
                count += (slot >= 0).astype(jnp.int32)
            return count

        count = lax.fori_loop(0, 8, piece, jnp.int32(0))
        for more in range(3):
            kept_left[count + more] = 0
            kept_right[count + more] = 0
            kept_at[count + more] = 32 * BS

        def block(j, number):
            def listing(number):
                start = number // GROUP
                def four(n, number):
                    for inner in range(4):
                        at = kept_at[n * 4 + inner] + j * BS
                        slot = slots[at >> 7, at & 127]
                        left_ref[number] = kept_left[n * 4 + inner]
                        right_ref[number] = kept_right[n * 4 + inner] + slot
                        number += (slot >= 0).astype(jnp.int32)
                    return number

                number = lax.fori_loop(0, (count + 3) // 4, four, number)
                for more in range(GROUP - 1):
                    left_ref[number + more] = 8 * CAP
                    right_ref[number + more] = 0
                end = (number + GROUP - 1) // GROUP

                def name(group, carry):
                    out_ref[group] = i * 8 + j
                    return carry

                lax.fori_loop(start, end, name, 0)
                return end * GROUP

            wanted = slots[i * 8 + j, row // 2 * 8 + col] >= 0
            return lax.cond(wanted, listing, lambda n: n, number)

        return lax.fori_loop(0, 8, block, number)

    number = lax.fori_loop(0, 4, block_row, jnp.int32(0))
    groups = number // GROUP
    for more in range(TURN):
        out_ref[groups + more] = 32
        for inner in range(GROUP):
            left_ref[number + more * GROUP + inner] = 8 * CAP
            right_ref[number + more * GROUP + inner] = 0
    turns_ref[0] = (groups + TURN - 1) // TURN


def scaling(frob_ref):
    total = jnp.sum(frob_ref[...], axis=(0, 1), keepdims=True)
    return lax.rsqrt(total / ORDER + 1e-6)


def prepare_kernel(
    place_ref, pattern_ref, shift_ref, frob_ref, core_ref, row_grid_ref, col_own_ref, col_other_ref, scaled_ref,
    linear_ref, col_grid_ref
):
    first_row = place_ref[0] * 4
    first_col = place_ref[1] * 8
    core = place_ref[0] % 2
    for n in range(4):
        col_grid_ref[core * 4 + n] = col_own_ref[n]
        col_grid_ref[(1 - core) * 4 + n] = col_other_ref[n]
    shift = shift_ref[0]
    scale = scaling(frob_ref)
    eye = identity()
    dot = functools.partial(jnp.dot, preferred_element_type=F32)
    for i in range(4):
        for j in range(8):
            block = (slice(i * BS, (i + 1) * BS), slice(j * BS, (j + 1) * BS))
            kept = pattern_ref[i, j] != 0
            diagonal = first_row + i == first_col + j

            @pl.when(kept)
            def _():
                here = core_ref[block]
                wide = here.astype(F32)
                linear_ref[i * 8 + j] = dot(row_grid_ref[i], here) + dot(here, col_grid_ref[j]) - 2.0 * shift * wide

                @pl.when(diagonal)
                def _():
                    grid = row_grid_ref[i]
                    grid_wide = grid.astype(F32)
                    linear_ref[i * 8 + j] += dot(grid, grid) - 2.0 * shift * grid_wide + shift * shift * eye
                    scaled_ref[block] = ((wide + grid_wide - shift * eye) * scale).astype(BF16)

                @pl.when(jnp.logical_not(diagonal))
                def _():
                    scaled_ref[block] = (wide * scale).astype(BF16)

            @pl.when(jnp.logical_not(kept))
            def _():
                scaled_ref[block] = jnp.zeros((BS, BS), BF16)


def product_kernel(
    place_ref, pattern_ref, turns_ref, out_ref, left_ref, right_ref, frob_ref, linear_ref, *rest
):
    payload, crossed, own_role, other_role, halves = rest[0], rest[1], rest[2:9], rest[9:16], rest[16:18]
    square_ref, left_all, right_all, acc_ref, sems = rest[18:]
    core = place_ref[0] % 2

    def part(whole, at, size, source, number):
        return pltpu.make_async_copy(source, whole.at[pl.ds(at, size)], sems.at[number])

    copies = [
        part(left_all, 0, CAP, payload, 0),
        part(right_all, core * CAP, CAP, payload, 1),
        part(right_all, (1 - core) * CAP, CAP, crossed, 2),
    ]
    for copy in copies:
        copy.start()
    along_x = {1: 0, 2: 2, 3: 1, 4: 3, 5: 5, 6: 6, 7: 4}
    along_z = {1: 0, 2: 2, 3: 1, 4: 4, 5: 5, 7: 6}
    low, high = halves
    for k in range(1, 8):
        of_core_0 = [part(right_all, 2 * k * CAP, 2 * CAP, own_role[along_x[k]], 2 + 2 * k)]
        of_core_1 = [part(right_all, 2 * k * CAP, 2 * CAP, other_role[along_x[k]], 2 + 2 * k)]
        if k == 6:
            of_core_0.append(part(left_all, k * CAP, CAP, high, 1 + 2 * k))
            of_core_1.append(part(left_all, k * CAP, CAP, low, 1 + 2 * k))
        else:
            theirs, mine = other_role[along_z[k]], own_role[along_z[k]]
            of_core_0.append(part(left_all, k * CAP, CAP, theirs.at[pl.ds(CAP, CAP)], 1 + 2 * k))
            of_core_1.append(part(left_all, k * CAP, CAP, mine.at[pl.ds(0, CAP)], 1 + 2 * k))
        copies += of_core_0

        @pl.when(core == 0)
        def _():
            for copy in of_core_0:
                copy.start()

        @pl.when(core == 1)
        def _():
            for copy in of_core_1:
                copy.start()

    left_all[8 * CAP] = jnp.zeros((BS, BS), BF16)
    acc_ref[...] = jnp.zeros_like(acc_ref)
    scale = scaling(frob_ref)
    dot = functools.partial(jnp.dot, preferred_element_type=F32)
    for i in range(4):
        for j in range(8):

            @pl.when(pattern_ref[i, j] == 0)
            def _():
                square_ref[i * BS : (i + 1) * BS, j * BS : (j + 1) * BS] = jnp.zeros((BS, BS), BF16)

    for copy in copies:
        copy.wait()

    def turn(t, carry):
        sums = []
        for group in range(TURN):
            at = [(t * TURN + group) * GROUP + n for n in range(GROUP)]
            left = jnp.concatenate([left_all[left_ref[n]] for n in at], axis=1)
            right = jnp.concatenate([right_all[right_ref[n]] for n in at], axis=0)
            sums.append(dot(left, right))
        for group in range(TURN):
            acc_ref[out_ref[t * TURN + group]] += sums[group]
        return carry

    lax.fori_loop(0, turns_ref[0], turn, 0)
    for i in range(4):
        for j in range(8):
            block = (slice(i * BS, (i + 1) * BS), slice(j * BS, (j + 1) * BS))

            @pl.when(pattern_ref[i, j] != 0)
            def _():
                square_ref[block] = ((acc_ref[i * 8 + j] + linear_ref[i * 8 + j]) * (scale * scale)).astype(BF16)


VM = pl.BlockSpec(memory_space=pltpu.VMEM)
SM = pl.BlockSpec(memory_space=pltpu.SMEM)
ANY = pl.BlockSpec(memory_space=pl.ANY)
HBM = pl.BlockSpec(memory_space=pltpu.HBM)


def to_all(value, axis, count, groups=None):
    copies = jnp.broadcast_to(value[None], (count,) + value.shape)
    return lax.all_to_all(copies, axis, 0, 0, axis_index_groups=groups)


def place_of(device):
    row, col = device // 8, device % 8
    return row // 2 % 4, col % 2 * 2 + row // 8, col // 2, row % 2


def device_of(x, y, z, core):
    return ((y % 2 * 4 + x % 4) * 2 + core) * 8 + z % 4 * 2 + y // 2


def move(value, where):
    return lax.ppermute(value, ("row", "col"), [(k, device_of(*where(*place_of(k)))) for k in range(128)])


def ring(value, off):
    return move(value, lambda x, y, z, core: (x, y, z - off, core) if core else (x - off, y, z, core))


def across_y(value):
    return move(value, lambda x, y, z, core: (x, 3 - y if core else y ^ 1, z, core))


def across_y_again(value):
    return move(value, lambda x, y, z, core: (x, y ^ 1, z, core) if core else (x + 1, y, z, core))


def from_core_1(value, off, core):
    pairs = []
    for k in range(128):
        x, y, z, source = place_of(k)
        if source == 1:
            pairs.append((k, device_of(x, y, z - off, core)))
    return lax.ppermute(value, ("row", "col"), pairs)


def to_core(value):
    return lax.ppermute(value, "row", [(k, k ^ 1) for k in range(16)])


def lasting(microseconds):
    return pl.CostEstimate(flops=int(microseconds * 1e9), bytes_accessed=2**20, transcendentals=0)


def body(core_matrix, pattern, shift, potential, home, centres, exponents, extents):
    row = lax.axis_index("row")
    col = lax.axis_index("col")
    place = jnp.stack([row, col]).astype(jnp.int32)

    brick = pl.pallas_call(
        brick_kernel,
        in_specs=[SM, VM],
        out_specs=VM,
        out_shape=jax.ShapeDtypeStruct((80, BS), BF16),
        compiler_params=params(4),
        cost_estimate=lasting(1),
        name="brick",
    )(pattern, potential.reshape(64, BS))
    same_core = [[row * 8 + col for row in range(core, 16, 2) for col in range(8)] for core in range(2)]
    half = to_all(brick, ("row", "col"), 64, same_core)

    (core_after_brick, _) = lax.optimization_barrier((core_matrix, brick))
    payload, squares = pl.pallas_call(
        pack_kernel,
        in_specs=[SM, SM, VM],
        out_specs=[VM, VM],
        out_shape=[jax.ShapeDtypeStruct((CAP * BS, BS), BF16), jax.ShapeDtypeStruct((8, BS), F32)],
        compiler_params=params(4),
        cost_estimate=lasting(2),
        name="pack",
    )(pattern, place, core_after_brick)
    payload = payload.reshape(CAP, BS, BS)
    crossed = to_core(payload)

    pair = jnp.concatenate([payload, crossed])
    step = across_y(pair)
    after, before = ring(pair, 1), ring(pair, -1)
    phi = pl.pallas_call(
        values_kernel,
        in_specs=[SM, VM, VM, VM],
        out_specs=HBM,
        out_shape=jax.ShapeDtypeStruct((8, 8, BS, 8 * BS), BF16),
        scratch_shapes=[
            pltpu.VMEM((8, BS, BS), F32),
            pltpu.VMEM((2, 8, BS, 8 * BS), BF16),
            pltpu.SemaphoreType.DMA((2,)),
        ],
        compiler_params=params(49),
        cost_estimate=lasting(10),
        name="values",
    )(place, centres, exponents, extents)

    half, phi, step, after, before = lax.optimization_barrier((half, phi, step, after, before))

    far = ring(after, 1)
    second = across_y_again(step)
    bricks = jnp.concatenate([half, to_core(half)])

    def grid_blocks(with_sum, *more):
        extra = [VM, VM] if with_sum else []
        out_shape = [jax.ShapeDtypeStruct((4, BS, BS), BF16)]
        if with_sum:
            out_shape.append(jax.ShapeDtypeStruct((1, BS), F32))
        return pl.pallas_call(
            functools.partial(grid_kernel, with_sum),
            in_specs=[SM, SM, SM, VM, HBM] + extra,
            out_specs=[VM] * len(out_shape),
            out_shape=out_shape,
            scratch_shapes=[pltpu.VMEM((4, 8, BS, 8 * BS), BF16), pltpu.SemaphoreType.DMA((4,))],
            compiler_params=params(49),
            cost_estimate=lasting(5),
            name="grid_rows" if with_sum else "grid_cols",
        )(place, home, shift, bricks, phi, *more)

    row_grid, total = grid_blocks(True, core_matrix, squares)
    crossings = [to_core(after), to_core(before)]
    frob = to_all(total, ("row", "col"), 128).reshape(128, BS)
    (col_grid,) = grid_blocks(False)
    after, before, far, step, second, row_grid, col_grid, frob, bricks, *crossings = lax.optimization_barrier(
        (after, before, far, step, second, row_grid, col_grid, frob, bricks, *crossings)
    )

    third = ring(second, -1)
    other_after = ring(jnp.where(row % 2 == 0, step, second), 1)
    crossings += [to_core(far), to_core(step)]
    col_grid_crossed = to_core(col_grid)
    *listed, most = pl.pallas_call(
        plan_kernel,
        in_specs=[SM, VM],
        out_specs=[SM] * 5,
        out_shape=[
            jax.ShapeDtypeStruct((1,), jnp.int32),
            jax.ShapeDtypeStruct((LISTED // GROUP,), jnp.int32),
            jax.ShapeDtypeStruct((LISTED,), jnp.int32),
            jax.ShapeDtypeStruct((LISTED,), jnp.int32),
            jax.ShapeDtypeStruct((1,), jnp.int32),
        ],
        scratch_shapes=[pltpu.VMEM((40, BS), jnp.int32), pltpu.SMEM((40, BS), jnp.int32)]
        + [pltpu.SMEM((72,), jnp.int32)] * 3
        + [pltpu.SemaphoreType.DMA],
        compiler_params=params(4),
        cost_estimate=lasting(9),
        name="plan",
    )(place, bricks)
    other_after, third, second, col_grid_crossed, *rest = lax.optimization_barrier(
        (other_after, third, second, col_grid_crossed, *crossings, *listed)
    )
    crossings, listed = rest[:4], rest[4:]

    low, high = from_core_1(third[:CAP], -1, 1), from_core_1(other_after[CAP:], 1, 0)
    crossings += [to_core(second), to_core(other_after), to_core(third)]
    scaled, linear = pl.pallas_call(
        prepare_kernel,
        in_specs=[SM] * 3 + [VM] * 5,
        out_specs=[VM, VM],
        out_shape=[jax.ShapeDtypeStruct((512, 1024), BF16), jax.ShapeDtypeStruct((32, BS, BS), F32)],
        scratch_shapes=[pltpu.VMEM((8, BS, BS), BF16)],
        compiler_params=params(4),
        cost_estimate=lasting(4),
        name="prepare",
    )(place, pattern, shift, frob, core_matrix, row_grid, col_grid, col_grid_crossed)
    low, high, scaled, linear, *crossings = lax.optimization_barrier((low, high, scaled, linear, *crossings))

    halves = [low, high]
    own_role = [after, before, far, step, second, other_after, third]
    overflow = most[0] > CAP

    def sparse():
        return pl.pallas_call(
            product_kernel,
            in_specs=[SM] * 6 + [VM] * 2 + [ANY] * 18,
            out_specs=VM,
            out_shape=jax.ShapeDtypeStruct((512, 1024), BF16),
            scratch_shapes=[
                pltpu.VMEM((8 * CAP + 1, BS, BS), BF16),
                pltpu.VMEM((16 * CAP, BS, BS), BF16),
                pltpu.VMEM((33, BS, BS), F32),
                pltpu.SemaphoreType.DMA((18,)),
            ],
            compiler_params=params(24),
            cost_estimate=lasting(12),
            name="product",
        )(place, pattern, *listed, frob, linear, payload, crossed, *own_role, *crossings, *halves)

    def dense():
        keep = pattern.astype(F32)[:, None, :, None]
        product = jnp.dot(
            lax.all_gather(scaled, "col", axis=1, tiled=True),
            lax.all_gather(scaled, "row", axis=0, tiled=True),
            preferred_element_type=F32,
        )
        return (product.reshape(4, BS, 8, BS) * keep).reshape(512, 1024).astype(BF16)

    return scaled, lax.cond(overflow, dense, sparse)


def solution(mesh):
    in_specs = (P("row", "col"), P("row", "col"), P(), P("row", "col", None), P(), P(), P(), P())
    out_specs = (P("row", "col"), P("row", "col"))
    return jax.shard_map(body, mesh=mesh, in_specs=in_specs, out_specs=out_specs, check_vma=False)
```

```python
import functools

import jax
import jax.numpy as jnp
from jax import lax
from jax.experimental import pallas as pl
from jax.experimental.pallas import tpu as pltpu
from jax.sharding import PartitionSpec as P

BS = 128
CAP = 20
GROUP = 4
TURN = 4
ORDER = 8192
VOLUME = 0.015625
SUM_LANE = 64
LISTED = 2048 + 32 * GROUP + TURN * GROUP
F32 = jnp.float32
BF16 = jnp.bfloat16


def params(mebibytes):
    return pltpu.CompilerParams(vmem_limit_bytes=mebibytes * 2**20)


def pack_kernel(pattern_ref, place_ref, core_ref, payload_ref, sum_ref):
    first_row = place_ref[0] * 4
    first_col = place_ref[1] * 8
    sum_ref[...] = jnp.zeros_like(sum_ref)

    def put(i, j, slot):
        payload_ref[pl.ds(pl.multiple_of(slot * BS, BS), BS), :] = core_ref[
            i * BS : (i + 1) * BS, j * BS : (j + 1) * BS
        ]

    slot = jnp.int32(0)
    for i in range(4):
        for j in range(8):
            kept = pattern_ref[i, j] != 0

            @pl.when(kept & (slot < CAP))
            def _():
                put(i, j, slot)

            @pl.when(kept & (first_row + i != first_col + j))
            def _():
                block = core_ref[i * BS : (i + 1) * BS, j * BS : (j + 1) * BS].astype(F32)
                squares = (block * block).reshape(16, 8, BS)
                sum_ref[...] += jnp.sum(squares, axis=0)

            slot += kept.astype(jnp.int32)
    for i in range(4):
        for j in range(8):
            dropped = pattern_ref[i, j] == 0

            @pl.when(dropped & (slot < CAP))
            def _():
                put(i, j, slot)

            slot += dropped.astype(jnp.int32)


def brick_kernel(potential_ref, brick_ref):
    brick_ref[...] = potential_ref[...].astype(BF16)


def column(row_values):
    return jnp.broadcast_to(row_values, (BS, BS)).T


def values_kernel(place_ref, centres_ref, exponents_ref, extents_ref, phi_ref, along_ref, slots, sems):
    row, col = place_ref[0], place_ref[1]

    def copy(k):
        return pltpu.make_async_copy(slots.at[k % 2], phi_ref.at[k], sems.at[k % 2])

    def one(k, carry):
        @pl.when(k >= 2)
        def _():
            copy(k - 2).wait()

        cluster = jnp.where(k < 4, row * 4 + k, col * 8 + row % 2 * 4 + k - 4)
        decay = column(exponents_ref[pl.ds(cluster, 1), :])
        reach = column(extents_ref[pl.ds(cluster, 1), :].astype(F32))
        cut = jnp.exp(-decay * (reach * reach + 0.5))
        at_x = column(centres_ref[0, pl.ds(cluster, 1), :].astype(F32))
        at_y = column(centres_ref[1, pl.ds(cluster, 1), :].astype(F32))
        at_z = column(centres_ref[2, pl.ds(cluster, 1), :].astype(F32))
        off_z = lax.broadcasted_iota(jnp.int32, (BS, BS), 1).astype(F32) - at_z
        along_z = jnp.exp(-decay * (off_z * off_z))
        for y in range(8):
            off_y = y - at_y
            along_ref[y] = jnp.exp(-decay * (off_y * off_y))
        for x in range(8):
            off_x = x - at_x
            along_xz = along_z * jnp.exp(-decay * (off_x * off_x))
            for y in range(8):
                phi = along_xz * along_ref[y]
                slots[k % 2, x, :, y * BS : (y + 1) * BS] = jnp.where(phi >= cut, phi, 0.0).astype(BF16)
        copy(k).start()
        return carry

    lax.fori_loop(0, 8, one, 0)
    copy(6).wait()
    copy(7).wait()


def grid_kernel(with_sum, place_ref, home_ref, shift_ref, bricks_ref, phi_ref, *rest):
    if with_sum:
        core_ref, sum_ref, pattern_ref, blocks_ref, total_ref, slots, sems = rest
    else:
        blocks_ref, slots, sems = rest
    row, col = place_ref[0], place_ref[1]
    first = row * 4 if with_sum else col * 8 + row % 2 * 4
    place = 0 if with_sum else 4

    def copy(k):
        return pltpu.make_async_copy(phi_ref.at[place + k], slots.at[k], sems.at[k])

    for k in range(4):
        copy(k).start()

    def one(k, carry):
        home = home_ref[first + k]
        index = (home // 8 ^ row) % 2 * 64 + home // 16 * 8 + home % 8
        copy(k).wait()
        total = jnp.zeros((BS, BS), F32)
        for x in range(8):
            values = jnp.concatenate([bricks_ref[index, x * 8 + y : x * 8 + y + 1, :] for y in range(8)], axis=1)
            phi = slots[k, x]
            total += lax.dot_general(phi * values, phi, (((1,), (1,)), ((), ())), preferred_element_type=F32)
        blocks_ref[k] = (total * VOLUME).astype(BF16)
        return carry

    lax.fori_loop(0, 4, one, 0)
    if with_sum:
        total_ref[...] = jnp.sum(sum_ref[...], axis=0, keepdims=True)

        @pl.when(col == row // 2)
        def _():
            eye = identity()
            for i in range(4):
                corner = pl.multiple_of((row % 2 * 4 + i) * BS, BS)
                block = core_ref[i * BS : (i + 1) * BS, pl.ds(corner, BS)].astype(F32)
                block = block + blocks_ref[i].astype(F32) - shift_ref[0] * eye
                total_ref[...] += jnp.sum(block * block, axis=0, keepdims=True)

        lanes = lax.broadcasted_iota(jnp.int32, (1, BS), 1)
        note = jnp.where(lanes == SUM_LANE, jnp.sum(total_ref[...], axis=1, keepdims=True), 0.0)
        for i in range(4):
            for j in range(8):
                note = jnp.where(lanes == i * 8 + j, pattern_ref[i, j].astype(F32), note)
        total_ref[...] = note


def identity():
    rows = lax.broadcasted_iota(jnp.int32, (BS, BS), 0)
    columns = lax.broadcasted_iota(jnp.int32, (BS, BS), 1)
    return (rows == columns).astype(F32)


def plan_kernel(
    place_ref, notes_ref, turns_ref, out_ref, left_ref, right_ref, most_ref, slots_ref, slots, kept_left, kept_right, kept_at, sem
):
    row, col = place_ref[0], place_ref[1]
    lanes = lax.broadcasted_iota(jnp.int32, (BS, BS), 1)
    kept = jnp.where(lanes < 32, notes_ref[...], 0.0).T
    earlier = lax.broadcasted_iota(jnp.int32, (BS, BS), 1) < lax.broadcasted_iota(jnp.int32, (BS, BS), 0)
    before = jnp.dot(earlier.astype(BF16), kept.astype(BF16), preferred_element_type=F32)
    slots_ref[...] = jnp.where(kept > 0.5, before, -1.0)[:40].astype(jnp.int32)
    most_ref[0] = jnp.max(jnp.sum(kept, axis=0, keepdims=True)).astype(jnp.int32)
    copy = pltpu.make_async_copy(slots_ref, slots, sem)
    copy.start()
    copy.wait()

    def block_row(i, number):
        def piece(other, count):
            device = row * 8 + other
            base = ((other ^ col) % 2 * 4 + (other // 2 - col // 2) % 4) * CAP
            right = ((other // 4 ^ row // 8) * 4 + (other - row // 2) % 4) * 2 * CAP
            for j in range(8):
                slot = slots[i * 8 + j, device]
                kept_left[count] = base + slot
                kept_right[count] = right + j // 4 * CAP
                kept_at[count] = j % 4 * 8 * BS + (other * 2 + j // 4) * 8 + col
                count += (slot >= 0).astype(jnp.int32)
            return count

        count = lax.fori_loop(0, 8, piece, jnp.int32(0))
        for more in range(3):
            kept_left[count + more] = 0
            kept_right[count + more] = 0
            kept_at[count + more] = 32 * BS

        def block(j, number):
            def listing(number):
                start = number // GROUP
                def four(n, number):
                    for inner in range(4):
                        at = kept_at[n * 4 + inner] + j * BS
                        slot = slots[at >> 7, at & 127]
                        left_ref[number] = kept_left[n * 4 + inner]
                        right_ref[number] = kept_right[n * 4 + inner] + slot
                        number += (slot >= 0).astype(jnp.int32)
                    return number

                number = lax.fori_loop(0, (count + 3) // 4, four, number)
                for more in range(GROUP - 1):
                    left_ref[number + more] = 8 * CAP
                    right_ref[number + more] = 0
                end = (number + GROUP - 1) // GROUP

                def name(group, carry):
                    out_ref[group] = i * 8 + j
                    return carry

                lax.fori_loop(start, end, name, 0)
                return end * GROUP

            wanted = slots[i * 8 + j, row * 8 + col] >= 0
            return lax.cond(wanted, listing, lambda n: n, number)

        return lax.fori_loop(0, 8, block, number)

    number = lax.fori_loop(0, 4, block_row, jnp.int32(0))
    groups = number // GROUP
    for more in range(TURN):
        out_ref[groups + more] = 32
        for inner in range(GROUP):
            left_ref[number + more * GROUP + inner] = 8 * CAP
            right_ref[number + more * GROUP + inner] = 0
    turns_ref[0] = (groups + TURN - 1) // TURN


def scaling(frob_ref):
    lanes = lax.broadcasted_iota(jnp.int32, (BS, BS), 1)
    total = jnp.sum(jnp.where(lanes == SUM_LANE, frob_ref[...], 0.0), axis=(0, 1), keepdims=True)
    return lax.rsqrt(total / ORDER + 1e-6)


def prepare_kernel(
    place_ref, pattern_ref, shift_ref, frob_ref, core_ref, row_grid_ref, col_own_ref, col_other_ref, scaled_ref,
    linear_ref, col_grid_ref
):
    first_row = place_ref[0] * 4
    first_col = place_ref[1] * 8
    core = place_ref[0] % 2
    for n in range(4):
        col_grid_ref[core * 4 + n] = col_own_ref[n]
        col_grid_ref[(1 - core) * 4 + n] = col_other_ref[n]
    shift = shift_ref[0]
    scale = scaling(frob_ref)
    eye = identity()
    dot = functools.partial(jnp.dot, preferred_element_type=F32)
    for i in range(4):
        for j in range(8):
            block = (slice(i * BS, (i + 1) * BS), slice(j * BS, (j + 1) * BS))
            kept = pattern_ref[i, j] != 0
            diagonal = first_row + i == first_col + j

            @pl.when(kept)
            def _():
                here = core_ref[block]
                wide = here.astype(F32)
                linear_ref[i * 8 + j] = dot(row_grid_ref[i], here) + dot(here, col_grid_ref[j]) - 2.0 * shift * wide

                @pl.when(diagonal)
                def _():
                    grid = row_grid_ref[i]
                    grid_wide = grid.astype(F32)
                    linear_ref[i * 8 + j] += dot(grid, grid) - 2.0 * shift * grid_wide + shift * shift * eye
                    scaled_ref[block] = ((wide + grid_wide - shift * eye) * scale).astype(BF16)

                @pl.when(jnp.logical_not(diagonal))
                def _():
                    scaled_ref[block] = (wide * scale).astype(BF16)

            @pl.when(jnp.logical_not(kept))
            def _():
                scaled_ref[block] = jnp.zeros((BS, BS), BF16)


def product_kernel(
    place_ref, pattern_ref, turns_ref, out_ref, left_ref, right_ref, frob_ref, linear_ref, *rest
):
    payload, crossed, own_role, other_role, halves = rest[0], rest[1], rest[2:9], rest[9:16], rest[16:18]
    square_ref, left_all, right_all, acc_ref, sems = rest[18:]
    core = place_ref[0] % 2

    def part(whole, at, size, source, number):
        return pltpu.make_async_copy(source, whole.at[pl.ds(at, size)], sems.at[number])

    copies = [
        part(left_all, 0, CAP, payload, 0),
        part(right_all, core * CAP, CAP, payload, 1),
        part(right_all, (1 - core) * CAP, CAP, crossed, 2),
    ]
    for copy in copies:
        copy.start()
    along_x = {1: 0, 2: 2, 3: 1, 4: 3, 5: 5, 6: 6, 7: 4}
    along_z = {1: 0, 2: 2, 3: 1, 4: 4, 5: 5, 7: 6}
    low, high = halves
    for k in range(1, 8):
        of_core_0 = [part(right_all, 2 * k * CAP, 2 * CAP, own_role[along_x[k]], 2 + 2 * k)]
        of_core_1 = [part(right_all, 2 * k * CAP, 2 * CAP, other_role[along_x[k]], 2 + 2 * k)]
        if k == 6:
            of_core_0.append(part(left_all, k * CAP, CAP, high, 1 + 2 * k))
            of_core_1.append(part(left_all, k * CAP, CAP, low, 1 + 2 * k))
        else:
            theirs, mine = other_role[along_z[k]], own_role[along_z[k]]
            of_core_0.append(part(left_all, k * CAP, CAP, theirs.at[pl.ds(CAP, CAP)], 1 + 2 * k))
            of_core_1.append(part(left_all, k * CAP, CAP, mine.at[pl.ds(0, CAP)], 1 + 2 * k))
        copies += of_core_0

        @pl.when(core == 0)
        def _():
            for copy in of_core_0:
                copy.start()

        @pl.when(core == 1)
        def _():
            for copy in of_core_1:
                copy.start()

    left_all[8 * CAP] = jnp.zeros((BS, BS), BF16)
    acc_ref[...] = jnp.zeros_like(acc_ref)
    scale = scaling(frob_ref)
    dot = functools.partial(jnp.dot, preferred_element_type=F32)
    for i in range(4):
        for j in range(8):

            @pl.when(pattern_ref[i, j] == 0)
            def _():
                square_ref[i * BS : (i + 1) * BS, j * BS : (j + 1) * BS] = jnp.zeros((BS, BS), BF16)

    for copy in copies:
        copy.wait()

    def turn(t, carry):
        sums = []
        for group in range(TURN):
            at = [(t * TURN + group) * GROUP + n for n in range(GROUP)]
            left = jnp.concatenate([left_all[left_ref[n]] for n in at], axis=1)
            right = jnp.concatenate([right_all[right_ref[n]] for n in at], axis=0)
            sums.append(dot(left, right))
        for group in range(TURN):
            acc_ref[out_ref[t * TURN + group]] += sums[group]
        return carry

    lax.fori_loop(0, turns_ref[0], turn, 0)
    for i in range(4):
        for j in range(8):
            block = (slice(i * BS, (i + 1) * BS), slice(j * BS, (j + 1) * BS))

            @pl.when(pattern_ref[i, j] != 0)
            def _():
                square_ref[block] = ((acc_ref[i * 8 + j] + linear_ref[i * 8 + j]) * (scale * scale)).astype(BF16)


VM = pl.BlockSpec(memory_space=pltpu.VMEM)
SM = pl.BlockSpec(memory_space=pltpu.SMEM)
ANY = pl.BlockSpec(memory_space=pl.ANY)
HBM = pl.BlockSpec(memory_space=pltpu.HBM)


def to_all(value, axis, count, groups=None):
    copies = jnp.broadcast_to(value[None], (count,) + value.shape)
    return lax.all_to_all(copies, axis, 0, 0, axis_index_groups=groups)


def place_of(device):
    row, col = device // 8, device % 8
    return row // 2 % 4, col % 2 * 2 + row // 8, col // 2, row % 2


def device_of(x, y, z, core):
    return ((y % 2 * 4 + x % 4) * 2 + core) * 8 + z % 4 * 2 + y // 2


def move(value, where):
    return lax.ppermute(value, ("row", "col"), [(k, device_of(*where(*place_of(k)))) for k in range(128)])


def ring(value, off):
    return move(value, lambda x, y, z, core: (x, y, z - off, core) if core else (x - off, y, z, core))


def across_y(value):
    return move(value, lambda x, y, z, core: (x, 3 - y if core else y ^ 1, z, core))


def across_y_again(value):
    return move(value, lambda x, y, z, core: (x, y ^ 1, z, core) if core else (x + 1, y, z, core))


def from_core_1(value, off, core):
    pairs = []
    for k in range(128):
        x, y, z, source = place_of(k)
        if source == 1:
            pairs.append((k, device_of(x, y, z - off, core)))
    return lax.ppermute(value, ("row", "col"), pairs)


def to_core(value):
    return lax.ppermute(value, "row", [(k, k ^ 1) for k in range(16)])


def lasting(microseconds):
    return pl.CostEstimate(flops=int(microseconds * 1e9), bytes_accessed=2**20, transcendentals=0)


def body(core_matrix, pattern, shift, potential, home, centres, exponents, extents):
    row = lax.axis_index("row")
    col = lax.axis_index("col")
    place = jnp.stack([row, col]).astype(jnp.int32)

    brick = pl.pallas_call(
        brick_kernel,
        in_specs=[VM],
        out_specs=VM,
        out_shape=jax.ShapeDtypeStruct((64, BS), BF16),
        compiler_params=params(4),
        cost_estimate=lasting(1),
        name="brick",
    )(potential.reshape(64, BS))
    same_core = [[row * 8 + col for row in range(core, 16, 2) for col in range(8)] for core in range(2)]
    half = to_all(brick, ("row", "col"), 64, same_core)

    (core_after_brick, _) = lax.optimization_barrier((core_matrix, brick))
    payload, squares = pl.pallas_call(
        pack_kernel,
        in_specs=[SM, SM, VM],
        out_specs=[VM, VM],
        out_shape=[jax.ShapeDtypeStruct((CAP * BS, BS), BF16), jax.ShapeDtypeStruct((8, BS), F32)],
        compiler_params=params(4),
        cost_estimate=lasting(2),
        name="pack",
    )(pattern, place, core_after_brick)
    payload = payload.reshape(CAP, BS, BS)
    crossed = to_core(payload)

    pair = jnp.concatenate([payload, crossed])
    step = across_y(pair)
    after, before = ring(pair, 1), ring(pair, -1)
    phi = pl.pallas_call(
        values_kernel,
        in_specs=[SM, VM, VM, VM],
        out_specs=HBM,
        out_shape=jax.ShapeDtypeStruct((8, 8, BS, 8 * BS), BF16),
        scratch_shapes=[
            pltpu.VMEM((8, BS, BS), F32),
            pltpu.VMEM((2, 8, BS, 8 * BS), BF16),
            pltpu.SemaphoreType.DMA((2,)),
        ],
        compiler_params=params(49),
        cost_estimate=lasting(10),
        name="values",
    )(place, centres, exponents, extents)

    half, phi, step, after, before = lax.optimization_barrier((half, phi, step, after, before))

    far = ring(after, 1)
    second = across_y_again(step)
    bricks = jnp.concatenate([half, to_core(half)])

    def grid_blocks(with_sum, *more):
        extra = [VM, VM, SM] if with_sum else []
        out_shape = [jax.ShapeDtypeStruct((4, BS, BS), BF16)]
        if with_sum:
            out_shape.append(jax.ShapeDtypeStruct((1, BS), F32))
        return pl.pallas_call(
            functools.partial(grid_kernel, with_sum),
            in_specs=[SM, SM, SM, VM, HBM] + extra,
            out_specs=[VM] * len(out_shape),
            out_shape=out_shape,
            scratch_shapes=[pltpu.VMEM((4, 8, BS, 8 * BS), BF16), pltpu.SemaphoreType.DMA((4,))],
            compiler_params=params(49),
            cost_estimate=lasting(5),
            name="grid_rows" if with_sum else "grid_cols",
        )(place, home, shift, bricks, phi, *more)

    row_grid, total = grid_blocks(True, core_matrix, squares, pattern)
    crossings = [to_core(after), to_core(before)]
    frob = to_all(total, ("row", "col"), 128).reshape(128, BS)
    after, before, far, step, second, row_grid, frob, bricks, *crossings = lax.optimization_barrier(
        (after, before, far, step, second, row_grid, frob, bricks, *crossings)
    )

    third = ring(second, -1)
    other_after = ring(jnp.where(row % 2 == 0, step, second), 1)
    crossings += [to_core(far), to_core(step), to_core(second)]
    (col_grid,) = grid_blocks(False)
    *listed, most = pl.pallas_call(
        plan_kernel,
        in_specs=[SM, VM],
        out_specs=[SM] * 5,
        out_shape=[
            jax.ShapeDtypeStruct((1,), jnp.int32),
            jax.ShapeDtypeStruct((LISTED // GROUP,), jnp.int32),
            jax.ShapeDtypeStruct((LISTED,), jnp.int32),
            jax.ShapeDtypeStruct((LISTED,), jnp.int32),
            jax.ShapeDtypeStruct((1,), jnp.int32),
        ],
        scratch_shapes=[pltpu.VMEM((40, BS), jnp.int32), pltpu.SMEM((40, BS), jnp.int32)]
        + [pltpu.SMEM((72,), jnp.int32)] * 3
        + [pltpu.SemaphoreType.DMA],
        compiler_params=params(4),
        cost_estimate=lasting(9),
        name="plan",
    )(place, frob)
    other_after, third, col_grid, *rest = lax.optimization_barrier(
        (other_after, third, col_grid, *crossings, *listed)
    )
    crossings, listed = rest[:5], rest[5:]

    low, high = from_core_1(third[:CAP], -1, 1), from_core_1(other_after[CAP:], 1, 0)
    crossings += [to_core(other_after), to_core(third)]
    col_grid_crossed = to_core(col_grid)
    scaled, linear = pl.pallas_call(
        prepare_kernel,
        in_specs=[SM] * 3 + [VM] * 5,
        out_specs=[VM, VM],
        out_shape=[jax.ShapeDtypeStruct((512, 1024), BF16), jax.ShapeDtypeStruct((32, BS, BS), F32)],
        scratch_shapes=[pltpu.VMEM((8, BS, BS), BF16)],
        compiler_params=params(4),
        cost_estimate=lasting(4),
        name="prepare",
    )(place, pattern, shift, frob, core_matrix, row_grid, col_grid, col_grid_crossed)
    low, high, scaled, linear, *crossings = lax.optimization_barrier((low, high, scaled, linear, *crossings))

    halves = [low, high]
    own_role = [after, before, far, step, second, other_after, third]
    overflow = most[0] > CAP

    def sparse():
        return pl.pallas_call(
            product_kernel,
            in_specs=[SM] * 6 + [VM] * 2 + [ANY] * 18,
            out_specs=VM,
            out_shape=jax.ShapeDtypeStruct((512, 1024), BF16),
            scratch_shapes=[
                pltpu.VMEM((8 * CAP + 1, BS, BS), BF16),
                pltpu.VMEM((16 * CAP, BS, BS), BF16),
                pltpu.VMEM((33, BS, BS), F32),
                pltpu.SemaphoreType.DMA((18,)),
            ],
            compiler_params=params(24),
            cost_estimate=lasting(12),
            name="product",
        )(place, pattern, *listed, frob, linear, payload, crossed, *own_role, *crossings, *halves)

    def dense():
        keep = pattern.astype(F32)[:, None, :, None]
        product = jnp.dot(
            lax.all_gather(scaled, "col", axis=1, tiled=True),
            lax.all_gather(scaled, "row", axis=0, tiled=True),
            preferred_element_type=F32,
        )
        return (product.reshape(4, BS, 8, BS) * keep).reshape(512, 1024).astype(BF16)

    return scaled, lax.cond(overflow, dense, sparse)


def solution(mesh):
    in_specs = (P("row", "col"), P("row", "col"), P(), P("row", "col", None), P(), P(), P(), P())
    out_specs = (P("row", "col"), P("row", "col"))
    return jax.shard_map(body, mesh=mesh, in_specs=in_specs, out_specs=out_specs, check_vma=False)
```

```python
import functools

import jax
import jax.numpy as jnp
from jax import lax
from jax.experimental import pallas as pl
from jax.experimental.pallas import tpu as pltpu
from jax.sharding import PartitionSpec as P

BS = 128
CAP = 20
GROUP = 4
TURN = 4
ORDER = 8192
VOLUME = 0.015625
SUM_LANE = 64
LISTED = 2048 + 32 * GROUP + TURN * GROUP
F32 = jnp.float32
BF16 = jnp.bfloat16


def params(mebibytes):
    return pltpu.CompilerParams(vmem_limit_bytes=mebibytes * 2**20)


def pack_kernel(pattern_ref, place_ref, core_ref, payload_ref, sum_ref):
    first_row = place_ref[0] * 4
    first_col = place_ref[1] * 8
    sum_ref[...] = jnp.zeros_like(sum_ref)

    def put(i, j, slot):
        payload_ref[pl.ds(pl.multiple_of(slot * BS, BS), BS), :] = core_ref[
            i * BS : (i + 1) * BS, j * BS : (j + 1) * BS
        ]

    slot = jnp.int32(0)
    for i in range(4):
        for j in range(8):
            kept = pattern_ref[i, j] != 0

            @pl.when(kept & (slot < CAP))
            def _():
                put(i, j, slot)

            @pl.when(kept & (first_row + i != first_col + j))
            def _():
                block = core_ref[i * BS : (i + 1) * BS, j * BS : (j + 1) * BS].astype(F32)
                squares = (block * block).reshape(16, 8, BS)
                sum_ref[...] += jnp.sum(squares, axis=0)

            slot += kept.astype(jnp.int32)
    for i in range(4):
        for j in range(8):
            dropped = pattern_ref[i, j] == 0

            @pl.when(dropped & (slot < CAP))
            def _():
                put(i, j, slot)

            slot += dropped.astype(jnp.int32)


def brick_kernel(potential_ref, brick_ref):
    brick_ref[...] = potential_ref[...].astype(BF16)


def column(row_values):
    return jnp.broadcast_to(row_values, (BS, BS)).T


def values_kernel(place_ref, centres_ref, exponents_ref, extents_ref, phi_ref, along_ref, slots, sems):
    row, col = place_ref[0], place_ref[1]

    def copy(k):
        return pltpu.make_async_copy(slots.at[k % 2], phi_ref.at[k], sems.at[k % 2])

    def one(k, carry):
        @pl.when(k >= 2)
        def _():
            copy(k - 2).wait()

        cluster = jnp.where(k < 4, row * 4 + k, col * 8 + row % 2 * 4 + k - 4)
        decay = column(exponents_ref[pl.ds(cluster, 1), :])
        reach = column(extents_ref[pl.ds(cluster, 1), :].astype(F32))
        cut = jnp.exp(-decay * (reach * reach + 0.5))
        at_x = column(centres_ref[0, pl.ds(cluster, 1), :].astype(F32))
        at_y = column(centres_ref[1, pl.ds(cluster, 1), :].astype(F32))
        at_z = column(centres_ref[2, pl.ds(cluster, 1), :].astype(F32))
        off_z = lax.broadcasted_iota(jnp.int32, (BS, BS), 1).astype(F32) - at_z
        along_z = jnp.exp(-decay * (off_z * off_z))
        for y in range(8):
            off_y = y - at_y
            along_ref[y] = jnp.exp(-decay * (off_y * off_y))
        for x in range(8):
            off_x = x - at_x
            along_xz = along_z * jnp.exp(-decay * (off_x * off_x))
            for y in range(8):
                phi = along_xz * along_ref[y]
                slots[k % 2, x, :, y * BS : (y + 1) * BS] = jnp.where(phi >= cut, phi, 0.0).astype(BF16)
        copy(k).start()
        return carry

    lax.fori_loop(0, 8, one, 0)
    copy(6).wait()
    copy(7).wait()


def grid_kernel(with_sum, place_ref, home_ref, shift_ref, bricks_ref, phi_ref, *rest):
    if with_sum:
        core_ref, sum_ref, pattern_ref, blocks_ref, total_ref, slots, sems = rest
    else:
        blocks_ref, slots, sems = rest
    row, col = place_ref[0], place_ref[1]
    first = row * 4 if with_sum else col * 8 + row % 2 * 4
    place = 0 if with_sum else 4

    def copy(k):
        return pltpu.make_async_copy(phi_ref.at[place + k], slots.at[k], sems.at[k])

    for k in range(4):
        copy(k).start()

    def one(k, carry):
        home = home_ref[first + k]
        index = (home // 8 ^ row) % 2 * 64 + home // 16 * 8 + home % 8
        copy(k).wait()
        total = jnp.zeros((BS, BS), F32)
        for x in range(8):
            values = jnp.concatenate([bricks_ref[index, x * 8 + y : x * 8 + y + 1, :] for y in range(8)], axis=1)
            phi = slots[k, x]
            total += lax.dot_general(phi * values, phi, (((1,), (1,)), ((), ())), preferred_element_type=F32)
        blocks_ref[k] = (total * VOLUME).astype(BF16)
        return carry

    lax.fori_loop(0, 4, one, 0)
    if with_sum:
        total_ref[...] = jnp.sum(sum_ref[...], axis=0, keepdims=True)

        @pl.when(col == row // 2)
        def _():
            eye = identity()
            for i in range(4):
                corner = pl.multiple_of((row % 2 * 4 + i) * BS, BS)
                block = core_ref[i * BS : (i + 1) * BS, pl.ds(corner, BS)].astype(F32)
                block = block + blocks_ref[i].astype(F32) - shift_ref[0] * eye
                total_ref[...] += jnp.sum(block * block, axis=0, keepdims=True)

        lanes = lax.broadcasted_iota(jnp.int32, (1, BS), 1)
        note = jnp.where(lanes == SUM_LANE, jnp.sum(total_ref[...], axis=1, keepdims=True), 0.0)
        for i in range(4):
            for j in range(8):
                note = jnp.where(lanes == i * 8 + j, pattern_ref[i, j].astype(F32), note)
        total_ref[...] = note


def identity():
    rows = lax.broadcasted_iota(jnp.int32, (BS, BS), 0)
    columns = lax.broadcasted_iota(jnp.int32, (BS, BS), 1)
    return (rows == columns).astype(F32)


def plan_kernel(
    place_ref, notes_ref, turns_ref, out_ref, left_ref, right_ref, most_ref, slots_ref, slots, kept_left, kept_right, kept_at, sem
):
    row, col = place_ref[0], place_ref[1]
    lanes = lax.broadcasted_iota(jnp.int32, (BS, BS), 1)
    kept = jnp.where(lanes < 32, notes_ref[...], 0.0).T
    earlier = lax.broadcasted_iota(jnp.int32, (BS, BS), 1) < lax.broadcasted_iota(jnp.int32, (BS, BS), 0)
    before = jnp.dot(earlier.astype(BF16), kept.astype(BF16), preferred_element_type=F32)
    slots_ref[...] = jnp.where(kept > 0.5, before, -1.0)[:40].astype(jnp.int32)
    most_ref[0] = jnp.max(jnp.sum(kept, axis=0, keepdims=True)).astype(jnp.int32)
    copy = pltpu.make_async_copy(slots_ref, slots, sem)
    copy.start()
    copy.wait()

    def block_row(i, number):
        def piece(other, count):
            device = row * 8 + other
            base = ((other ^ col) % 2 * 4 + (other // 2 - col // 2) % 4) * CAP
            right = ((other // 4 ^ row // 8) * 4 + (other - row // 2) % 4) * 2 * CAP
            for j in range(8):
                slot = slots[i * 8 + j, device]
                kept_left[count] = base + slot
                kept_right[count] = right + j // 4 * CAP
                kept_at[count] = j % 4 * 8 * BS + (other * 2 + j // 4) * 8 + col
                count += (slot >= 0).astype(jnp.int32)
            return count

        count = lax.fori_loop(0, 8, piece, jnp.int32(0))
        for more in range(3):
            kept_left[count + more] = 0
            kept_right[count + more] = 0
            kept_at[count + more] = 32 * BS

        def block(j, number):
            def listing(number):
                start = number // GROUP
                def four(n, number):
                    for inner in range(4):
                        at = kept_at[n * 4 + inner] + j * BS
                        slot = slots[at >> 7, at & 127]
                        left_ref[number] = kept_left[n * 4 + inner]
                        right_ref[number] = kept_right[n * 4 + inner] + slot
                        number += (slot >= 0).astype(jnp.int32)
                    return number

                number = lax.fori_loop(0, (count + 3) // 4, four, number)
                for more in range(GROUP - 1):
                    left_ref[number + more] = 8 * CAP
                    right_ref[number + more] = 0
                end = (number + GROUP - 1) // GROUP

                def name(group, carry):
                    out_ref[group] = i * 8 + j
                    return carry

                lax.fori_loop(start, end, name, 0)
                return end * GROUP

            wanted = slots[i * 8 + j, row * 8 + col] >= 0
            return lax.cond(wanted, listing, lambda n: n, number)

        return lax.fori_loop(0, 8, block, number)

    number = lax.fori_loop(0, 4, block_row, jnp.int32(0))
    groups = number // GROUP
    for more in range(TURN):
        out_ref[groups + more] = 32
        for inner in range(GROUP):
            left_ref[number + more * GROUP + inner] = 8 * CAP
            right_ref[number + more * GROUP + inner] = 0
    turns_ref[0] = (groups + TURN - 1) // TURN


def scaling(frob_ref):
    lanes = lax.broadcasted_iota(jnp.int32, (BS, BS), 1)
    total = jnp.sum(jnp.where(lanes == SUM_LANE, frob_ref[...], 0.0), axis=(0, 1), keepdims=True)
    return lax.rsqrt(total / ORDER + 1e-6)


def prepare_kernel(
    place_ref, pattern_ref, shift_ref, frob_ref, core_ref, row_grid_ref, col_own_ref, col_other_ref, scaled_ref,
    linear_ref, col_grid_ref
):
    first_row = place_ref[0] * 4
    first_col = place_ref[1] * 8
    core = place_ref[0] % 2
    for n in range(4):
        col_grid_ref[core * 4 + n] = col_own_ref[n]
        col_grid_ref[(1 - core) * 4 + n] = col_other_ref[n]
    shift = shift_ref[0]
    scale = scaling(frob_ref)
    eye = identity()
    dot = functools.partial(jnp.dot, preferred_element_type=F32)
    for i in range(4):
        for j in range(8):
            block = (slice(i * BS, (i + 1) * BS), slice(j * BS, (j + 1) * BS))
            kept = pattern_ref[i, j] != 0
            diagonal = first_row + i == first_col + j

            @pl.when(kept)
            def _():
                here = core_ref[block]
                wide = here.astype(F32)
                linear_ref[i * 8 + j] = dot(row_grid_ref[i], here) + dot(here, col_grid_ref[j]) - 2.0 * shift * wide

                @pl.when(diagonal)
                def _():
                    grid = row_grid_ref[i]
                    grid_wide = grid.astype(F32)
                    linear_ref[i * 8 + j] += dot(grid, grid) - 2.0 * shift * grid_wide + shift * shift * eye
                    scaled_ref[block] = ((wide + grid_wide - shift * eye) * scale).astype(BF16)

                @pl.when(jnp.logical_not(diagonal))
                def _():
                    scaled_ref[block] = (wide * scale).astype(BF16)

            @pl.when(jnp.logical_not(kept))
            def _():
                scaled_ref[block] = jnp.zeros((BS, BS), BF16)


def product_kernel(
    place_ref, pattern_ref, turns_ref, out_ref, left_ref, right_ref, frob_ref, linear_ref, *rest
):
    payload, crossed, own_role, other_role, halves = rest[0], rest[1], rest[2:9], rest[9:16], rest[16:18]
    square_ref, left_all, right_all, acc_ref, sems = rest[18:]
    core = place_ref[0] % 2

    def part(whole, at, size, source, number):
        return pltpu.make_async_copy(source, whole.at[pl.ds(at, size)], sems.at[number])

    copies = [
        part(left_all, 0, CAP, payload, 0),
        part(right_all, core * CAP, CAP, payload, 1),
        part(right_all, (1 - core) * CAP, CAP, crossed, 2),
    ]
    for copy in copies:
        copy.start()
    along_x = {1: 0, 2: 2, 3: 3, 4: 1, 5: 5, 6: 6, 7: 4}
    along_z = {1: 0, 2: 2, 3: 3, 4: 4, 5: 5, 7: 6}
    low, high = halves
    for k in range(1, 8):
        of_core_0 = [part(right_all, 2 * k * CAP, 2 * CAP, own_role[along_x[k]], 2 + 2 * k)]
        of_core_1 = [part(right_all, 2 * k * CAP, 2 * CAP, other_role[along_x[k]], 2 + 2 * k)]
        if k == 6:
            of_core_0.append(part(left_all, k * CAP, CAP, high, 1 + 2 * k))
            of_core_1.append(part(left_all, k * CAP, CAP, low, 1 + 2 * k))
        else:
            theirs, mine = other_role[along_z[k]], own_role[along_z[k]]
            of_core_0.append(part(left_all, k * CAP, CAP, theirs.at[pl.ds(CAP, CAP)], 1 + 2 * k))
            of_core_1.append(part(left_all, k * CAP, CAP, mine.at[pl.ds(0, CAP)], 1 + 2 * k))
        copies += of_core_0

        @pl.when(core == 0)
        def _():
            for copy in of_core_0:
                copy.start()

        @pl.when(core == 1)
        def _():
            for copy in of_core_1:
                copy.start()

    left_all[8 * CAP] = jnp.zeros((BS, BS), BF16)
    acc_ref[...] = jnp.zeros_like(acc_ref)
    scale = scaling(frob_ref)
    dot = functools.partial(jnp.dot, preferred_element_type=F32)
    for i in range(4):
        for j in range(8):

            @pl.when(pattern_ref[i, j] == 0)
            def _():
                square_ref[i * BS : (i + 1) * BS, j * BS : (j + 1) * BS] = jnp.zeros((BS, BS), BF16)

    for copy in copies:
        copy.wait()

    def turn(t, carry):
        sums = []
        for group in range(TURN):
            at = [(t * TURN + group) * GROUP + n for n in range(GROUP)]
            left = jnp.concatenate([left_all[left_ref[n]] for n in at], axis=1)
            right = jnp.concatenate([right_all[right_ref[n]] for n in at], axis=0)
            sums.append(dot(left, right))
        for group in range(TURN):
            acc_ref[out_ref[t * TURN + group]] += sums[group]
        return carry

    lax.fori_loop(0, turns_ref[0], turn, 0)
    for i in range(4):
        for j in range(8):
            block = (slice(i * BS, (i + 1) * BS), slice(j * BS, (j + 1) * BS))

            @pl.when(pattern_ref[i, j] != 0)
            def _():
                square_ref[block] = ((acc_ref[i * 8 + j] + linear_ref[i * 8 + j]) * (scale * scale)).astype(BF16)


VM = pl.BlockSpec(memory_space=pltpu.VMEM)
SM = pl.BlockSpec(memory_space=pltpu.SMEM)
ANY = pl.BlockSpec(memory_space=pl.ANY)
HBM = pl.BlockSpec(memory_space=pltpu.HBM)


def to_all(value, axis, count, groups=None):
    copies = jnp.broadcast_to(value[None], (count,) + value.shape)
    return lax.all_to_all(copies, axis, 0, 0, axis_index_groups=groups)


def place_of(device):
    row, col = device // 8, device % 8
    return row // 2 % 4, col % 2 * 2 + row // 8, col // 2, row % 2


def device_of(x, y, z, core):
    return ((y % 2 * 4 + x % 4) * 2 + core) * 8 + z % 4 * 2 + y // 2


def move(value, where):
    return lax.ppermute(value, ("row", "col"), [(k, device_of(*where(*place_of(k)))) for k in range(128)])


def ring(value, off):
    return move(value, lambda x, y, z, core: (x, y, z - off, core) if core else (x - off, y, z, core))


def across_y(value):
    return move(value, lambda x, y, z, core: (x, 3 - y if core else y ^ 1, z, core))


def across_y_again(value):
    return move(value, lambda x, y, z, core: (x, y ^ 1, z, core) if core else (x + 1, y, z, core))


def from_core_1(value, off, core):
    pairs = []
    for k in range(128):
        x, y, z, source = place_of(k)
        if source == 1:
            pairs.append((k, device_of(x, y, z - off, core)))
    return lax.ppermute(value, ("row", "col"), pairs)


def to_core(value):
    return lax.ppermute(value, "row", [(k, k ^ 1) for k in range(16)])


def lasting(microseconds):
    return pl.CostEstimate(flops=int(microseconds * 1e9), bytes_accessed=2**20, transcendentals=0)


def body(core_matrix, pattern, shift, potential, home, centres, exponents, extents):
    row = lax.axis_index("row")
    col = lax.axis_index("col")
    place = jnp.stack([row, col]).astype(jnp.int32)

    brick = pl.pallas_call(
        brick_kernel,
        in_specs=[VM],
        out_specs=VM,
        out_shape=jax.ShapeDtypeStruct((64, BS), BF16),
        compiler_params=params(4),
        cost_estimate=lasting(1),
        name="brick",
    )(potential.reshape(64, BS))
    same_core = [[row * 8 + col for row in range(core, 16, 2) for col in range(8)] for core in range(2)]
    half = to_all(brick, ("row", "col"), 64, same_core)

    (core_after_brick, _) = lax.optimization_barrier((core_matrix, brick))
    payload, squares = pl.pallas_call(
        pack_kernel,
        in_specs=[SM, SM, VM],
        out_specs=[VM, VM],
        out_shape=[jax.ShapeDtypeStruct((CAP * BS, BS), BF16), jax.ShapeDtypeStruct((8, BS), F32)],
        compiler_params=params(4),
        cost_estimate=lasting(2),
        name="pack",
    )(pattern, place, core_after_brick)
    payload = payload.reshape(CAP, BS, BS)
    crossed = to_core(payload)

    pair = jnp.concatenate([payload, crossed])
    step = across_y(pair)
    after = ring(pair, 1)
    phi = pl.pallas_call(
        values_kernel,
        in_specs=[SM, VM, VM, VM],
        out_specs=HBM,
        out_shape=jax.ShapeDtypeStruct((8, 8, BS, 8 * BS), BF16),
        scratch_shapes=[
            pltpu.VMEM((8, BS, BS), F32),
            pltpu.VMEM((2, 8, BS, 8 * BS), BF16),
            pltpu.SemaphoreType.DMA((2,)),
        ],
        compiler_params=params(49),
        cost_estimate=lasting(10),
        name="values",
    )(place, centres, exponents, extents)

    half, phi, step, after, pair = lax.optimization_barrier((half, phi, step, after, pair))

    far, before = ring(after, 1), ring(pair, -1)
    second = across_y_again(step)
    bricks = jnp.concatenate([half, to_core(half)])

    def grid_blocks(with_sum, *more):
        extra = [VM, VM, SM] if with_sum else []
        out_shape = [jax.ShapeDtypeStruct((4, BS, BS), BF16)]
        if with_sum:
            out_shape.append(jax.ShapeDtypeStruct((1, BS), F32))
        return pl.pallas_call(
            functools.partial(grid_kernel, with_sum),
            in_specs=[SM, SM, SM, VM, HBM] + extra,
            out_specs=[VM] * len(out_shape),
            out_shape=out_shape,
            scratch_shapes=[pltpu.VMEM((4, 8, BS, 8 * BS), BF16), pltpu.SemaphoreType.DMA((4,))],
            compiler_params=params(49),
            cost_estimate=lasting(5),
            name="grid_rows" if with_sum else "grid_cols",
        )(place, home, shift, bricks, phi, *more)

    row_grid, total = grid_blocks(True, core_matrix, squares, pattern)
    crossings = [to_core(after), to_core(step)]
    frob = to_all(total, ("row", "col"), 128).reshape(128, BS)
    after, before, far, step, second, row_grid, frob, bricks, *crossings = lax.optimization_barrier(
        (after, before, far, step, second, row_grid, frob, bricks, *crossings)
    )

    third = ring(second, -1)
    other_after = ring(jnp.where(row % 2 == 0, step, second), 1)
    crossings += [to_core(far), to_core(before), to_core(second)]
    (col_grid,) = grid_blocks(False)
    *listed, most = pl.pallas_call(
        plan_kernel,
        in_specs=[SM, VM],
        out_specs=[SM] * 5,
        out_shape=[
            jax.ShapeDtypeStruct((1,), jnp.int32),
            jax.ShapeDtypeStruct((LISTED // GROUP,), jnp.int32),
            jax.ShapeDtypeStruct((LISTED,), jnp.int32),
            jax.ShapeDtypeStruct((LISTED,), jnp.int32),
            jax.ShapeDtypeStruct((1,), jnp.int32),
        ],
        scratch_shapes=[pltpu.VMEM((40, BS), jnp.int32), pltpu.SMEM((40, BS), jnp.int32)]
        + [pltpu.SMEM((72,), jnp.int32)] * 3
        + [pltpu.SemaphoreType.DMA],
        compiler_params=params(4),
        cost_estimate=lasting(9),
        name="plan",
    )(place, frob)
    other_after, third, col_grid, *rest = lax.optimization_barrier(
        (other_after, third, col_grid, *crossings, *listed)
    )
    crossings, listed = rest[:5], rest[5:]

    low, high = from_core_1(third[:CAP], -1, 1), from_core_1(other_after[CAP:], 1, 0)
    crossings += [to_core(other_after), to_core(third)]
    col_grid_crossed = to_core(col_grid)
    scaled, linear = pl.pallas_call(
        prepare_kernel,
        in_specs=[SM] * 3 + [VM] * 5,
        out_specs=[VM, VM],
        out_shape=[jax.ShapeDtypeStruct((512, 1024), BF16), jax.ShapeDtypeStruct((32, BS, BS), F32)],
        scratch_shapes=[pltpu.VMEM((8, BS, BS), BF16)],
        compiler_params=params(4),
        cost_estimate=lasting(4),
        name="prepare",
    )(place, pattern, shift, frob, core_matrix, row_grid, col_grid, col_grid_crossed)
    low, high, scaled, linear, *crossings = lax.optimization_barrier((low, high, scaled, linear, *crossings))

    halves = [low, high]
    own_role = [after, step, far, before, second, other_after, third]
    overflow = most[0] > CAP

    def sparse():
        return pl.pallas_call(
            product_kernel,
            in_specs=[SM] * 6 + [VM] * 2 + [ANY] * 18,
            out_specs=VM,
            out_shape=jax.ShapeDtypeStruct((512, 1024), BF16),
            scratch_shapes=[
                pltpu.VMEM((8 * CAP + 1, BS, BS), BF16),
                pltpu.VMEM((16 * CAP, BS, BS), BF16),
                pltpu.VMEM((33, BS, BS), F32),
                pltpu.SemaphoreType.DMA((18,)),
            ],
            compiler_params=params(24),
            cost_estimate=lasting(12),
            name="product",
        )(place, pattern, *listed, frob, linear, payload, crossed, *own_role, *crossings, *halves)

    def dense():
        keep = pattern.astype(F32)[:, None, :, None]
        product = jnp.dot(
            lax.all_gather(scaled, "col", axis=1, tiled=True),
            lax.all_gather(scaled, "row", axis=0, tiled=True),
            preferred_element_type=F32,
        )
        return (product.reshape(4, BS, 8, BS) * keep).reshape(512, 1024).astype(BF16)

    return scaled, lax.cond(overflow, dense, sparse)


def solution(mesh):
    in_specs = (P("row", "col"), P("row", "col"), P(), P("row", "col", None), P(), P(), P(), P())
    out_specs = (P("row", "col"), P("row", "col"))
    return jax.shard_map(body, mesh=mesh, in_specs=in_specs, out_specs=out_specs, check_vma=False)
```

```python
import functools

import jax
import jax.numpy as jnp
from jax import lax
from jax.experimental import pallas as pl
from jax.experimental.pallas import tpu as pltpu
from jax.sharding import PartitionSpec as P

BS = 128
CAP = 20
FIRST = 12
GROUP = 4
TURN = 4
ORDER = 8192
VOLUME = 0.015625
SUM_LANE = 64
LISTED = 2048 + 32 * GROUP + TURN * GROUP
F32 = jnp.float32
BF16 = jnp.bfloat16


def params(mebibytes):
    return pltpu.CompilerParams(vmem_limit_bytes=mebibytes * 2**20)


def pack_kernel(pattern_ref, place_ref, core_ref, payload_ref, sum_ref):
    first_row = place_ref[0] * 4
    first_col = place_ref[1] * 8
    sum_ref[...] = jnp.zeros_like(sum_ref)

    def put(i, j, slot):
        payload_ref[pl.ds(pl.multiple_of(slot * BS, BS), BS), :] = core_ref[
            i * BS : (i + 1) * BS, j * BS : (j + 1) * BS
        ]

    slot = jnp.int32(0)
    for i in range(4):
        for j in range(8):
            kept = pattern_ref[i, j] != 0

            @pl.when(kept & (slot < CAP))
            def _():
                put(i, j, slot)

            @pl.when(kept & (first_row + i != first_col + j))
            def _():
                block = core_ref[i * BS : (i + 1) * BS, j * BS : (j + 1) * BS].astype(F32)
                squares = (block * block).reshape(16, 8, BS)
                sum_ref[...] += jnp.sum(squares, axis=0)

            slot += kept.astype(jnp.int32)
    for i in range(4):
        for j in range(8):
            dropped = pattern_ref[i, j] == 0

            @pl.when(dropped & (slot < CAP))
            def _():
                put(i, j, slot)

            slot += dropped.astype(jnp.int32)


def brick_kernel(potential_ref, brick_ref):
    brick_ref[...] = potential_ref[...].astype(BF16)


def column(row_values):
    return jnp.broadcast_to(row_values, (BS, BS)).T


def values_kernel(place_ref, centres_ref, exponents_ref, extents_ref, phi_ref, along_ref, slots, sems):
    row, col = place_ref[0], place_ref[1]

    def copy(k):
        return pltpu.make_async_copy(slots.at[k % 2], phi_ref.at[k], sems.at[k % 2])

    def one(k, carry):
        @pl.when(k >= 2)
        def _():
            copy(k - 2).wait()

        cluster = jnp.where(k < 4, row * 4 + k, col * 8 + row % 2 * 4 + k - 4)
        decay = column(exponents_ref[pl.ds(cluster, 1), :])
        reach = column(extents_ref[pl.ds(cluster, 1), :].astype(F32))
        cut = jnp.exp(-decay * (reach * reach + 0.5))
        at_x = column(centres_ref[0, pl.ds(cluster, 1), :].astype(F32))
        at_y = column(centres_ref[1, pl.ds(cluster, 1), :].astype(F32))
        at_z = column(centres_ref[2, pl.ds(cluster, 1), :].astype(F32))
        off_z = lax.broadcasted_iota(jnp.int32, (BS, BS), 1).astype(F32) - at_z
        along_z = jnp.exp(-decay * (off_z * off_z))
        for y in range(8):
            off_y = y - at_y
            along_ref[y] = jnp.exp(-decay * (off_y * off_y))
        for x in range(8):
            off_x = x - at_x
            along_xz = along_z * jnp.exp(-decay * (off_x * off_x))
            for y in range(8):
                phi = along_xz * along_ref[y]
                slots[k % 2, x, :, y * BS : (y + 1) * BS] = jnp.where(phi >= cut, phi, 0.0).astype(BF16)
        copy(k).start()
        return carry

    lax.fori_loop(0, 8, one, 0)
    copy(6).wait()
    copy(7).wait()


def grid_kernel(with_sum, place_ref, home_ref, shift_ref, bricks_ref, phi_ref, *rest):
    if with_sum:
        core_ref, sum_ref, pattern_ref, blocks_ref, total_ref, slots, sems = rest
    else:
        blocks_ref, slots, sems = rest
    row, col = place_ref[0], place_ref[1]
    first = row * 4 if with_sum else col * 8 + row % 2 * 4
    place = 0 if with_sum else 4

    def copy(k):
        return pltpu.make_async_copy(phi_ref.at[place + k], slots.at[k], sems.at[k])

    for k in range(4):
        copy(k).start()

    def one(k, carry):
        home = home_ref[first + k]
        index = (home // 8 ^ row) % 2 * 64 + home // 16 * 8 + home % 8
        copy(k).wait()
        total = jnp.zeros((BS, BS), F32)
        for x in range(8):
            values = jnp.concatenate([bricks_ref[index, x * 8 + y : x * 8 + y + 1, :] for y in range(8)], axis=1)
            phi = slots[k, x]
            total += lax.dot_general(phi * values, phi, (((1,), (1,)), ((), ())), preferred_element_type=F32)
        blocks_ref[k] = (total * VOLUME).astype(BF16)
        return carry

    lax.fori_loop(0, 4, one, 0)
    if with_sum:
        total_ref[...] = jnp.sum(sum_ref[...], axis=0, keepdims=True)

        @pl.when(col == row // 2)
        def _():
            eye = identity()
            for i in range(4):
                corner = pl.multiple_of((row % 2 * 4 + i) * BS, BS)
                block = core_ref[i * BS : (i + 1) * BS, pl.ds(corner, BS)].astype(F32)
                block = block + blocks_ref[i].astype(F32) - shift_ref[0] * eye
                total_ref[...] += jnp.sum(block * block, axis=0, keepdims=True)

        lanes = lax.broadcasted_iota(jnp.int32, (1, BS), 1)
        note = jnp.where(lanes == SUM_LANE, jnp.sum(total_ref[...], axis=1, keepdims=True), 0.0)
        for i in range(4):
            for j in range(8):
                note = jnp.where(lanes == i * 8 + j, pattern_ref[i, j].astype(F32), note)
        total_ref[...] = note


def identity():
    rows = lax.broadcasted_iota(jnp.int32, (BS, BS), 0)
    columns = lax.broadcasted_iota(jnp.int32, (BS, BS), 1)
    return (rows == columns).astype(F32)


def plan_kernel(
    place_ref, notes_ref, turns_ref, out_ref, left_ref, right_ref, counts_ref, most_ref, slots_ref, slots, kept_left, kept_right, kept_at, sem
):
    row, col = place_ref[0], place_ref[1]
    lanes = lax.broadcasted_iota(jnp.int32, (BS, BS), 1)
    kept = jnp.where(lanes < 32, notes_ref[...], 0.0).T
    earlier = lax.broadcasted_iota(jnp.int32, (BS, BS), 1) < lax.broadcasted_iota(jnp.int32, (BS, BS), 0)
    before = jnp.dot(earlier.astype(BF16), kept.astype(BF16), preferred_element_type=F32)
    counts = jnp.sum(kept, axis=0, keepdims=True)
    rows = lax.broadcasted_iota(jnp.int32, (BS, BS), 0)
    slots_ref[...] = jnp.where(rows == 40, counts, jnp.where(kept > 0.5, before, -1.0))[:48].astype(jnp.int32)
    most_ref[0] = jnp.max(counts).astype(jnp.int32)
    copy = pltpu.make_async_copy(slots_ref, slots, sem)
    copy.start()
    copy.wait()

    for other in range(8):
        piece_left = (other ^ col) % 2 * 4 + (other // 2 - col // 2) % 4
        piece_right = (other // 4 ^ row // 8) * 4 + (other - row // 2) % 4
        counts_ref[piece_left] = slots[40, row * 8 + other]
        for core in range(2):
            counts_ref[8 + 2 * piece_right + core] = slots[40, (other * 2 + core) * 8 + col]

    def block_row(i, number):
        def piece(other, count):
            device = row * 8 + other
            base = ((other ^ col) % 2 * 4 + (other // 2 - col // 2) % 4) * CAP
            right = ((other // 4 ^ row // 8) * 4 + (other - row // 2) % 4) * 2 * CAP
            for j in range(8):
                slot = slots[i * 8 + j, device]
                kept_left[count] = base + slot
                kept_right[count] = right + j // 4 * CAP
                kept_at[count] = j % 4 * 8 * BS + (other * 2 + j // 4) * 8 + col
                count += (slot >= 0).astype(jnp.int32)
            return count

        count = lax.fori_loop(0, 8, piece, jnp.int32(0))
        for more in range(3):
            kept_left[count + more] = 0
            kept_right[count + more] = 0
            kept_at[count + more] = 32 * BS

        def block(j, number):
            def listing(number):
                start = number // GROUP
                def four(n, number):
                    for inner in range(4):
                        at = kept_at[n * 4 + inner] + j * BS
                        slot = slots[at >> 7, at & 127]
                        left_ref[number] = kept_left[n * 4 + inner]
                        right_ref[number] = kept_right[n * 4 + inner] + slot
                        number += (slot >= 0).astype(jnp.int32)
                    return number

                number = lax.fori_loop(0, (count + 3) // 4, four, number)
                for more in range(GROUP - 1):
                    left_ref[number + more] = 8 * CAP
                    right_ref[number + more] = 0
                end = (number + GROUP - 1) // GROUP

                def name(group, carry):
                    out_ref[group] = i * 8 + j
                    return carry

                lax.fori_loop(start, end, name, 0)
                return end * GROUP

            wanted = slots[i * 8 + j, row * 8 + col] >= 0
            return lax.cond(wanted, listing, lambda n: n, number)

        return lax.fori_loop(0, 8, block, number)

    number = lax.fori_loop(0, 4, block_row, jnp.int32(0))
    groups = number // GROUP
    for more in range(TURN):
        out_ref[groups + more] = 32
        for inner in range(GROUP):
            left_ref[number + more * GROUP + inner] = 8 * CAP
            right_ref[number + more * GROUP + inner] = 0
    turns_ref[0] = (groups + TURN - 1) // TURN


def scaling(frob_ref):
    lanes = lax.broadcasted_iota(jnp.int32, (BS, BS), 1)
    total = jnp.sum(jnp.where(lanes == SUM_LANE, frob_ref[...], 0.0), axis=(0, 1), keepdims=True)
    return lax.rsqrt(total / ORDER + 1e-6)


def prepare_kernel(
    place_ref, pattern_ref, shift_ref, frob_ref, core_ref, row_grid_ref, col_own_ref, col_other_ref, scaled_ref,
    linear_ref, col_grid_ref
):
    first_row = place_ref[0] * 4
    first_col = place_ref[1] * 8
    core = place_ref[0] % 2
    for n in range(4):
        col_grid_ref[core * 4 + n] = col_own_ref[n]
        col_grid_ref[(1 - core) * 4 + n] = col_other_ref[n]
    shift = shift_ref[0]
    scale = scaling(frob_ref)
    eye = identity()
    dot = functools.partial(jnp.dot, preferred_element_type=F32)
    for i in range(4):
        for j in range(8):
            block = (slice(i * BS, (i + 1) * BS), slice(j * BS, (j + 1) * BS))
            kept = pattern_ref[i, j] != 0
            diagonal = first_row + i == first_col + j

            @pl.when(kept)
            def _():
                here = core_ref[block]
                wide = here.astype(F32)
                linear_ref[i * 8 + j] = dot(row_grid_ref[i], here) + dot(here, col_grid_ref[j]) - 2.0 * shift * wide

                @pl.when(diagonal)
                def _():
                    grid = row_grid_ref[i]
                    grid_wide = grid.astype(F32)
                    linear_ref[i * 8 + j] += dot(grid, grid) - 2.0 * shift * grid_wide + shift * shift * eye
                    scaled_ref[block] = ((wide + grid_wide - shift * eye) * scale).astype(BF16)

                @pl.when(jnp.logical_not(diagonal))
                def _():
                    scaled_ref[block] = (wide * scale).astype(BF16)

            @pl.when(jnp.logical_not(kept))
            def _():
                scaled_ref[block] = jnp.zeros((BS, BS), BF16)


def product_kernel(
    place_ref, pattern_ref, turns_ref, out_ref, left_ref, right_ref, counts_ref, frob_ref, linear_ref, *rest
):
    payload, crossed, own_role, other_role, halves = rest[0], rest[1], rest[2:9], rest[9:16], rest[16:18]
    square_ref, left_all, right_all, acc_ref, sems = rest[18:]
    core = place_ref[0] % 2

    def part(whole, at, size, source, number):
        return pltpu.make_async_copy(source, whole.at[pl.ds(at, size)], sems.at[number])

    waits = [
        part(left_all, 0, CAP, payload, 0),
        part(right_all, core * CAP, CAP, payload, 1),
        part(right_all, (1 - core) * CAP, CAP, crossed, 2),
    ]
    for copy in waits:
        copy.start()
    more_waits = []

    along_x = {1: 0, 2: 2, 3: 1, 4: 3, 5: 5, 6: 6, 7: 4}
    along_z = {1: 0, 2: 2, 3: 1, 4: 4, 5: 5, 7: 6}
    low, high = halves
    for k in range(1, 8):
        if k == 6:
            left_of = [(high, 0), (low, 0)]
        else:
            left_of = [(other_role[along_z[k]], CAP), (own_role[along_z[k]], 0)]
        moves = [(left_all, k * CAP, left_of, k)]
        for half in range(2):
            right_of = [(own_role[along_x[k]], half * CAP), (other_role[along_x[k]], half * CAP)]
            moves.append((right_all, (2 * k + half) * CAP, right_of, 8 + 2 * k + half))
        for n, (whole, at, sources, count) in enumerate(moves):
            number = 3 + 6 * (k - 1) + 2 * n
            full = counts_ref[count] > FIRST
            for mine, (source, offset) in enumerate(sources):
                first = part(whole, at, FIRST, source.at[pl.ds(offset, FIRST)], number)
                others = part(whole, at + FIRST, CAP - FIRST, source.at[pl.ds(offset + FIRST, CAP - FIRST)], number + 1)

                @pl.when(core == mine)
                def _():
                    first.start()

                @pl.when((core == mine) & full)
                def _():
                    others.start()

            waits.append(first)
            more_waits.append((full, others))

    left_all[8 * CAP] = jnp.zeros((BS, BS), BF16)
    acc_ref[...] = jnp.zeros_like(acc_ref)
    scale = scaling(frob_ref)
    dot = functools.partial(jnp.dot, preferred_element_type=F32)
    for i in range(4):
        for j in range(8):

            @pl.when(pattern_ref[i, j] == 0)
            def _():
                square_ref[i * BS : (i + 1) * BS, j * BS : (j + 1) * BS] = jnp.zeros((BS, BS), BF16)

    for copy in waits:
        copy.wait()
    for full, copy in more_waits:

        @pl.when(full)
        def _():
            copy.wait()

    def turn(t, carry):
        sums = []
        for group in range(TURN):
            at = [(t * TURN + group) * GROUP + n for n in range(GROUP)]
            left = jnp.concatenate([left_all[left_ref[n]] for n in at], axis=1)
            right = jnp.concatenate([right_all[right_ref[n]] for n in at], axis=0)
            sums.append(dot(left, right))
        for group in range(TURN):
            acc_ref[out_ref[t * TURN + group]] += sums[group]
        return carry

    lax.fori_loop(0, turns_ref[0], turn, 0)
    for i in range(4):
        for j in range(8):
            block = (slice(i * BS, (i + 1) * BS), slice(j * BS, (j + 1) * BS))

            @pl.when(pattern_ref[i, j] != 0)
            def _():
                square_ref[block] = ((acc_ref[i * 8 + j] + linear_ref[i * 8 + j]) * (scale * scale)).astype(BF16)


VM = pl.BlockSpec(memory_space=pltpu.VMEM)
SM = pl.BlockSpec(memory_space=pltpu.SMEM)
ANY = pl.BlockSpec(memory_space=pl.ANY)
HBM = pl.BlockSpec(memory_space=pltpu.HBM)


def to_all(value, axis, count, groups=None):
    copies = jnp.broadcast_to(value[None], (count,) + value.shape)
    return lax.all_to_all(copies, axis, 0, 0, axis_index_groups=groups)


def place_of(device):
    row, col = device // 8, device % 8
    return row // 2 % 4, col % 2 * 2 + row // 8, col // 2, row % 2


def device_of(x, y, z, core):
    return ((y % 2 * 4 + x % 4) * 2 + core) * 8 + z % 4 * 2 + y // 2


def move(value, where):
    return lax.ppermute(value, ("row", "col"), [(k, device_of(*where(*place_of(k)))) for k in range(128)])


def ring(value, off):
    return move(value, lambda x, y, z, core: (x, y, z - off, core) if core else (x - off, y, z, core))


def across_y(value):
    return move(value, lambda x, y, z, core: (x, 3 - y if core else y ^ 1, z, core))


def across_y_again(value):
    return move(value, lambda x, y, z, core: (x, y ^ 1, z, core) if core else (x + 1, y, z, core))


def from_core_1(value, off, core):
    pairs = []
    for k in range(128):
        x, y, z, source = place_of(k)
        if source == 1:
            pairs.append((k, device_of(x, y, z - off, core)))
    return lax.ppermute(value, ("row", "col"), pairs)


def to_core(value):
    return lax.ppermute(value, "row", [(k, k ^ 1) for k in range(16)])


def lasting(microseconds):
    return pl.CostEstimate(flops=int(microseconds * 1e9), bytes_accessed=2**20, transcendentals=0)


def body(core_matrix, pattern, shift, potential, home, centres, exponents, extents):
    row = lax.axis_index("row")
    col = lax.axis_index("col")
    place = jnp.stack([row, col]).astype(jnp.int32)

    brick = pl.pallas_call(
        brick_kernel,
        in_specs=[VM],
        out_specs=VM,
        out_shape=jax.ShapeDtypeStruct((64, BS), BF16),
        compiler_params=params(4),
        cost_estimate=lasting(1),
        name="brick",
    )(potential.reshape(64, BS))
    same_core = [[row * 8 + col for row in range(core, 16, 2) for col in range(8)] for core in range(2)]
    half = to_all(brick, ("row", "col"), 64, same_core)

    (core_after_brick, _) = lax.optimization_barrier((core_matrix, brick))
    payload, squares = pl.pallas_call(
        pack_kernel,
        in_specs=[SM, SM, VM],
        out_specs=[VM, VM],
        out_shape=[jax.ShapeDtypeStruct((CAP * BS, BS), BF16), jax.ShapeDtypeStruct((8, BS), F32)],
        compiler_params=params(4),
        cost_estimate=lasting(2),
        name="pack",
    )(pattern, place, core_after_brick)
    payload = payload.reshape(CAP, BS, BS)
    crossed = to_core(payload)

    pair = jnp.concatenate([payload, crossed])
    step = across_y(pair)
    after, before = ring(pair, 1), ring(pair, -1)
    phi = pl.pallas_call(
        values_kernel,
        in_specs=[SM, VM, VM, VM],
        out_specs=HBM,
        out_shape=jax.ShapeDtypeStruct((8, 8, BS, 8 * BS), BF16),
        scratch_shapes=[
            pltpu.VMEM((8, BS, BS), F32),
            pltpu.VMEM((2, 8, BS, 8 * BS), BF16),
            pltpu.SemaphoreType.DMA((2,)),
        ],
        compiler_params=params(49),
        cost_estimate=lasting(10),
        name="values",
    )(place, centres, exponents, extents)

    half, phi, step, after, before = lax.optimization_barrier((half, phi, step, after, before))

    far = ring(after, 1)
    second = across_y_again(step)
    bricks = jnp.concatenate([half, to_core(half)])

    def grid_blocks(with_sum, *more):
        extra = [VM, VM, SM] if with_sum else []
        out_shape = [jax.ShapeDtypeStruct((4, BS, BS), BF16)]
        if with_sum:
            out_shape.append(jax.ShapeDtypeStruct((1, BS), F32))
        return pl.pallas_call(
            functools.partial(grid_kernel, with_sum),
            in_specs=[SM, SM, SM, VM, HBM] + extra,
            out_specs=[VM] * len(out_shape),
            out_shape=out_shape,
            scratch_shapes=[pltpu.VMEM((4, 8, BS, 8 * BS), BF16), pltpu.SemaphoreType.DMA((4,))],
            compiler_params=params(49),
            cost_estimate=lasting(5),
            name="grid_rows" if with_sum else "grid_cols",
        )(place, home, shift, bricks, phi, *more)

    row_grid, total = grid_blocks(True, core_matrix, squares, pattern)
    crossings = [to_core(after), to_core(before)]
    frob = to_all(total, ("row", "col"), 128).reshape(128, BS)
    partner = jnp.where(row % 2 == 0, step, second)
    after, before, far, step, second, partner, row_grid, frob, bricks, *crossings = lax.optimization_barrier(
        (after, before, far, step, second, partner, row_grid, frob, bricks, *crossings)
    )

    third = ring(second, -1)
    other_after = ring(partner, 1)
    crossings += [to_core(far), to_core(step), to_core(second)]
    (col_grid,) = grid_blocks(False)
    *listed, most = pl.pallas_call(
        plan_kernel,
        in_specs=[SM, VM],
        out_specs=[SM] * 6,
        out_shape=[
            jax.ShapeDtypeStruct((1,), jnp.int32),
            jax.ShapeDtypeStruct((LISTED // GROUP,), jnp.int32),
            jax.ShapeDtypeStruct((LISTED,), jnp.int32),
            jax.ShapeDtypeStruct((LISTED,), jnp.int32),
            jax.ShapeDtypeStruct((24,), jnp.int32),
            jax.ShapeDtypeStruct((1,), jnp.int32),
        ],
        scratch_shapes=[pltpu.VMEM((48, BS), jnp.int32), pltpu.SMEM((48, BS), jnp.int32)]
        + [pltpu.SMEM((72,), jnp.int32)] * 3
        + [pltpu.SemaphoreType.DMA],
        compiler_params=params(4),
        cost_estimate=lasting(9),
        name="plan",
    )(place, frob)
    other_after, third, col_grid, *rest = lax.optimization_barrier(
        (other_after, third, col_grid, *crossings, *listed)
    )
    crossings, listed = rest[:5], rest[5:]

    low, high = from_core_1(third[:CAP], -1, 1), from_core_1(other_after[CAP:], 1, 0)
    crossings += [to_core(other_after), to_core(third)]
    col_grid_crossed = to_core(col_grid)
    scaled, linear = pl.pallas_call(
        prepare_kernel,
        in_specs=[SM] * 3 + [VM] * 5,
        out_specs=[VM, VM],
        out_shape=[jax.ShapeDtypeStruct((512, 1024), BF16), jax.ShapeDtypeStruct((32, BS, BS), F32)],
        scratch_shapes=[pltpu.VMEM((8, BS, BS), BF16)],
        compiler_params=params(4),
        cost_estimate=lasting(4),
        name="prepare",
    )(place, pattern, shift, frob, core_matrix, row_grid, col_grid, col_grid_crossed)
    low, high, scaled, linear, *crossings = lax.optimization_barrier((low, high, scaled, linear, *crossings))

    halves = [low, high]
    own_role = [after, before, far, step, second, other_after, third]
    overflow = most[0] > CAP

    def sparse():
        return pl.pallas_call(
            product_kernel,
            in_specs=[SM] * 7 + [VM] * 2 + [ANY] * 18,
            out_specs=VM,
            out_shape=jax.ShapeDtypeStruct((512, 1024), BF16),
            scratch_shapes=[
                pltpu.VMEM((8 * CAP + 1, BS, BS), BF16),
                pltpu.VMEM((16 * CAP, BS, BS), BF16),
                pltpu.VMEM((33, BS, BS), F32),
                pltpu.SemaphoreType.DMA((45,)),
            ],
            compiler_params=params(24),
            cost_estimate=lasting(12),
            name="product",
        )(place, pattern, *listed, frob, linear, payload, crossed, *own_role, *crossings, *halves)

    def dense():
        keep = pattern.astype(F32)[:, None, :, None]
        product = jnp.dot(
            lax.all_gather(scaled, "col", axis=1, tiled=True),
            lax.all_gather(scaled, "row", axis=0, tiled=True),
            preferred_element_type=F32,
        )
        return (product.reshape(4, BS, 8, BS) * keep).reshape(512, 1024).astype(BF16)

    return scaled, lax.cond(overflow, dense, sparse)


def solution(mesh):
    in_specs = (P("row", "col"), P("row", "col"), P(), P("row", "col", None), P(), P(), P(), P())
    out_specs = (P("row", "col"), P("row", "col"))
    return jax.shard_map(body, mesh=mesh, in_specs=in_specs, out_specs=out_specs, check_vma=False)
```

```python
import functools

import jax
import jax.numpy as jnp
from jax import lax
from jax.experimental import pallas as pl
from jax.experimental.pallas import tpu as pltpu
from jax.sharding import PartitionSpec as P

BS = 128
CAP = 20
GROUP = 4
TURN = 4
ORDER = 8192
VOLUME = 0.015625
SUM_LANE = 64
LISTED = 2048 + 32 * GROUP + TURN * GROUP
F32 = jnp.float32
BF16 = jnp.bfloat16


def params(mebibytes):
    return pltpu.CompilerParams(vmem_limit_bytes=mebibytes * 2**20)


def pack_kernel(pattern_ref, place_ref, core_ref, payload_ref, sum_ref):
    first_row = place_ref[0] * 4
    first_col = place_ref[1] * 8
    sum_ref[...] = jnp.zeros_like(sum_ref)

    def put(i, j, slot):
        payload_ref[pl.ds(pl.multiple_of(slot * BS, BS), BS), :] = core_ref[
            i * BS : (i + 1) * BS, j * BS : (j + 1) * BS
        ]

    slot = jnp.int32(0)
    for i in range(4):
        for j in range(8):
            kept = pattern_ref[i, j] != 0

            @pl.when(kept & (slot < CAP))
            def _():
                put(i, j, slot)

            @pl.when(kept & (first_row + i != first_col + j))
            def _():
                block = core_ref[i * BS : (i + 1) * BS, j * BS : (j + 1) * BS].astype(F32)
                squares = (block * block).reshape(16, 8, BS)
                sum_ref[...] += jnp.sum(squares, axis=0)

            slot += kept.astype(jnp.int32)
    for i in range(4):
        for j in range(8):
            dropped = pattern_ref[i, j] == 0

            @pl.when(dropped & (slot < CAP))
            def _():
                put(i, j, slot)

            slot += dropped.astype(jnp.int32)


def brick_kernel(potential_ref, brick_ref):
    brick_ref[...] = potential_ref[...].astype(BF16)


def column(row_values):
    return jnp.broadcast_to(row_values, (BS, BS)).T


def values_kernel(place_ref, centres_ref, exponents_ref, extents_ref, phi_ref, along_ref, slots, sems):
    row, col = place_ref[0], place_ref[1]

    def copy(k):
        return pltpu.make_async_copy(slots.at[k % 2], phi_ref.at[k], sems.at[k % 2])

    def one(k, carry):
        @pl.when(k >= 2)
        def _():
            copy(k - 2).wait()

        cluster = jnp.where(k < 4, row * 4 + k, col * 8 + row % 2 * 4 + k - 4)
        decay = column(exponents_ref[pl.ds(cluster, 1), :])
        reach = column(extents_ref[pl.ds(cluster, 1), :].astype(F32))
        cut = jnp.exp(-decay * (reach * reach + 0.5))
        at_x = column(centres_ref[0, pl.ds(cluster, 1), :].astype(F32))
        at_y = column(centres_ref[1, pl.ds(cluster, 1), :].astype(F32))
        at_z = column(centres_ref[2, pl.ds(cluster, 1), :].astype(F32))
        off_z = lax.broadcasted_iota(jnp.int32, (BS, BS), 1).astype(F32) - at_z
        along_z = jnp.exp(-decay * (off_z * off_z))
        for y in range(8):
            off_y = y - at_y
            along_ref[y] = jnp.exp(-decay * (off_y * off_y))
        for x in range(8):
            off_x = x - at_x
            along_xz = along_z * jnp.exp(-decay * (off_x * off_x))
            for y in range(8):
                phi = along_xz * along_ref[y]
                slots[k % 2, x, :, y * BS : (y + 1) * BS] = jnp.where(phi >= cut, phi, 0.0).astype(BF16)
        copy(k).start()
        return carry

    lax.fori_loop(0, 8, one, 0)
    copy(6).wait()
    copy(7).wait()


def grid_kernel(with_sum, place_ref, home_ref, shift_ref, same_ref, other_ref, phi_ref, *rest):
    if with_sum:
        core_ref, sum_ref, pattern_ref, blocks_ref, total_ref, slots, sems = rest
    else:
        blocks_ref, slots, sems = rest
    row, col = place_ref[0], place_ref[1]
    first = row * 4 if with_sum else col * 8 + row % 2 * 4
    place = 0 if with_sum else 4

    def copy(k):
        return pltpu.make_async_copy(phi_ref.at[place + k], slots.at[k], sems.at[k])

    for k in range(4):
        copy(k).start()

    def one(k, carry):
        home = home_ref[first + k]
        same = (home // 8 ^ row) % 2 == 0
        index = home // 16 * 8 + home % 8
        copy(k).wait()
        total = jnp.zeros((BS, BS), F32)
        for x in range(8):
            slab = slice(x * 8, x * 8 + 8)
            brick = jnp.where(same, same_ref[index, slab, :].astype(F32), other_ref[index, slab, :].astype(F32))
            values = jnp.concatenate([brick[y : y + 1] for y in range(8)], axis=1).astype(BF16)
            phi = slots[k, x]
            total += lax.dot_general(phi * values, phi, (((1,), (1,)), ((), ())), preferred_element_type=F32)
        blocks_ref[k] = (total * VOLUME).astype(BF16)
        return carry

    lax.fori_loop(0, 4, one, 0)
    if with_sum:
        total_ref[...] = jnp.sum(sum_ref[...], axis=0, keepdims=True)

        @pl.when(col == row // 2)
        def _():
            eye = identity()
            for i in range(4):
                corner = pl.multiple_of((row % 2 * 4 + i) * BS, BS)
                block = core_ref[i * BS : (i + 1) * BS, pl.ds(corner, BS)].astype(F32)
                block = block + blocks_ref[i].astype(F32) - shift_ref[0] * eye
                total_ref[...] += jnp.sum(block * block, axis=0, keepdims=True)

        lanes = lax.broadcasted_iota(jnp.int32, (1, BS), 1)
        note = jnp.where(lanes == SUM_LANE, jnp.sum(total_ref[...], axis=1, keepdims=True), 0.0)
        for i in range(4):
            for j in range(8):
                note = jnp.where(lanes == i * 8 + j, pattern_ref[i, j].astype(F32), note)
        total_ref[...] = note


def identity():
    rows = lax.broadcasted_iota(jnp.int32, (BS, BS), 0)
    columns = lax.broadcasted_iota(jnp.int32, (BS, BS), 1)
    return (rows == columns).astype(F32)


def plan_kernel(
    place_ref, notes_ref, turns_ref, out_ref, left_ref, right_ref, most_ref, slots_ref, slots, kept_left, kept_right, kept_at, sem
):
    row, col = place_ref[0], place_ref[1]
    lanes = lax.broadcasted_iota(jnp.int32, (BS, BS), 1)
    kept = jnp.where(lanes < 32, notes_ref[...], 0.0).T
    earlier = lax.broadcasted_iota(jnp.int32, (BS, BS), 1) < lax.broadcasted_iota(jnp.int32, (BS, BS), 0)
    before = jnp.dot(earlier.astype(BF16), kept.astype(BF16), preferred_element_type=F32)
    slots_ref[...] = jnp.where(kept > 0.5, before, -1.0)[:40].astype(jnp.int32)
    most_ref[0] = jnp.max(jnp.sum(kept, axis=0, keepdims=True)).astype(jnp.int32)
    copy = pltpu.make_async_copy(slots_ref, slots, sem)
    copy.start()
    copy.wait()

    def block_row(i, number):
        def piece(other, count):
            device = row * 8 + other
            base = ((other ^ col) % 2 * 4 + (other // 2 - col // 2) % 4) * CAP
            right = ((other // 4 ^ row // 8) * 4 + (other - row // 2) % 4) * 2 * CAP
            for j in range(8):
                slot = slots[i * 8 + j, device]
                kept_left[count] = base + slot
                kept_right[count] = right + j // 4 * CAP
                kept_at[count] = j % 4 * 8 * BS + (other * 2 + j // 4) * 8 + col
                count += (slot >= 0).astype(jnp.int32)
            return count

        count = lax.fori_loop(0, 8, piece, jnp.int32(0))
        for more in range(3):
            kept_left[count + more] = 0
            kept_right[count + more] = 0
            kept_at[count + more] = 32 * BS

        def block(j, number):
            def listing(number):
                start = number // GROUP
                def four(n, number):
                    for inner in range(4):
                        at = kept_at[n * 4 + inner] + j * BS
                        slot = slots[at >> 7, at & 127]
                        left_ref[number] = kept_left[n * 4 + inner]
                        right_ref[number] = kept_right[n * 4 + inner] + slot
                        number += (slot >= 0).astype(jnp.int32)
                    return number

                number = lax.fori_loop(0, (count + 3) // 4, four, number)
                for more in range(GROUP - 1):
                    left_ref[number + more] = 8 * CAP
                    right_ref[number + more] = 0
                end = (number + GROUP - 1) // GROUP

                def name(group, carry):
                    out_ref[group] = i * 8 + j
                    return carry

                lax.fori_loop(start, end, name, 0)
                return end * GROUP

            wanted = slots[i * 8 + j, row * 8 + col] >= 0
            return lax.cond(wanted, listing, lambda n: n, number)

        return lax.fori_loop(0, 8, block, number)

    number = lax.fori_loop(0, 4, block_row, jnp.int32(0))
    groups = number // GROUP
    for more in range(TURN):
        out_ref[groups + more] = 32
        for inner in range(GROUP):
            left_ref[number + more * GROUP + inner] = 8 * CAP
            right_ref[number + more * GROUP + inner] = 0
    turns_ref[0] = (groups + TURN - 1) // TURN


def scaling(frob_ref):
    lanes = lax.broadcasted_iota(jnp.int32, (BS, BS), 1)
    total = jnp.sum(jnp.where(lanes == SUM_LANE, frob_ref[...], 0.0), axis=(0, 1), keepdims=True)
    return lax.rsqrt(total / ORDER + 1e-6)


def prepare_kernel(
    place_ref, pattern_ref, shift_ref, frob_ref, core_ref, row_grid_ref, col_own_ref, col_other_ref, scaled_ref,
    linear_ref, col_grid_ref
):
    first_row = place_ref[0] * 4
    first_col = place_ref[1] * 8
    core = place_ref[0] % 2
    for n in range(4):
        col_grid_ref[core * 4 + n] = col_own_ref[n]
        col_grid_ref[(1 - core) * 4 + n] = col_other_ref[n]
    shift = shift_ref[0]
    scale = scaling(frob_ref)
    eye = identity()
    dot = functools.partial(jnp.dot, preferred_element_type=F32)
    for i in range(4):
        for j in range(8):
            block = (slice(i * BS, (i + 1) * BS), slice(j * BS, (j + 1) * BS))
            kept = pattern_ref[i, j] != 0
            diagonal = first_row + i == first_col + j

            @pl.when(kept)
            def _():
                here = core_ref[block]
                wide = here.astype(F32)
                linear_ref[i * 8 + j] = dot(row_grid_ref[i], here) + dot(here, col_grid_ref[j]) - 2.0 * shift * wide

                @pl.when(diagonal)
                def _():
                    grid = row_grid_ref[i]
                    grid_wide = grid.astype(F32)
                    linear_ref[i * 8 + j] += dot(grid, grid) - 2.0 * shift * grid_wide + shift * shift * eye
                    scaled_ref[block] = ((wide + grid_wide - shift * eye) * scale).astype(BF16)

                @pl.when(jnp.logical_not(diagonal))
                def _():
                    scaled_ref[block] = (wide * scale).astype(BF16)

            @pl.when(jnp.logical_not(kept))
            def _():
                scaled_ref[block] = jnp.zeros((BS, BS), BF16)


def product_kernel(
    place_ref, pattern_ref, turns_ref, out_ref, left_ref, right_ref, frob_ref, linear_ref, *rest
):
    payload, crossed, own_role, other_role, halves = rest[0], rest[1], rest[2:9], rest[9:16], rest[16:18]
    square_ref, left_all, right_all, acc_ref, sems = rest[18:]
    core = place_ref[0] % 2

    def part(whole, at, size, source, number):
        return pltpu.make_async_copy(source, whole.at[pl.ds(at, size)], sems.at[number])

    copies = [
        part(left_all, 0, CAP, payload, 0),
        part(right_all, core * CAP, CAP, payload, 1),
        part(right_all, (1 - core) * CAP, CAP, crossed, 2),
    ]
    for copy in copies:
        copy.start()
    along_x = {1: 0, 2: 2, 3: 1, 4: 3, 5: 5, 6: 6, 7: 4}
    along_z = {1: 0, 2: 2, 3: 1, 4: 4, 5: 5, 7: 6}
    low, high = halves
    for k in range(1, 8):
        of_core_0 = [part(right_all, 2 * k * CAP, 2 * CAP, own_role[along_x[k]], 2 + 2 * k)]
        of_core_1 = [part(right_all, 2 * k * CAP, 2 * CAP, other_role[along_x[k]], 2 + 2 * k)]
        if k == 6:
            of_core_0.append(part(left_all, k * CAP, CAP, high, 1 + 2 * k))
            of_core_1.append(part(left_all, k * CAP, CAP, low, 1 + 2 * k))
        else:
            theirs, mine = other_role[along_z[k]], own_role[along_z[k]]
            of_core_0.append(part(left_all, k * CAP, CAP, theirs.at[pl.ds(CAP, CAP)], 1 + 2 * k))
            of_core_1.append(part(left_all, k * CAP, CAP, mine.at[pl.ds(0, CAP)], 1 + 2 * k))
        copies += of_core_0

        @pl.when(core == 0)
        def _():
            for copy in of_core_0:
                copy.start()

        @pl.when(core == 1)
        def _():
            for copy in of_core_1:
                copy.start()

    left_all[8 * CAP] = jnp.zeros((BS, BS), BF16)
    acc_ref[...] = jnp.zeros_like(acc_ref)
    scale = scaling(frob_ref)
    dot = functools.partial(jnp.dot, preferred_element_type=F32)
    for i in range(4):
        for j in range(8):

            @pl.when(pattern_ref[i, j] == 0)
            def _():
                square_ref[i * BS : (i + 1) * BS, j * BS : (j + 1) * BS] = jnp.zeros((BS, BS), BF16)

    for copy in copies:
        copy.wait()

    def turn(t, carry):
        sums = []
        for group in range(TURN):
            at = [(t * TURN + group) * GROUP + n for n in range(GROUP)]
            left = jnp.concatenate([left_all[left_ref[n]] for n in at], axis=1)
            right = jnp.concatenate([right_all[right_ref[n]] for n in at], axis=0)
            sums.append(dot(left, right))
        for group in range(TURN):
            acc_ref[out_ref[t * TURN + group]] += sums[group]
        return carry

    lax.fori_loop(0, turns_ref[0], turn, 0)
    for i in range(4):
        for j in range(8):
            block = (slice(i * BS, (i + 1) * BS), slice(j * BS, (j + 1) * BS))

            @pl.when(pattern_ref[i, j] != 0)
            def _():
                square_ref[block] = ((acc_ref[i * 8 + j] + linear_ref[i * 8 + j]) * (scale * scale)).astype(BF16)


VM = pl.BlockSpec(memory_space=pltpu.VMEM)
SM = pl.BlockSpec(memory_space=pltpu.SMEM)
ANY = pl.BlockSpec(memory_space=pl.ANY)
HBM = pl.BlockSpec(memory_space=pltpu.HBM)


def to_all(value, axis, count, groups=None):
    copies = jnp.broadcast_to(value[None], (count,) + value.shape)
    return lax.all_to_all(copies, axis, 0, 0, axis_index_groups=groups)


def place_of(device):
    row, col = device // 8, device % 8
    return row // 2 % 4, col % 2 * 2 + row // 8, col // 2, row % 2


def device_of(x, y, z, core):
    return ((y % 2 * 4 + x % 4) * 2 + core) * 8 + z % 4 * 2 + y // 2


def move(value, where):
    return lax.ppermute(value, ("row", "col"), [(k, device_of(*where(*place_of(k)))) for k in range(128)])


def ring(value, off):
    return move(value, lambda x, y, z, core: (x, y, z - off, core) if core else (x - off, y, z, core))


def across_y(value):
    return move(value, lambda x, y, z, core: (x, 3 - y if core else y ^ 1, z, core))


def across_y_again(value):
    return move(value, lambda x, y, z, core: (x, y ^ 1, z, core) if core else (x + 1, y, z, core))


def from_core_1(value, off, core):
    pairs = []
    for k in range(128):
        x, y, z, source = place_of(k)
        if source == 1:
            pairs.append((k, device_of(x, y, z - off, core)))
    return lax.ppermute(value, ("row", "col"), pairs)


def to_core(value):
    return lax.ppermute(value, "row", [(k, k ^ 1) for k in range(16)])


def lasting(microseconds):
    return pl.CostEstimate(flops=int(microseconds * 1e9), bytes_accessed=2**20, transcendentals=0)


def body(core_matrix, pattern, shift, potential, home, centres, exponents, extents):
    row = lax.axis_index("row")
    col = lax.axis_index("col")
    place = jnp.stack([row, col]).astype(jnp.int32)

    brick = pl.pallas_call(
        brick_kernel,
        in_specs=[VM],
        out_specs=VM,
        out_shape=jax.ShapeDtypeStruct((64, BS), BF16),
        compiler_params=params(4),
        cost_estimate=lasting(1),
        name="brick",
    )(potential.reshape(64, BS))
    same_core = [[row * 8 + col for row in range(core, 16, 2) for col in range(8)] for core in range(2)]
    half = to_all(brick, ("row", "col"), 64, same_core)

    (core_after_brick, _) = lax.optimization_barrier((core_matrix, brick))
    payload, squares = pl.pallas_call(
        pack_kernel,
        in_specs=[SM, SM, VM],
        out_specs=[VM, VM],
        out_shape=[jax.ShapeDtypeStruct((CAP * BS, BS), BF16), jax.ShapeDtypeStruct((8, BS), F32)],
        compiler_params=params(4),
        cost_estimate=lasting(2),
        name="pack",
    )(pattern, place, core_after_brick)
    payload = payload.reshape(CAP, BS, BS)
    crossed = to_core(payload)

    pair = jnp.concatenate([payload, crossed])
    step = across_y(pair)
    after, before = ring(pair, 1), ring(pair, -1)
    phi = pl.pallas_call(
        values_kernel,
        in_specs=[SM, VM, VM, VM],
        out_specs=HBM,
        out_shape=jax.ShapeDtypeStruct((8, 8, BS, 8 * BS), BF16),
        scratch_shapes=[
            pltpu.VMEM((8, BS, BS), F32),
            pltpu.VMEM((2, 8, BS, 8 * BS), BF16),
            pltpu.SemaphoreType.DMA((2,)),
        ],
        compiler_params=params(49),
        cost_estimate=lasting(10),
        name="values",
    )(place, centres, exponents, extents)

    half, phi, step, after, before = lax.optimization_barrier((half, phi, step, after, before))

    far = ring(after, 1)
    second = across_y_again(step)
    bricks = [half, to_core(half)]

    def grid_blocks(with_sum, *more):
        extra = [VM, VM, SM] if with_sum else []
        out_shape = [jax.ShapeDtypeStruct((4, BS, BS), BF16)]
        if with_sum:
            out_shape.append(jax.ShapeDtypeStruct((1, BS), F32))
        return pl.pallas_call(
            functools.partial(grid_kernel, with_sum),
            in_specs=[SM, SM, SM, VM, VM, HBM] + extra,
            out_specs=[VM] * len(out_shape),
            out_shape=out_shape,
            scratch_shapes=[pltpu.VMEM((4, 8, BS, 8 * BS), BF16), pltpu.SemaphoreType.DMA((4,))],
            compiler_params=params(49),
            cost_estimate=lasting(5),
            name="grid_rows" if with_sum else "grid_cols",
        )(place, home, shift, *bricks, phi, *more)

    row_grid, total = grid_blocks(True, core_matrix, squares, pattern)
    crossings = [to_core(after), to_core(before)]
    frob = to_all(total, ("row", "col"), 128).reshape(128, BS)
    partner = jnp.where(row % 2 == 0, step, second)
    after, before, far, step, second, partner, row_grid, frob, *rest = lax.optimization_barrier(
        (after, before, far, step, second, partner, row_grid, frob, *bricks, *crossings)
    )
    bricks, crossings = rest[:2], rest[2:]

    third = ring(second, -1)
    other_after = ring(partner, 1)
    crossings += [to_core(far), to_core(step), to_core(second)]
    (col_grid,) = grid_blocks(False)
    *listed, most = pl.pallas_call(
        plan_kernel,
        in_specs=[SM, VM],
        out_specs=[SM] * 5,
        out_shape=[
            jax.ShapeDtypeStruct((1,), jnp.int32),
            jax.ShapeDtypeStruct((LISTED // GROUP,), jnp.int32),
            jax.ShapeDtypeStruct((LISTED,), jnp.int32),
            jax.ShapeDtypeStruct((LISTED,), jnp.int32),
            jax.ShapeDtypeStruct((1,), jnp.int32),
        ],
        scratch_shapes=[pltpu.VMEM((40, BS), jnp.int32), pltpu.SMEM((40, BS), jnp.int32)]
        + [pltpu.SMEM((72,), jnp.int32)] * 3
        + [pltpu.SemaphoreType.DMA],
        compiler_params=params(4),
        cost_estimate=lasting(9),
        name="plan",
    )(place, frob)
    other_after, third, col_grid, *rest = lax.optimization_barrier(
        (other_after, third, col_grid, *crossings, *listed)
    )
    crossings, listed = rest[:5], rest[5:]

    low, high = from_core_1(third[:CAP], -1, 1), from_core_1(other_after[CAP:], 1, 0)
    crossings += [to_core(other_after), to_core(third)]
    col_grid_crossed = to_core(col_grid)
    scaled, linear = pl.pallas_call(
        prepare_kernel,
        in_specs=[SM] * 3 + [VM] * 5,
        out_specs=[VM, VM],
        out_shape=[jax.ShapeDtypeStruct((512, 1024), BF16), jax.ShapeDtypeStruct((32, BS, BS), F32)],
        scratch_shapes=[pltpu.VMEM((8, BS, BS), BF16)],
        compiler_params=params(4),
        cost_estimate=lasting(4),
        name="prepare",
    )(place, pattern, shift, frob, core_matrix, row_grid, col_grid, col_grid_crossed)
    low, high, scaled, linear, *crossings = lax.optimization_barrier((low, high, scaled, linear, *crossings))

    halves = [low, high]
    own_role = [after, before, far, step, second, other_after, third]
    overflow = most[0] > CAP

    def sparse():
        return pl.pallas_call(
            product_kernel,
            in_specs=[SM] * 6 + [VM] * 2 + [ANY] * 18,
            out_specs=VM,
            out_shape=jax.ShapeDtypeStruct((512, 1024), BF16),
            scratch_shapes=[
                pltpu.VMEM((8 * CAP + 1, BS, BS), BF16),
                pltpu.VMEM((16 * CAP, BS, BS), BF16),
                pltpu.VMEM((33, BS, BS), F32),
                pltpu.SemaphoreType.DMA((18,)),
            ],
            compiler_params=params(24),
            cost_estimate=lasting(12),
            name="product",
        )(place, pattern, *listed, frob, linear, payload, crossed, *own_role, *crossings, *halves)

    def dense():
        keep = pattern.astype(F32)[:, None, :, None]
        product = jnp.dot(
            lax.all_gather(scaled, "col", axis=1, tiled=True),
            lax.all_gather(scaled, "row", axis=0, tiled=True),
            preferred_element_type=F32,
        )
        return (product.reshape(4, BS, 8, BS) * keep).reshape(512, 1024).astype(BF16)

    return scaled, lax.cond(overflow, dense, sparse)


def solution(mesh):
    in_specs = (P("row", "col"), P("row", "col"), P(), P("row", "col", None), P(), P(), P(), P())
    out_specs = (P("row", "col"), P("row", "col"))
    return jax.shard_map(body, mesh=mesh, in_specs=in_specs, out_specs=out_specs, check_vma=False)
```

```python
import functools

import jax
import jax.numpy as jnp
from jax import lax
from jax.experimental import pallas as pl
from jax.experimental.pallas import tpu as pltpu
from jax.sharding import PartitionSpec as P

BS = 128
CAP = 20
GROUP = 2
TURN = 8
ORDER = 8192
VOLUME = 0.015625
SUM_LANE = 64
LISTED = 2048 + 32 * GROUP + TURN * GROUP
F32 = jnp.float32
BF16 = jnp.bfloat16


def params(mebibytes):
    return pltpu.CompilerParams(vmem_limit_bytes=mebibytes * 2**20)


def pack_kernel(pattern_ref, place_ref, core_ref, payload_ref, sum_ref):
    first_row = place_ref[0] * 4
    first_col = place_ref[1] * 8
    sum_ref[...] = jnp.zeros_like(sum_ref)

    def put(i, j, slot):
        payload_ref[pl.ds(pl.multiple_of(slot * BS, BS), BS), :] = core_ref[
            i * BS : (i + 1) * BS, j * BS : (j + 1) * BS
        ]

    slot = jnp.int32(0)
    for i in range(4):
        for j in range(8):
            kept = pattern_ref[i, j] != 0

            @pl.when(kept & (slot < CAP))
            def _():
                put(i, j, slot)

            @pl.when(kept & (first_row + i != first_col + j))
            def _():
                block = core_ref[i * BS : (i + 1) * BS, j * BS : (j + 1) * BS].astype(F32)
                squares = (block * block).reshape(16, 8, BS)
                sum_ref[...] += jnp.sum(squares, axis=0)

            slot += kept.astype(jnp.int32)
    for i in range(4):
        for j in range(8):
            dropped = pattern_ref[i, j] == 0

            @pl.when(dropped & (slot < CAP))
            def _():
                put(i, j, slot)

            slot += dropped.astype(jnp.int32)


def brick_kernel(potential_ref, brick_ref):
    brick_ref[...] = potential_ref[...].astype(BF16)


def column(row_values):
    return jnp.broadcast_to(row_values, (BS, BS)).T


def values_kernel(place_ref, centres_ref, exponents_ref, extents_ref, phi_ref, along_ref, slots, sems):
    row, col = place_ref[0], place_ref[1]

    def copy(k):
        return pltpu.make_async_copy(slots.at[k % 2], phi_ref.at[k], sems.at[k % 2])

    def one(k, carry):
        @pl.when(k >= 2)
        def _():
            copy(k - 2).wait()

        cluster = jnp.where(k < 4, row * 4 + k, col * 8 + row % 2 * 4 + k - 4)
        decay = column(exponents_ref[pl.ds(cluster, 1), :])
        reach = column(extents_ref[pl.ds(cluster, 1), :].astype(F32))
        cut = jnp.exp(-decay * (reach * reach + 0.5))
        at_x = column(centres_ref[0, pl.ds(cluster, 1), :].astype(F32))
        at_y = column(centres_ref[1, pl.ds(cluster, 1), :].astype(F32))
        at_z = column(centres_ref[2, pl.ds(cluster, 1), :].astype(F32))
        off_z = lax.broadcasted_iota(jnp.int32, (BS, BS), 1).astype(F32) - at_z
        along_z = jnp.exp(-decay * (off_z * off_z))
        for y in range(8):
            off_y = y - at_y
            along_ref[y] = jnp.exp(-decay * (off_y * off_y))
        for x in range(8):
            off_x = x - at_x
            along_xz = along_z * jnp.exp(-decay * (off_x * off_x))
            for y in range(8):
                phi = along_xz * along_ref[y]
                slots[k % 2, x, :, y * BS : (y + 1) * BS] = jnp.where(phi >= cut, phi, 0.0).astype(BF16)
        copy(k).start()
        return carry

    lax.fori_loop(0, 8, one, 0)
    copy(6).wait()
    copy(7).wait()


def grid_kernel(with_sum, place_ref, home_ref, shift_ref, same_ref, other_ref, phi_ref, *rest):
    if with_sum:
        core_ref, sum_ref, pattern_ref, blocks_ref, total_ref, slots, sems = rest
    else:
        blocks_ref, slots, sems = rest
    row, col = place_ref[0], place_ref[1]
    first = row * 4 if with_sum else col * 8 + row % 2 * 4
    place = 0 if with_sum else 4

    def copy(k):
        return pltpu.make_async_copy(phi_ref.at[place + k], slots.at[k], sems.at[k])

    for k in range(4):
        copy(k).start()

    def one(k, carry):
        home = home_ref[first + k]
        same = (home // 8 ^ row) % 2 == 0
        index = home // 16 * 8 + home % 8
        copy(k).wait()
        total = jnp.zeros((BS, BS), F32)
        for x in range(8):
            slab = slice(x * 8, x * 8 + 8)
            brick = jnp.where(same, same_ref[index, slab, :].astype(F32), other_ref[index, slab, :].astype(F32))
            values = jnp.concatenate([brick[y : y + 1] for y in range(8)], axis=1).astype(BF16)
            phi = slots[k, x]
            total += lax.dot_general(phi * values, phi, (((1,), (1,)), ((), ())), preferred_element_type=F32)
        blocks_ref[k] = (total * VOLUME).astype(BF16)
        return carry

    lax.fori_loop(0, 4, one, 0)
    if with_sum:
        total_ref[...] = jnp.sum(sum_ref[...], axis=0, keepdims=True)

        @pl.when(col == row // 2)
        def _():
            eye = identity()
            for i in range(4):
                corner = pl.multiple_of((row % 2 * 4 + i) * BS, BS)
                block = core_ref[i * BS : (i + 1) * BS, pl.ds(corner, BS)].astype(F32)
                block = block + blocks_ref[i].astype(F32) - shift_ref[0] * eye
                total_ref[...] += jnp.sum(block * block, axis=0, keepdims=True)

        lanes = lax.broadcasted_iota(jnp.int32, (1, BS), 1)
        note = jnp.where(lanes == SUM_LANE, jnp.sum(total_ref[...], axis=1, keepdims=True), 0.0)
        for i in range(4):
            for j in range(8):
                note = jnp.where(lanes == i * 8 + j, pattern_ref[i, j].astype(F32), note)
        total_ref[...] = note


def identity():
    rows = lax.broadcasted_iota(jnp.int32, (BS, BS), 0)
    columns = lax.broadcasted_iota(jnp.int32, (BS, BS), 1)
    return (rows == columns).astype(F32)


def plan_kernel(
    place_ref, notes_ref, turns_ref, out_ref, left_ref, right_ref, most_ref, slots_ref, slots, kept_left, kept_right, kept_at, sem
):
    row, col = place_ref[0], place_ref[1]
    lanes = lax.broadcasted_iota(jnp.int32, (BS, BS), 1)
    kept = jnp.where(lanes < 32, notes_ref[...], 0.0).T
    earlier = lax.broadcasted_iota(jnp.int32, (BS, BS), 1) < lax.broadcasted_iota(jnp.int32, (BS, BS), 0)
    before = jnp.dot(earlier.astype(BF16), kept.astype(BF16), preferred_element_type=F32)
    slots_ref[...] = jnp.where(kept > 0.5, before, -1.0)[:40].astype(jnp.int32)
    most_ref[0] = jnp.max(jnp.sum(kept, axis=0, keepdims=True)).astype(jnp.int32)
    copy = pltpu.make_async_copy(slots_ref, slots, sem)
    copy.start()
    copy.wait()

    def block_row(i, number):
        def piece(other, count):
            device = row * 8 + other
            base = ((other ^ col) % 2 * 4 + (other // 2 - col // 2) % 4) * CAP
            right = ((other // 4 ^ row // 8) * 4 + (other - row // 2) % 4) * 2 * CAP
            for j in range(8):
                slot = slots[i * 8 + j, device]
                kept_left[count] = base + slot
                kept_right[count] = right + j // 4 * CAP
                kept_at[count] = j % 4 * 8 * BS + (other * 2 + j // 4) * 8 + col
                count += (slot >= 0).astype(jnp.int32)
            return count

        count = lax.fori_loop(0, 8, piece, jnp.int32(0))
        for more in range(3):
            kept_left[count + more] = 0
            kept_right[count + more] = 0
            kept_at[count + more] = 32 * BS

        def block(j, number):
            def listing(number):
                start = number // GROUP
                def four(n, number):
                    for inner in range(4):
                        at = kept_at[n * 4 + inner] + j * BS
                        slot = slots[at >> 7, at & 127]
                        left_ref[number] = kept_left[n * 4 + inner]
                        right_ref[number] = kept_right[n * 4 + inner] + slot
                        number += (slot >= 0).astype(jnp.int32)
                    return number

                number = lax.fori_loop(0, (count + 3) // 4, four, number)
                for more in range(GROUP - 1):
                    left_ref[number + more] = 8 * CAP
                    right_ref[number + more] = 0
                end = (number + GROUP - 1) // GROUP

                def name(group, carry):
                    out_ref[group] = i * 8 + j
                    return carry

                lax.fori_loop(start, end, name, 0)
                return end * GROUP

            wanted = slots[i * 8 + j, row * 8 + col] >= 0
            return lax.cond(wanted, listing, lambda n: n, number)

        return lax.fori_loop(0, 8, block, number)

    number = lax.fori_loop(0, 4, block_row, jnp.int32(0))
    groups = number // GROUP
    for more in range(TURN):
        out_ref[groups + more] = 32
        for inner in range(GROUP):
            left_ref[number + more * GROUP + inner] = 8 * CAP
            right_ref[number + more * GROUP + inner] = 0
    turns_ref[0] = (groups + TURN - 1) // TURN


def scaling(frob_ref):
    lanes = lax.broadcasted_iota(jnp.int32, (BS, BS), 1)
    total = jnp.sum(jnp.where(lanes == SUM_LANE, frob_ref[...], 0.0), axis=(0, 1), keepdims=True)
    return lax.rsqrt(total / ORDER + 1e-6)


def prepare_kernel(
    place_ref, pattern_ref, shift_ref, frob_ref, core_ref, row_grid_ref, col_own_ref, col_other_ref, scaled_ref,
    linear_ref, col_grid_ref
):
    first_row = place_ref[0] * 4
    first_col = place_ref[1] * 8
    core = place_ref[0] % 2
    for n in range(4):
        col_grid_ref[core * 4 + n] = col_own_ref[n]
        col_grid_ref[(1 - core) * 4 + n] = col_other_ref[n]
    shift = shift_ref[0]
    scale = scaling(frob_ref)
    eye = identity()
    dot = functools.partial(jnp.dot, preferred_element_type=F32)
    for i in range(4):
        for j in range(8):
            block = (slice(i * BS, (i + 1) * BS), slice(j * BS, (j + 1) * BS))
            kept = pattern_ref[i, j] != 0
            diagonal = first_row + i == first_col + j

            @pl.when(kept)
            def _():
                here = core_ref[block]
                wide = here.astype(F32)
                linear_ref[i * 8 + j] = dot(row_grid_ref[i], here) + dot(here, col_grid_ref[j]) - 2.0 * shift * wide

                @pl.when(diagonal)
                def _():
                    grid = row_grid_ref[i]
                    grid_wide = grid.astype(F32)
                    linear_ref[i * 8 + j] += dot(grid, grid) - 2.0 * shift * grid_wide + shift * shift * eye
                    scaled_ref[block] = ((wide + grid_wide - shift * eye) * scale).astype(BF16)

                @pl.when(jnp.logical_not(diagonal))
                def _():
                    scaled_ref[block] = (wide * scale).astype(BF16)

            @pl.when(jnp.logical_not(kept))
            def _():
                scaled_ref[block] = jnp.zeros((BS, BS), BF16)


def product_kernel(
    place_ref, pattern_ref, turns_ref, out_ref, left_ref, right_ref, frob_ref, linear_ref, *rest
):
    payload, crossed, own_role, other_role, halves = rest[0], rest[1], rest[2:9], rest[9:16], rest[16:18]
    square_ref, left_all, right_all, acc_ref, sems = rest[18:]
    core = place_ref[0] % 2

    def part(whole, at, size, source, number):
        return pltpu.make_async_copy(source, whole.at[pl.ds(at, size)], sems.at[number])

    copies = [
        part(left_all, 0, CAP, payload, 0),
        part(right_all, core * CAP, CAP, payload, 1),
        part(right_all, (1 - core) * CAP, CAP, crossed, 2),
    ]
    for copy in copies:
        copy.start()
    along_x = {1: 0, 2: 2, 3: 1, 4: 3, 5: 5, 6: 6, 7: 4}
    along_z = {1: 0, 2: 2, 3: 1, 4: 4, 5: 5, 7: 6}
    low, high = halves
    for k in range(1, 8):
        of_core_0 = [part(right_all, 2 * k * CAP, 2 * CAP, own_role[along_x[k]], 2 + 2 * k)]
        of_core_1 = [part(right_all, 2 * k * CAP, 2 * CAP, other_role[along_x[k]], 2 + 2 * k)]
        if k == 6:
            of_core_0.append(part(left_all, k * CAP, CAP, high, 1 + 2 * k))
            of_core_1.append(part(left_all, k * CAP, CAP, low, 1 + 2 * k))
        else:
            theirs, mine = other_role[along_z[k]], own_role[along_z[k]]
            of_core_0.append(part(left_all, k * CAP, CAP, theirs.at[pl.ds(CAP, CAP)], 1 + 2 * k))
            of_core_1.append(part(left_all, k * CAP, CAP, mine.at[pl.ds(0, CAP)], 1 + 2 * k))
        copies += of_core_0

        @pl.when(core == 0)
        def _():
            for copy in of_core_0:
                copy.start()

        @pl.when(core == 1)
        def _():
            for copy in of_core_1:
                copy.start()

    left_all[8 * CAP] = jnp.zeros((BS, BS), BF16)
    acc_ref[...] = jnp.zeros_like(acc_ref)
    scale = scaling(frob_ref)
    dot = functools.partial(jnp.dot, preferred_element_type=F32)
    for i in range(4):
        for j in range(8):

            @pl.when(pattern_ref[i, j] == 0)
            def _():
                square_ref[i * BS : (i + 1) * BS, j * BS : (j + 1) * BS] = jnp.zeros((BS, BS), BF16)

    for copy in copies:
        copy.wait()

    def turn(t, carry):
        sums = []
        for group in range(TURN):
            at = [(t * TURN + group) * GROUP + n for n in range(GROUP)]
            left = jnp.concatenate([left_all[left_ref[n]] for n in at], axis=1)
            right = jnp.concatenate([right_all[right_ref[n]] for n in at], axis=0)
            sums.append(dot(left, right))
        for group in range(TURN):
            acc_ref[out_ref[t * TURN + group]] += sums[group]
        return carry

    lax.fori_loop(0, turns_ref[0], turn, 0)
    for i in range(4):
        for j in range(8):
            block = (slice(i * BS, (i + 1) * BS), slice(j * BS, (j + 1) * BS))

            @pl.when(pattern_ref[i, j] != 0)
            def _():
                square_ref[block] = ((acc_ref[i * 8 + j] + linear_ref[i * 8 + j]) * (scale * scale)).astype(BF16)


VM = pl.BlockSpec(memory_space=pltpu.VMEM)
SM = pl.BlockSpec(memory_space=pltpu.SMEM)
ANY = pl.BlockSpec(memory_space=pl.ANY)
HBM = pl.BlockSpec(memory_space=pltpu.HBM)


def to_all(value, axis, count, groups=None):
    copies = jnp.broadcast_to(value[None], (count,) + value.shape)
    return lax.all_to_all(copies, axis, 0, 0, axis_index_groups=groups)


def place_of(device):
    row, col = device // 8, device % 8
    return row // 2 % 4, col % 2 * 2 + row // 8, col // 2, row % 2


def device_of(x, y, z, core):
    return ((y % 2 * 4 + x % 4) * 2 + core) * 8 + z % 4 * 2 + y // 2


def move(value, where):
    return lax.ppermute(value, ("row", "col"), [(k, device_of(*where(*place_of(k)))) for k in range(128)])


def ring(value, off):
    return move(value, lambda x, y, z, core: (x, y, z - off, core) if core else (x - off, y, z, core))


def across_y(value):
    return move(value, lambda x, y, z, core: (x, 3 - y if core else y ^ 1, z, core))


def across_y_again(value):
    return move(value, lambda x, y, z, core: (x, y ^ 1, z, core) if core else (x + 1, y, z, core))


def from_core_1(value, off, core):
    pairs = []
    for k in range(128):
        x, y, z, source = place_of(k)
        if source == 1:
            pairs.append((k, device_of(x, y, z - off, core)))
    return lax.ppermute(value, ("row", "col"), pairs)


def to_core(value):
    return lax.ppermute(value, "row", [(k, k ^ 1) for k in range(16)])


def lasting(microseconds):
    return pl.CostEstimate(flops=int(microseconds * 1e9), bytes_accessed=2**20, transcendentals=0)


def body(core_matrix, pattern, shift, potential, home, centres, exponents, extents):
    row = lax.axis_index("row")
    col = lax.axis_index("col")
    place = jnp.stack([row, col]).astype(jnp.int32)

    brick = pl.pallas_call(
        brick_kernel,
        in_specs=[VM],
        out_specs=VM,
        out_shape=jax.ShapeDtypeStruct((64, BS), BF16),
        compiler_params=params(4),
        cost_estimate=lasting(1),
        name="brick",
    )(potential.reshape(64, BS))
    same_core = [[row * 8 + col for row in range(core, 16, 2) for col in range(8)] for core in range(2)]
    half = to_all(brick, ("row", "col"), 64, same_core)

    (core_after_brick, _) = lax.optimization_barrier((core_matrix, brick))
    payload, squares = pl.pallas_call(
        pack_kernel,
        in_specs=[SM, SM, VM],
        out_specs=[VM, VM],
        out_shape=[jax.ShapeDtypeStruct((CAP * BS, BS), BF16), jax.ShapeDtypeStruct((8, BS), F32)],
        compiler_params=params(4),
        cost_estimate=lasting(2),
        name="pack",
    )(pattern, place, core_after_brick)
    payload = payload.reshape(CAP, BS, BS)
    crossed = to_core(payload)

    pair = jnp.concatenate([payload, crossed])
    step = across_y(pair)
    after, before = ring(pair, 1), ring(pair, -1)
    phi = pl.pallas_call(
        values_kernel,
        in_specs=[SM, VM, VM, VM],
        out_specs=HBM,
        out_shape=jax.ShapeDtypeStruct((8, 8, BS, 8 * BS), BF16),
        scratch_shapes=[
            pltpu.VMEM((8, BS, BS), F32),
            pltpu.VMEM((2, 8, BS, 8 * BS), BF16),
            pltpu.SemaphoreType.DMA((2,)),
        ],
        compiler_params=params(49),
        cost_estimate=lasting(10),
        name="values",
    )(place, centres, exponents, extents)

    half, phi, step, after, before = lax.optimization_barrier((half, phi, step, after, before))

    far = ring(after, 1)
    second = across_y_again(step)
    bricks = [half, to_core(half)]

    def grid_blocks(with_sum, *more):
        extra = [VM, VM, SM] if with_sum else []
        out_shape = [jax.ShapeDtypeStruct((4, BS, BS), BF16)]
        if with_sum:
            out_shape.append(jax.ShapeDtypeStruct((1, BS), F32))
        return pl.pallas_call(
            functools.partial(grid_kernel, with_sum),
            in_specs=[SM, SM, SM, VM, VM, HBM] + extra,
            out_specs=[VM] * len(out_shape),
            out_shape=out_shape,
            scratch_shapes=[pltpu.VMEM((4, 8, BS, 8 * BS), BF16), pltpu.SemaphoreType.DMA((4,))],
            compiler_params=params(49),
            cost_estimate=lasting(5),
            name="grid_rows" if with_sum else "grid_cols",
        )(place, home, shift, *bricks, phi, *more)

    row_grid, total = grid_blocks(True, core_matrix, squares, pattern)
    crossings = [to_core(after), to_core(before)]
    frob = to_all(total, ("row", "col"), 128).reshape(128, BS)
    partner = jnp.where(row % 2 == 0, step, second)
    after, before, far, step, second, partner, row_grid, frob, *rest = lax.optimization_barrier(
        (after, before, far, step, second, partner, row_grid, frob, *bricks, *crossings)
    )
    bricks, crossings = rest[:2], rest[2:]

    third = ring(second, -1)
    other_after = ring(partner, 1)
    crossings += [to_core(far), to_core(step), to_core(second)]
    (col_grid,) = grid_blocks(False)
    *listed, most = pl.pallas_call(
        plan_kernel,
        in_specs=[SM, VM],
        out_specs=[SM] * 5,
        out_shape=[
            jax.ShapeDtypeStruct((1,), jnp.int32),
            jax.ShapeDtypeStruct((LISTED // GROUP,), jnp.int32),
            jax.ShapeDtypeStruct((LISTED,), jnp.int32),
            jax.ShapeDtypeStruct((LISTED,), jnp.int32),
            jax.ShapeDtypeStruct((1,), jnp.int32),
        ],
        scratch_shapes=[pltpu.VMEM((40, BS), jnp.int32), pltpu.SMEM((40, BS), jnp.int32)]
        + [pltpu.SMEM((72,), jnp.int32)] * 3
        + [pltpu.SemaphoreType.DMA],
        compiler_params=params(4),
        cost_estimate=lasting(9),
        name="plan",
    )(place, frob)
    other_after, third, col_grid, *rest = lax.optimization_barrier(
        (other_after, third, col_grid, *crossings, *listed)
    )
    crossings, listed = rest[:5], rest[5:]

    low, high = from_core_1(third[:CAP], -1, 1), from_core_1(other_after[CAP:], 1, 0)
    crossings += [to_core(other_after), to_core(third)]
    col_grid_crossed = to_core(col_grid)
    scaled, linear = pl.pallas_call(
        prepare_kernel,
        in_specs=[SM] * 3 + [VM] * 5,
        out_specs=[VM, VM],
        out_shape=[jax.ShapeDtypeStruct((512, 1024), BF16), jax.ShapeDtypeStruct((32, BS, BS), F32)],
        scratch_shapes=[pltpu.VMEM((8, BS, BS), BF16)],
        compiler_params=params(4),
        cost_estimate=lasting(4),
        name="prepare",
    )(place, pattern, shift, frob, core_matrix, row_grid, col_grid, col_grid_crossed)
    low, high, scaled, linear, *crossings = lax.optimization_barrier((low, high, scaled, linear, *crossings))

    halves = [low, high]
    own_role = [after, before, far, step, second, other_after, third]
    overflow = most[0] > CAP

    def sparse():
        return pl.pallas_call(
            product_kernel,
            in_specs=[SM] * 6 + [VM] * 2 + [ANY] * 18,
            out_specs=VM,
            out_shape=jax.ShapeDtypeStruct((512, 1024), BF16),
            scratch_shapes=[
                pltpu.VMEM((8 * CAP + 1, BS, BS), BF16),
                pltpu.VMEM((16 * CAP, BS, BS), BF16),
                pltpu.VMEM((33, BS, BS), F32),
                pltpu.SemaphoreType.DMA((18,)),
            ],
            compiler_params=params(24),
            cost_estimate=lasting(12),
            name="product",
        )(place, pattern, *listed, frob, linear, payload, crossed, *own_role, *crossings, *halves)

    def dense():
        keep = pattern.astype(F32)[:, None, :, None]
        product = jnp.dot(
            lax.all_gather(scaled, "col", axis=1, tiled=True),
            lax.all_gather(scaled, "row", axis=0, tiled=True),
            preferred_element_type=F32,
        )
        return (product.reshape(4, BS, 8, BS) * keep).reshape(512, 1024).astype(BF16)

    return scaled, lax.cond(overflow, dense, sparse)


def solution(mesh):
    in_specs = (P("row", "col"), P("row", "col"), P(), P("row", "col", None), P(), P(), P(), P())
    out_specs = (P("row", "col"), P("row", "col"))
    return jax.shard_map(body, mesh=mesh, in_specs=in_specs, out_specs=out_specs, check_vma=False)
```
